32 devices in a mesh: dp: 16 (over z, y, x), tensor: 2 (over core).
Axes of the slice: x: 2, y: 2, z: 4, core: 2. Of those that a mesh axis runs over, the one named last changes fastest.
Arguments:
- tokens: bfloat16 [8192, 2048], P(('dp', 'tensor')), may hold values from -6 to 6
- cotangent: bfloat16 [8192, 2048], P(('dp', 'tensor')), may hold values from -6 to 6
- lengths: int32 [16, 4], P('dp'), may hold values from 1 to 509, as said below
- slot_of: int32 [8192], P(('dp', 'tensor')), may hold values from 0 to 8191, as said below
- norm_gains: float32 [2, 2048], replicated, may hold values from 0.5 to 1.5
- w_query: bfloat16 [2048, 2048], P('dp', 'tensor'), may hold values from -0.125 to 0.125
- w_key: bfloat16 [2048, 2048], P('dp', 'tensor'), may hold values from -0.125 to 0.125
- w_value: bfloat16 [2048, 4096], P('dp', 'tensor'), may hold values from -0.125 to 0.125
- w_gate: bfloat16 [2048, 4096], P('dp', 'tensor'), may hold values from -0.125 to 0.125
- w_decay: bfloat16 [2048, 16], P('dp', 'tensor'), may hold values from -0.125 to 0.125
- w_beta: bfloat16 [2048, 16], P('dp', 'tensor'), may hold values from -0.125 to 0.125
- conv_weights: float32 [4, 8192], replicated, may hold values from -3 to 3
- a_log: float32 [16], replicated, may hold values from -8 to -2.5
- dt_bias: float32 [16], replicated, may hold values from -2 to 0
- out_gain: float32 [256], replicated, may hold values from 0.5 to 1.5
- w_out: bfloat16 [4096, 2048], P('tensor', 'dp'), may hold values from -0.1875 to 0.1875
- w_mlp_gate: bfloat16 [2048, 5632], P('dp', 'tensor'), may hold values from -0.125 to 0.125
- w_mlp_up: bfloat16 [2048, 5632], P('dp', 'tensor'), may hold values from -0.125 to 0.125
- w_mlp_down: bfloat16 [5632, 2048], P('tensor', 'dp'), may hold values from -0.15625 to 0.15625
Outputs:
- output: bfloat16 [8192, 2048], P(('dp', 'tensor'))
- tokens_grad: bfloat16 [8192, 2048], P(('dp', 'tensor'))
- norm_gains_grad: float32 [2, 2048], replicated
- w_query_grad: float32 [2048, 2048], P('dp', 'tensor')
- w_key_grad: float32 [2048, 2048], P('dp', 'tensor')
- w_value_grad: float32 [2048, 4096], P('dp', 'tensor')
- w_gate_grad: float32 [2048, 4096], P('dp', 'tensor')
- w_decay_grad: float32 [2048, 16], P('dp', 'tensor')
- w_beta_grad: float32 [2048, 16], P('dp', 'tensor')
- conv_weights_grad: float32 [4, 8192], replicated
- a_log_grad: float32 [16], replicated
- dt_bias_grad: float32 [16], replicated
- out_gain_grad: float32 [256], replicated
- w_out_grad: float32 [4096, 2048], P('tensor', 'dp')
- w_mlp_gate_grad: float32 [2048, 5632], P('dp', 'tensor')
- w_mlp_up_grad: float32 [2048, 5632], P('dp', 'tensor')
- w_mlp_down_grad: float32 [5632, 2048], P('tensor', 'dp')
The draws below stay inside these ranges and needn't reach their ends.
Inputs may be any that keep to these rules, and one draw needn't show every extreme that they name: `slot_of`: A permutation of the slots; slot s lies on device s // 256 of the dp+tensor order. Each device sends at most 10 of its tokens to any one device, sends exactly 10 to one device and receives exactly 10 from one device. Each group's lengths fill its first slots in order and sum to 260 or more; in every group one sequence covers slots of all its tensor devices; some group holds a sequence of 509.
All inputs are finite; a program needn't handle non-finite values.
Results may differ from the reference program's by a relative error of at most 0.028.
Values may be sent and summed in bfloat16 or wider, within the bound.
No kernel may reach another device: no remote copies, remote signals or barrier semaphores. Data moves between devices by JAX's collectives and lax.ppermute only.
A program may use at most 448 MiB of HBM per device.

```python
import jax
import jax.numpy as jnp
from jax import lax

D = 2048
HEADS = 16
DK = 128
DV = 256
FF = 5632
WIDTH = 4
BLOCK = 64
TOK_DEV = 256
SEQ_G = 4
TOKENS = 8192
GROUP_ROWS = 512
KEYS = 2048
VALS = 4096
CONV_CH = 8192
N_DP = 16
N_TENSOR = 2


def derange(key, count):
    order = jax.random.permutation(key, count).astype(jnp.int32)
    offset = jax.random.randint(jax.random.fold_in(key, 1), (), 1, count)
    inverse = jnp.zeros((count,), jnp.int32).at[order].set(jnp.arange(count, dtype=jnp.int32))
    return order[(inverse + offset) % count]


def draw_slot_of(key, part):
    key = jax.random.fold_in(key, 11)
    count = TOKENS // TOK_DEV
    base_load = TOK_DEV // count
    first = jax.random.permutation(jax.random.fold_in(key, 1), count).astype(jnp.int32)
    second = first[derange(jax.random.fold_in(key, 2), count)]
    third = first[derange(jax.random.fold_in(key, 3), count)]
    labels = jnp.arange(count, dtype=jnp.int32)
    loads = base_load + 2 * (first[:, None] == labels[None, :]).astype(jnp.int32) - (second[:, None] == labels[None, :]).astype(jnp.int32) - (third[:, None] == labels[None, :]).astype(jnp.int32)
    targets = jax.vmap(lambda counts: jnp.repeat(labels, counts, total_repeat_length=TOK_DEV))(loads)
    row_keys = jax.random.split(jax.random.fold_in(key, 4), count)
    targets = jax.vmap(lambda row_key, row_vals: jax.random.permutation(row_key, row_vals))(row_keys, targets)
    targets = targets.reshape(-1).astype(jnp.int32)
    sorted_order = jnp.argsort(targets, stable=True)
    arrival = jnp.zeros((TOKENS,), jnp.int32).at[sorted_order].set(jnp.arange(TOKENS, dtype=jnp.int32))
    arrival = arrival - targets * TOK_DEV
    slot_keys = jax.random.split(jax.random.fold_in(key, 5), count)
    shuffles = jax.vmap(lambda slot_key: jax.random.permutation(slot_key, TOK_DEV))(slot_keys).astype(jnp.int32)
    return (targets * TOK_DEV + shuffles[targets, arrival]).astype(jnp.int32)


def draw_lengths(key, part):
    key = jax.random.fold_in(key, 23)
    chosen = jax.random.randint(jax.random.fold_in(key, 1), (), 0, N_DP)
    reach = TOK_DEV * (N_TENSOR - 1)
    candidates = jnp.arange(1, GROUP_ROWS, dtype=jnp.int32)
    forced = jnp.arange(1, SEQ_G, dtype=jnp.int32)

    def one_group(number):
        group_key = jax.random.fold_in(key, 100 + number)
        filled = jax.random.randint(jax.random.fold_in(group_key, 1), (), reach + SEQ_G, GROUP_ROWS + 1)
        banned = (candidates >= filled) | (candidates >= TOK_DEV) & (candidates <= reach)
        scores = jax.random.randint(jax.random.fold_in(group_key, 2), candidates.shape, 0, 4096) * GROUP_ROWS + candidates
        scores = jnp.where(banned, scores + (1 << 28), scores)
        _, picked = lax.top_k(-scores, SEQ_G - 1)
        cuts = jnp.sort(candidates[picked])
        cuts = jnp.where(number == chosen, forced, cuts)
        filled = jnp.where(number == chosen, GROUP_ROWS, filled)
        bounds = jnp.concatenate([jnp.zeros((1,), jnp.int32), cuts, filled[None].astype(jnp.int32)])
        return bounds[1:] - bounds[:-1]
    return jax.vmap(one_group)(jnp.arange(N_DP, dtype=jnp.int32)).astype(jnp.int32)


def block_scale(own_key, shape, shards, least, high):
    factor_of = 1.0
    for dim, parts in shards:
        heights = jax.random.uniform(jax.random.fold_in(jax.random.fold_in(own_key, 6), dim), (parts,), jnp.float32, least / len(shards), high / len(shards))
        factor_of = factor_of * jnp.repeat(jnp.exp(heights), shape[dim] // parts).reshape((-1,) + (1,) * (len(shape) - 1 - dim))
    return factor_of


def bell_draw(rng, dims, deviation, limit, cuts=(), held_as=jnp.bfloat16):
    values = deviation * jax.random.normal(rng, dims, jnp.float32)
    if cuts:
        values = values * block_scale(rng, dims, cuts, -0.22, 0.18)
    return jnp.clip(values, -limit, limit).astype(held_as)


def setup_inputs(seed: int = 0) -> dict:
    keys = jax.random.split(jax.random.key(seed), 20)
    return {
        "tokens": bell_draw(keys[0], (TOKENS, D), 1.0, 6.0, ((0, 32),)),
        "cotangent": bell_draw(keys[1], (TOKENS, D), 1.0, 6.0, ((0, 32),)),
        "lengths": draw_lengths(jax.random.fold_in(keys[19], 71), 0),
        "slot_of": draw_slot_of(jax.random.fold_in(keys[19], 71), 0),
        "norm_gains": jnp.clip(1.0 + 0.1 * jax.random.normal(keys[4], (2, D), jnp.float32), 0.5, 1.5),
        "w_query": bell_draw(keys[5], (D, KEYS), D ** -0.5, 0.125, ((0, 16), (1, 2))),
        "w_key": bell_draw(keys[6], (D, KEYS), D ** -0.5, 0.125, ((0, 16), (1, 2))),
        "w_value": bell_draw(keys[7], (D, VALS), D ** -0.5, 0.125, ((0, 16), (1, 2))),
        "w_gate": bell_draw(keys[8], (D, VALS), D ** -0.5, 0.125, ((0, 16), (1, 2))),
        "w_decay": bell_draw(keys[9], (D, HEADS), D ** -0.5, 0.125, ((0, 16), (1, 2))),
        "w_beta": bell_draw(keys[10], (D, HEADS), D ** -0.5, 0.125, ((0, 16), (1, 2))),
        "conv_weights": bell_draw(keys[11], (WIDTH, CONV_CH), 0.5, 3.0, (), jnp.float32),
        "a_log": jnp.clip(jax.random.uniform(keys[12], (HEADS,), jnp.float32, -8.0, -2.5), -8.0, -2.5),
        "dt_bias": jnp.clip(jax.random.uniform(keys[13], (HEADS,), jnp.float32, -2.0, 0.0), -2.0, 0.0),
        "out_gain": jnp.clip(1.0 + 0.1 * jax.random.normal(keys[14], (DV,), jnp.float32), 0.5, 1.5),
        "w_out": bell_draw(keys[15], (VALS, D), (VALS // 4) ** -0.5, 0.1875, ((0, 2), (1, 16))),
        "w_mlp_gate": bell_draw(keys[16], (D, FF), D ** -0.5, 0.125, ((0, 16), (1, 2))),
        "w_mlp_up": bell_draw(keys[17], (D, FF), D ** -0.5, 0.125, ((0, 16), (1, 2))),
        "w_mlp_down": bell_draw(keys[18], (FF, D), (FF // 4) ** -0.5, 0.15625, ((0, 2), (1, 16))),
    }


EPS_ROW = 1e-06
EPS_UNIT = 1e-06
EPS_HEAD = 1e-05
HIGH = lax.Precision.HIGHEST

@jax.custom_vjp
def low(v):
    return lax.optimization_barrier(v.astype(jnp.bfloat16)).astype(jnp.float32)

@jax.custom_vjp
def low_back(v):
    return v

def low_keep(v):
    return (low(v), None)

def low_pass(kept, grad):
    return (grad,)

def back_keep(v):
    return (v, None)

def back_low(kept, grad):
    return (low(grad),)
low.defvjp(low_keep, low_pass)
low_back.defvjp(back_keep, back_low)

def product(left, right):
    return jnp.dot(left, right, precision=HIGH, preferred_element_type=jnp.float32)

def row_norm(values, gain):
    return values * lax.rsqrt(lax.optimization_barrier(jnp.mean(values * values, axis=-1, keepdims=True)) + EPS_ROW) * gain

def unit_rows(values):
    return values * lax.rsqrt(lax.optimization_barrier(jnp.sum(values * values, axis=-1, keepdims=True)) + EPS_UNIT)

def group_marks(lengths):
    seq_ends = jnp.cumsum(lengths, axis=1)
    begins = seq_ends - lengths
    position = jnp.arange(GROUP_ROWS, dtype=jnp.int32)
    starts = jnp.any(position[None, :, None] == begins[:, None, :], axis=2).astype(jnp.float32)
    live_mask = (position[None, :] < seq_ends[:, -1:]).astype(jnp.float32)
    segment = jnp.cumsum(starts.astype(jnp.int32), axis=1)
    return (starts, live_mask, segment)

def conv_group(joined, conv_taps, segment):
    summed = conv_taps[0] * joined
    for offset in range(1, WIDTH):
        shifted = jnp.pad(joined, ((offset, 0), (0, 0)))[:-offset]
        before = jnp.pad(segment, (offset, 0), constant_values=-1)[:-offset]
        summed = summed + conv_taps[offset] * shifted * (before == segment).astype(jnp.float32)[:, None]
    return jax.nn.silu(summed)

def rule_step(memory, inputs):
    queries, key_vecs, values, retain, beta_gate = inputs
    decayed = retain[:, None, None] * memory
    predicted = jnp.einsum('hvk,hk->hv', decayed, key_vecs, precision=HIGH)
    memory = decayed + (beta_gate[:, None] * (values - predicted))[:, :, None] * key_vecs[:, None, :]
    return (memory, jnp.einsum('hvk,hk->hv', memory, queries, precision=HIGH))

def block_steps(memory, pieces):
    return lax.scan(rule_step, memory, pieces)

def group_rule(pieces):
    blocks = tuple((member.reshape((GROUP_ROWS // BLOCK, BLOCK) + member.shape[1:]) for member in pieces))
    memory = jnp.zeros((HEADS, DV, DK), jnp.float32)
    _, results = lax.scan(jax.checkpoint(block_steps), memory, blocks)
    return results.reshape(GROUP_ROWS, HEADS, DV)

def forward(tokens, norm_gains, w_query, w_key, w_value, w_gate, w_decay, w_beta, conv_weights, a_log, dt_bias, out_gain, w_out, w_mlp_gate, w_mlp_up, w_mlp_down, starts, live_mask, segment):
    row_count = tokens.shape[0]
    key_width = HEADS * DK
    first_in = low(row_norm(tokens, norm_gains[0]))
    joined = low_back(product(first_in, jnp.concatenate([w_query, w_key, w_value], axis=1)))
    gate_in = low_back(product(first_in, w_gate))
    decay_in = low_back(product(first_in, w_decay))
    beta_in = low_back(product(first_in, w_beta))
    activated = jax.vmap(conv_group, in_axes=(0, None, 0))(joined.reshape(N_DP, GROUP_ROWS, -1), conv_weights, segment)
    activated = activated.reshape(row_count, -1)
    queries = low(unit_rows(activated[:, :key_width].reshape(row_count, HEADS, DK)) * DK ** (-0.5))
    key_vecs = low(unit_rows(activated[:, key_width:2 * key_width].reshape(row_count, HEADS, DK)))
    values = low(activated[:, 2 * key_width:].reshape(row_count, HEADS, DV))
    beta_gate = jax.nn.sigmoid(beta_in)
    retain = jnp.exp(-jnp.exp(a_log) * jax.nn.softplus(decay_in + dt_bias)) * (1.0 - starts.reshape(row_count, 1))
    pieces = tuple((member.reshape((N_DP, GROUP_ROWS) + member.shape[1:]) for member in (queries, key_vecs, values, retain, beta_gate)))
    mixture = lax.map(jax.checkpoint(group_rule), pieces).reshape(row_count, HEADS, DV)
    normed = mixture * lax.rsqrt(lax.optimization_barrier(jnp.mean(mixture * mixture, axis=2, keepdims=True)) + EPS_HEAD) * out_gain
    heads_out = low((normed * jax.nn.silu(gate_in.reshape(row_count, HEADS, DV))).reshape(row_count, HEADS * DV))
    live_col = live_mask.reshape(row_count, 1)
    middle = tokens + live_col * low_back(product(heads_out, w_out))
    second_in = low(row_norm(middle, norm_gains[1]))
    gate_pre = low_back(product(second_in, w_mlp_gate))
    up_proj = low_back(product(second_in, w_mlp_up))
    hidden = low(jax.nn.silu(gate_pre) * up_proj)
    return middle + live_col * low_back(product(hidden, w_mlp_down))

def reference(tokens, cotangent, lengths, slot_of, norm_gains, w_query, w_key, w_value, w_gate, w_decay, w_beta, conv_weights, a_log, dt_bias, out_gain, w_out, w_mlp_gate, w_mlp_up, w_mlp_down):
    starts, live_mask, segment = group_marks(lengths)
    placed = jnp.zeros((TOKENS, D), jnp.float32).at[slot_of].set(tokens.astype(jnp.float32))
    pulled = jnp.zeros((TOKENS, D), jnp.float32).at[slot_of].set(cotangent.astype(jnp.float32))
    params = (norm_gains, w_query.astype(jnp.float32), w_key.astype(jnp.float32), w_value.astype(jnp.float32), w_gate.astype(jnp.float32), w_decay.astype(jnp.float32), w_beta.astype(jnp.float32), conv_weights, a_log, dt_bias, out_gain, w_out.astype(jnp.float32), w_mlp_gate.astype(jnp.float32), w_mlp_up.astype(jnp.float32), w_mlp_down.astype(jnp.float32))

    def apply_layer(inputs, *weights):
        return forward(inputs, *weights, starts, live_mask, segment)
    result, pullback = jax.vjp(apply_layer, placed, *params)
    gradients = pullback(pulled)
    return (result[slot_of].astype(jnp.bfloat16), gradients[0][slot_of].astype(jnp.bfloat16), gradients[1], gradients[2], gradients[3], gradients[4], gradients[5], gradients[6], gradients[7], gradients[8], gradients[9], gradients[10], gradients[11], gradients[12], gradients[13], gradients[14], gradients[15])
```

```python
import functools

import jax
import jax.numpy as jnp
from jax import lax
from jax.experimental import pallas as pl
from jax.experimental.pallas import tpu as pltpu
from jax.sharding import PartitionSpec as P

bf = jnp.bfloat16
f32 = jnp.float32
DK = 128
DV = 256
CHUNK = 128
LANES = 128
EPS_ROW = 1e-06
EPS_UNIT = 1e-06
EPS_HEAD = 1e-05
NEG = -1e30


def nn(left, right):
    return lax.dot_general(left.astype(bf), right.astype(bf), (((1,), (0,)), ((), ())), preferred_element_type=f32)


def nt(left, right):
    return lax.dot_general(left.astype(bf), right.astype(bf), (((1,), (1,)), ((), ())), preferred_element_type=f32)


def tn(left, right):
    return lax.dot_general(left.astype(bf), right.astype(bf), (((0,), (0,)), ((), ())), preferred_element_type=f32)


def exact(left, right):
    return lax.dot_general(left, right, (((1,), (0,)), ((), ())), precision=lax.Precision.HIGHEST, preferred_element_type=f32)


def softplus(v):
    return jnp.maximum(v, 0.0) + jnp.log(1.0 + jnp.exp(-jnp.abs(v)))


def sigmoid(v):
    return 1.0 / (1.0 + jnp.exp(-v))


def unit_lower_inverses(systems, places, others):
    eye = (places == others).astype(f32)
    size = 16
    same = (places // size) == (others // size)
    power = [jnp.where(same, a, 0.0) for a in systems]
    inverse = [eye - a for a in power]
    span = 2
    while span < size:
        power = [nn(a, a) for a in power]
        inverse = [t + nn(t, a) for t, a in zip(inverse, power)]
        span *= 2
    while size < places.shape[0]:
        corner = ((places // (2 * size)) == (others // (2 * size))) & ((places // size) != (others // size))
        steps = [nn(jnp.where(corner, a, 0.0), t) for a, t in zip(systems, inverse)]
        inverse = [t - nn(t, s) for t, s in zip(inverse, steps)]
        size *= 2
    return inverse


def conv_channels(padded, taps, marks, columns):
    total = taps[0:1, columns] * padded[8 : 8 + CHUNK, columns]
    for offset in range(1, 4):
        total = total + (taps[offset : offset + 1, columns] * marks[:, offset : offset + 1]) * padded[8 - offset : 8 - offset + CHUNK, columns]
    return total


def decay_terms(decays, head_params):
    biased = decays + head_params[0:1, :]
    log_decay = -head_params[1:2, :] * softplus(biased)
    return biased, log_decay


def chunk_terms(heads, decays, head_params, marks, seg_row, places, others):
    biased, log_decay = decay_terms(decays, head_params)
    lower = (places >= others).astype(f32)
    cum = exact(lower, log_decay)
    cum_rows = cum.T
    beta = sigmoid(decays)
    seg = marks[:, 0:1]
    causal = (places >= others) & (seg == seg_row)
    opening = marks[:, 4:5] > 0.0
    closing = marks[:, 5:6] > 0.0
    terms = []
    for head in range(heads):
        col = cum[:, head : head + 1]
        row = cum_rows[head : head + 1, :]
        decay = jnp.exp(jnp.where(causal, col - row, NEG))
        opened = jnp.exp(jnp.where(opening, col, NEG))
        last = cum[CHUNK - 1 : CHUNK, head : head + 1]
        closed = jnp.exp(jnp.where(closing, last - col, NEG))
        opened_last = opened[CHUNK - 1 : CHUNK, :]
        terms.append((decay, opened, closed, opened_last, beta[:, heads + head : heads + head + 1]))
    return biased, log_decay, beta, terms


def forward_kernel(heads, proj, marks_ref, seg_ref, taps, params, gain, out, kept_state, kept_inverse, state, padded):
    keys = heads * DK
    vals = heads * DV
    conv_width = 2 * keys + vals

    @pl.when(pl.program_id(1) == 0)
    def _():
        state[...] = jnp.zeros_like(state)
        padded[0:8, :] = jnp.zeros((8, conv_width), f32)

    padded[8:, :] = proj[:, :conv_width].astype(f32)
    marks = marks_ref[...]
    places = lax.broadcasted_iota(jnp.int32, (CHUNK, CHUNK), 0)
    others = lax.broadcasted_iota(jnp.int32, (CHUNK, CHUNK), 1)
    decays = proj[:, conv_width + vals :].astype(f32)
    _, _, _, terms = chunk_terms(heads, decays, params[...], marks, seg_ref[0], places, others)
    strict = places > others
    queries, key_vecs, values = [], [], []
    for head in range(heads):
        summed = conv_channels(padded, taps, marks, slice(head * DK, head * DK + DK))
        act = summed * sigmoid(summed)
        queries.append((act * (lax.rsqrt(jnp.sum(act * act, axis=1, keepdims=True) + EPS_UNIT) * DK**-0.5)).astype(bf))
        summed = conv_channels(padded, taps, marks, slice(keys + head * DK, keys + head * DK + DK))
        act = summed * sigmoid(summed)
        key_vecs.append((act * lax.rsqrt(jnp.sum(act * act, axis=1, keepdims=True) + EPS_UNIT)).astype(bf))
    dots = [nt(jnp.concatenate([q, k], axis=0), k) for q, k in zip(queries, key_vecs)]
    systems = [jnp.where(strict, term[4] * term[0] * dot[CHUNK:], 0.0) for term, dot in zip(terms, dots)]
    inverses = unit_lower_inverses(systems, places, others)
    for head in range(heads):
        summed = conv_channels(padded, taps, marks, slice(2 * keys + head * DV, 2 * keys + head * DV + DV))
        values.append((summed * sigmoid(summed)).astype(bf).astype(f32))
    padded[0:8, :] = padded[CHUNK : CHUNK + 8, :]
    before = [state[head] for head in range(heads)]
    for head in range(heads):
        kept_state[0, head] = before[head].astype(bf)
        kept_inverse[:, head * CHUNK : head * CHUNK + CHUNK] = inverses[head].astype(bf)
    reads = [nn(jnp.concatenate([k, q], axis=0), s) for k, q, s in zip(key_vecs, queries, before)]
    rights = [term[4] * (v - term[1] * read[:CHUNK]) for term, v, read in zip(terms, values, reads)]
    news = [nn(t, r) for t, r in zip(inverses, rights)]
    mixed = [
        term[1] * read[CHUNK:] + nn(dot[:CHUNK] * term[0], new)
        for term, read, dot, new in zip(terms, reads, dots, news)
    ]
    for head in range(heads):
        term = terms[head]
        state[head] = term[3] * before[head] + tn(key_vecs[head], term[2] * news[head])
    for head in range(heads):
        gate = proj[:, conv_width + head * DV : conv_width + head * DV + DV].astype(f32)
        mix = mixed[head]
        scale = lax.rsqrt(jnp.mean(mix * mix, axis=1, keepdims=True) + EPS_HEAD)
        out[:, head * DV : head * DV + DV] = (mix * scale * gain[...] * (gate * sigmoid(gate))).astype(bf)


def backward_kernel(heads, proj, prev_rows, grads, marks_ref, seg_ref, taps, params, gain, kept_state, kept_inverse,
                    proj_grad, taps_grad, params_grad, gain_grad, state_grad, padded, summed_grad):
    keys = heads * DK
    vals = heads * DV
    conv_width = 2 * keys + vals
    step = pl.program_id(1)

    @pl.when((pl.program_id(0) == 0) & (step == 0))
    def _():
        taps_grad[...] = jnp.zeros_like(taps_grad)
        params_grad[...] = jnp.zeros_like(params_grad)
        gain_grad[...] = jnp.zeros_like(gain_grad)

    @pl.when(step == 0)
    def _():
        state_grad[...] = jnp.zeros_like(state_grad)
        summed_grad[CHUNK:, :] = jnp.zeros((8, conv_width), f32)

    marks = marks_ref[...]
    padded[0:8, :] = prev_rows[...].astype(f32)[-8:, :conv_width]
    padded[8:, :] = proj[:, :conv_width].astype(f32)
    places = lax.broadcasted_iota(jnp.int32, (CHUNK, CHUNK), 0)
    others = lax.broadcasted_iota(jnp.int32, (CHUNK, CHUNK), 1)
    decays = proj[:, conv_width + vals :].astype(f32)
    biased, log_decay, beta, terms = chunk_terms(heads, decays, params[...], marks, seg_ref[0], places, others)
    strict = places > others
    q_sums, k_sums, v_sums = [], [], []
    q_acts, k_acts, q_scale, k_scale = [], [], [], []
    queries, key_vecs, values = [], [], []
    for head in range(heads):
        summed = conv_channels(padded, taps, marks, slice(head * DK, head * DK + DK))
        act = summed * sigmoid(summed)
        scale = lax.rsqrt(jnp.sum(act * act, axis=1, keepdims=True) + EPS_UNIT)
        queries.append((act * (scale * DK**-0.5)).astype(bf))
        q_sums.append(summed)
        q_acts.append(act)
        q_scale.append(scale)
        summed = conv_channels(padded, taps, marks, slice(keys + head * DK, keys + head * DK + DK))
        act = summed * sigmoid(summed)
        scale = lax.rsqrt(jnp.sum(act * act, axis=1, keepdims=True) + EPS_UNIT)
        key_vecs.append((act * scale).astype(bf))
        k_sums.append(summed)
        k_acts.append(act)
        k_scale.append(scale)
        summed = conv_channels(padded, taps, marks, slice(2 * keys + head * DV, 2 * keys + head * DV + DV))
        values.append((summed * sigmoid(summed)).astype(bf).astype(f32))
        v_sums.append(summed)
    pairs = [jnp.concatenate([q, k], axis=0) for q, k in zip(queries, key_vecs)]
    dots = [nt(pair, k) for pair, k in zip(pairs, key_vecs)]
    before = [kept_state[0, head] for head in range(heads)]
    after_grad = [state_grad[head] for head in range(heads)]
    inverses = [kept_inverse[:, head * CHUNK : head * CHUNK + CHUNK] for head in range(heads)]
    reads = [nn(pair, s) for pair, s in zip(pairs, before)]
    gaps = [v - term[1] * read[CHUNK:] for term, v, read in zip(terms, values, reads)]
    news = [nn(t, term[4] * g) for t, term, g in zip(inverses, terms, gaps)]
    scores = [(dot[:CHUNK] * term[0]) for dot, term in zip(dots, terms)]
    mixed = [term[1] * read[:CHUNK] + nn(score, new) for term, read, score, new in zip(terms, reads, scores, news)]
    mix_grads = []
    gain_row = gain[...]
    for head in range(heads):
        columns = slice(head * DV, head * DV + DV)
        gate_columns = slice(conv_width + head * DV, conv_width + head * DV + DV)
        gate = proj[:, gate_columns].astype(f32)
        grad = grads[:, columns].astype(f32)
        mix = mixed[head]
        scale = lax.rsqrt(jnp.mean(mix * mix, axis=1, keepdims=True) + EPS_HEAD)
        soft = sigmoid(gate)
        normed = mix * scale
        grad_normed = grad * normed
        proj_grad[:, gate_columns] = (grad_normed * gain_row * (soft * (1.0 + gate * (1.0 - soft)))).astype(bf)
        silu = gate * soft
        gain_grad[0:1, :] += jnp.sum(grad_normed * silu, axis=0, keepdims=True)
        inner = grad * silu * gain_row
        mix_grads.append(scale * inner - mix * (scale * scale * scale) * jnp.mean(inner * mix, axis=1, keepdims=True))
    pushes = [nn(k, g) for k, g in zip(key_vecs, after_grad)]
    new_grads = [tn(score, grad) + term[2] * push for score, grad, term, push in zip(scores, mix_grads, terms, pushes)]
    score_grads = [nt(grad, new) for grad, new in zip(mix_grads, news)]
    right_grads = [tn(t, grad) for t, grad in zip(inverses, new_grads)]
    system_grads = [jnp.where(strict, -nt(grad, new), 0.0) for grad, new in zip(right_grads, news)]
    cum_grad = jnp.zeros((CHUNK, LANES), f32)
    beta_grads = jnp.zeros((CHUNK, LANES), f32)
    cross_rows = []
    lanes = lax.broadcasted_iota(jnp.int32, (CHUNK, LANES), 1)
    rows_down = lax.broadcasted_iota(jnp.int32, (CHUNK, 1), 0)
    raised = []
    for head in range(heads):
        decay, opened, closed, opened_last, strength = terms[head]
        read_key = reads[head][CHUNK:]
        read_query = reads[head][:CHUNK]
        gram = dots[head][CHUNK:]
        decayed_score_grad = score_grads[head] * decay
        decayed_system = system_grads[head] * decay
        system_gram = decayed_system * gram
        crossing = decayed_score_grad * dots[head][:CHUNK] + strength * system_gram
        value_grad = strength * right_grads[head]
        beta_grad = jnp.sum(system_gram, axis=1, keepdims=True) + jnp.sum(right_grads[head] * gaps[head], axis=1, keepdims=True)
        open_grad = jnp.sum(mix_grads[head] * read_query - value_grad * read_key, axis=1, keepdims=True)
        close_grad = closed * jnp.sum(news[head] * pushes[head], axis=1, keepdims=True)
        last_grad = jnp.sum(close_grad, axis=0, keepdims=True) + opened_last * jnp.sum(
            jnp.sum(after_grad[head] * before[head].astype(f32), axis=1, keepdims=True), axis=0, keepdims=True
        )
        col = jnp.sum(crossing, axis=1, keepdims=True) + opened * open_grad - close_grad
        col = col + jnp.where(rows_down == CHUNK - 1, last_grad, 0.0)
        cross_rows.append(jnp.sum(crossing, axis=0, keepdims=True))
        cum_grad = jnp.where(lanes == head, col, cum_grad)
        beta_grads = jnp.where(lanes == heads + head, beta_grad, beta_grads)
        raised.append((decayed_score_grad.astype(bf), (strength * decayed_system).astype(bf), value_grad, opened))
    cross = jnp.concatenate(cross_rows + [jnp.zeros((CHUNK - heads, CHUNK), f32)], axis=0).T
    cum_grad = cum_grad - cross
    stacked = [
        jnp.concatenate([(opened * grad).astype(bf), (-opened * value_grad).astype(bf)], axis=0)
        for (_, _, value_grad, opened), grad in zip(raised, mix_grads)
    ]
    through = [nt(x, s) for x, s in zip(stacked, before)]
    grams = [jnp.concatenate([item[0], item[1]], axis=0) for item in raised]
    direct = [nn(g, k) for g, k in zip(grams, key_vecs)]
    turned = [tn(g, pair) for g, pair in zip(grams, pairs)]
    pushed = [nt(terms[head][2] * news[head], after_grad[head]) for head in range(heads)]
    for head in range(heads):
        state_grad[head] = terms[head][3] * after_grad[head] + tn(pairs[head], stacked[head])
    for head in range(heads):
        query_grad = (through[head][:CHUNK] + direct[head][:CHUNK]) * DK**-0.5
        key_grad = through[head][CHUNK:] + direct[head][CHUNK:] + turned[head] + pushed[head]
        for grad, act, scale, summed, start in (
            (query_grad, q_acts[head], q_scale[head], q_sums[head], head * DK),
            (key_grad, k_acts[head], k_scale[head], k_sums[head], keys + head * DK),
        ):
            inner = scale * (grad - act * (scale * scale) * jnp.sum(grad * act, axis=1, keepdims=True))
            soft = sigmoid(summed)
            summed_grad[0:CHUNK, start : start + DK] = inner * (soft * (1.0 + summed * (1.0 - soft)))
        summed = v_sums[head]
        soft = sigmoid(summed)
        start = 2 * keys + head * DV
        summed_grad[0:CHUNK, start : start + DV] = raised[head][2] * (soft * (1.0 + summed * (1.0 - soft)))
    for start in range(0, conv_width, LANES):
        columns = slice(start, start + LANES)
        grad = summed_grad[0:CHUNK, columns]
        total = taps[0:1, columns] * grad
        taps_grad[0:1, columns] += jnp.sum(grad * padded[8 : 8 + CHUNK, columns], axis=0, keepdims=True)
        for offset in range(1, 4):
            later = summed_grad[offset : offset + CHUNK, columns]
            total = total + (taps[offset : offset + 1, columns] * marks[:, 5 + offset : 6 + offset]) * later
            taps_grad[offset : offset + 1, columns] += jnp.sum(
                (grad * marks[:, offset : offset + 1]) * padded[8 - offset : 8 - offset + CHUNK, columns], axis=0, keepdims=True
            )
        proj_grad[:, columns] = total.astype(bf)
    summed_grad[CHUNK:, :] = summed_grad[0:8, :]
    upper = (places <= others).astype(f32)
    log_grad = exact(upper, cum_grad)
    decay_grad = log_grad * (-params[1:2, :]) * sigmoid(biased)
    both = decay_grad + beta_grads * beta * (1.0 - beta)
    proj_grad[:, conv_width + vals :] = both.astype(bf)
    params_grad[0:1, :] += jnp.sum(log_grad * log_decay, axis=0, keepdims=True)
    params_grad[1:2, :] += jnp.sum(decay_grad, axis=0, keepdims=True)


def mixer_forward(proj, marks, seg_rows, taps, params, gain, group_rows):
    rows, width = proj.shape
    heads = (width - LANES) // (2 * DK + 2 * DV)
    groups = rows // group_rows
    chunks = group_rows // CHUNK
    conv_width = heads * (2 * DK + DV)
    at = lambda g, c: (g * chunks + c, 0)
    return pl.pallas_call(
        functools.partial(forward_kernel, heads),
        grid=(groups, chunks),
        in_specs=[
            pl.BlockSpec((CHUNK, width), at),
            pl.BlockSpec((CHUNK, LANES), at),
            pl.BlockSpec((1, 1, CHUNK), lambda g, c: (g * chunks + c, 0, 0)),
            pl.BlockSpec((4, conv_width), lambda g, c: (0, 0)),
            pl.BlockSpec((8, LANES), lambda g, c: (0, 0)),
            pl.BlockSpec((1, DV), lambda g, c: (0, 0)),
        ],
        out_specs=[
            pl.BlockSpec((CHUNK, heads * DV), at),
            pl.BlockSpec((1, heads, DK, DV), lambda g, c: (g * chunks + c, 0, 0, 0)),
            pl.BlockSpec((CHUNK, heads * CHUNK), at),
        ],
        out_shape=[
            jax.ShapeDtypeStruct((rows, heads * DV), bf),
            jax.ShapeDtypeStruct((groups * chunks, heads, DK, DV), bf),
            jax.ShapeDtypeStruct((rows, heads * CHUNK), bf),
        ],
        scratch_shapes=[pltpu.VMEM((heads, DK, DV), f32), pltpu.VMEM((CHUNK + 8, conv_width), f32)],
        compiler_params=pltpu.CompilerParams(vmem_limit_bytes=48 * 2**20),
        cost_estimate=pl.CostEstimate(flops=rows * heads * 1500000, bytes_accessed=rows * width * 8, transcendentals=0),
        name="mixer_forward",
    )(proj, marks, seg_rows, taps, params, gain)


def mixer_backward(proj, grads, marks, seg_rows, taps, params, gain, states, inverses, group_rows):
    rows, width = proj.shape
    heads = (width - LANES) // (2 * DK + 2 * DV)
    groups = rows // group_rows
    chunks = group_rows // CHUNK
    conv_width = heads * (2 * DK + DV)
    at = lambda g, c: (g * chunks + chunks - 1 - c, 0)
    prev = lambda g, c: (jnp.maximum((g * chunks + chunks - 1 - c) * (CHUNK // 16) - 1, 0), 0)
    return pl.pallas_call(
        functools.partial(backward_kernel, heads),
        grid=(groups, chunks),
        in_specs=[
            pl.BlockSpec((CHUNK, width), at),
            pl.BlockSpec((16, width), prev),
            pl.BlockSpec((CHUNK, heads * DV), at),
            pl.BlockSpec((CHUNK, LANES), at),
            pl.BlockSpec((1, 1, CHUNK), lambda g, c: (g * chunks + chunks - 1 - c, 0, 0)),
            pl.BlockSpec((4, conv_width), lambda g, c: (0, 0)),
            pl.BlockSpec((8, LANES), lambda g, c: (0, 0)),
            pl.BlockSpec((1, DV), lambda g, c: (0, 0)),
            pl.BlockSpec((1, heads, DK, DV), lambda g, c: (g * chunks + chunks - 1 - c, 0, 0, 0)),
            pl.BlockSpec((CHUNK, heads * CHUNK), at),
        ],
        out_specs=[
            pl.BlockSpec((CHUNK, width), at),
            pl.BlockSpec((4, conv_width), lambda g, c: (0, 0)),
            pl.BlockSpec((8, LANES), lambda g, c: (0, 0)),
            pl.BlockSpec((8, DV), lambda g, c: (0, 0)),
        ],
        out_shape=[
            jax.ShapeDtypeStruct((rows, width), bf),
            jax.ShapeDtypeStruct((4, conv_width), f32),
            jax.ShapeDtypeStruct((8, LANES), f32),
            jax.ShapeDtypeStruct((8, DV), f32),
        ],
        scratch_shapes=[
            pltpu.VMEM((heads, DK, DV), f32),
            pltpu.VMEM((CHUNK + 8, conv_width), f32),
            pltpu.VMEM((CHUNK + 8, conv_width), f32),
        ],
        compiler_params=pltpu.CompilerParams(vmem_limit_bytes=48 * 2**20),
        cost_estimate=pl.CostEstimate(flops=rows * heads * 3000000, bytes_accessed=rows * width * 12, transcendentals=0),
        name="mixer_backward",
    )(proj, proj, grads, marks, seg_rows, taps, params, gain, states, inverses)


def group_marks(lengths, group_rows):
    groups, count = lengths.shape
    position = jnp.arange(group_rows, dtype=jnp.int32)[None, :]
    segment = jnp.zeros((groups, group_rows), jnp.int32)
    end = jnp.zeros((groups, 1), jnp.int32)
    for number in range(count):
        segment = segment + (position >= end).astype(jnp.int32)
        end = end + lengths[:, number : number + 1]
    live = (position < end).astype(f32)
    padded = jnp.pad(segment, ((0, 0), (CHUNK, CHUNK)))
    later = lambda offset: padded[:, CHUNK + offset : CHUNK + offset + group_rows]
    chunked = segment.reshape(groups, group_rows // CHUNK, CHUNK)
    before = padded[:, CHUNK - 1 : CHUNK - 1 + group_rows].reshape(chunked.shape)[:, :, :1]
    columns = [segment]
    columns += [later(-offset) == segment for offset in (1, 2, 3)]
    columns += [(chunked == before).reshape(segment.shape), (chunked == chunked[:, :, -1:]).reshape(segment.shape)]
    columns += [later(offset) == segment for offset in (1, 2, 3)]
    marks = jnp.stack([c.astype(f32) for c in columns], axis=-1).reshape(groups * group_rows, len(columns))
    marks = jnp.pad(marks, ((0, 0), (0, LANES - len(columns))))
    seg_rows = segment.astype(f32).reshape(groups * group_rows // CHUNK, 1, CHUNK)
    return marks, seg_rows, live


RING = (0, 1, 3, 2)


def matmul(left, right):
    return jnp.dot(left, right, preferred_element_type=f32)


def outer_sum(left, right):
    return lax.dot_general(left, right, (((0,), (0,)), ((), ())), preferred_element_type=f32)


def times_back(left, right):
    return lax.dot_general(left, right, (((1,), (1,)), ((), ())), preferred_element_type=f32)


def norm_back(inputs, scale, gain, grad_out):
    scaled = grad_out * gain
    grad_in = scale * scaled - inputs * scale**3 * jnp.mean(scaled * inputs, axis=1, keepdims=True)
    return (grad_in, jnp.sum(grad_out * inputs * scale, axis=0))


class Layout:
    def __init__(self):
        self.ways = lax.axis_size("dp")
        self.spans = self.ways // 8
        dp = lax.axis_index("dp")
        self.core = lax.axis_index("tensor")
        self.dp = dp
        self.turn = (dp // 4) % 2
        self.far = dp // 8
        near = dp % 4
        self.spot = near ^ (near >> 1)

    def ring(self, values, step):
        pairs = []
        for number in range(self.ways):
            near = number % 4
            pairs.append((number, number - near + RING[((near ^ (near >> 1)) + step) % 4]))
        return lax.ppermute(values, "dp", pairs)

    def flip(self, values, bit):
        return lax.ppermute(values, "dp", [(n, n ^ bit) for n in range(self.ways)])

    def turned(self, values):
        return self.flip(values, 4)

    def crossed(self, values):
        return lax.ppermute(values, "tensor", [(0, 1), (1, 0)])

    def far_bits(self):
        bit = 8
        while bit < self.ways:
            yield bit
            bit *= 2

    def sources(self):
        places = jnp.arange(self.ways, dtype=jnp.int32)
        step = places // (2 * self.spans)
        jump = (places // 2) % self.spans
        spot = (self.spot + step) % 4
        return ((self.far ^ jump) * 2 + places % 2) * 4 + (spot ^ (spot >> 1))

    def ordered(self, first, second, flag):
        return jnp.where(
            flag == 0, jnp.concatenate([first, second], axis=0), jnp.concatenate([second, first], axis=0)
        )

    def halves(self, weight):
        half = weight.shape[1] // 2
        keep = lax.dynamic_slice_in_dim(weight, self.turn * half, half, 1)
        give = lax.dynamic_slice_in_dim(weight, (1 - self.turn) * half, half, 1)
        return keep, give

    def spread(self, weights):
        pairs = [self.halves(weight) for weight in weights]
        keep = jnp.concatenate([pair[0] for pair in pairs], axis=1)
        give = jnp.concatenate([pair[1] for pair in pairs], axis=1)
        short = -keep.shape[1] % LANES
        if short:
            keep = jnp.pad(keep, ((0, 0), (0, short)))
            give = jnp.pad(give, ((0, 0), (0, short)))
        chunk = self.ordered(keep, self.turned(give), self.turn)
        for bit in self.far_bits():
            chunk = jnp.concatenate([chunk, self.flip(chunk, bit)], axis=0)
        half = chunk.shape[0] // 2
        ahead = self.ring(chunk, -1)
        behind = self.ring(chunk, 1)
        top = self.ring(ahead[:half], -1)
        bottom = self.ring(behind[half:], 1)
        return jnp.concatenate([chunk, ahead, top, bottom, behind], axis=0)

    def collect(self, grad):
        width = grad.shape[1]
        pieces = grad.reshape(4, -1, width)
        half = pieces.shape[1] // 2
        up = self.ring(pieces[2, :half].astype(bf), 1)
        down = self.ring(pieces[2, half:].astype(bf), -1)
        up = self.ring(jnp.concatenate([pieces[1, :half] + up, pieces[1, half:]], axis=0).astype(bf), 1)
        down = self.ring(jnp.concatenate([pieces[3, :half], pieces[3, half:] + down], axis=0).astype(bf), -1)
        own = pieces[0] + up + down
        for bit in reversed(list(self.far_bits())):
            half = own.shape[0] // 2
            own = own[:half] + self.flip(own[half:].astype(bf), bit)
        half = own.shape[0] // 2
        mine = lax.dynamic_slice_in_dim(own, self.turn * half, half, 0)
        other = lax.dynamic_slice_in_dim(own, (1 - self.turn) * half, half, 0)
        return mine, self.turned(other.astype(bf)).astype(f32)

    def columns(self, mine, theirs, start, stop):
        return jnp.where(
            self.turn == 0,
            jnp.concatenate([mine[:, start:stop], theirs[:, start:stop]], axis=1),
            jnp.concatenate([theirs[:, start:stop], mine[:, start:stop]], axis=1),
        )

    def rows_of(self, own):
        across = self.crossed(own)
        there = self.turned(own)
        return across, there, self.crossed(there)

    def own_of(self, mine, give):
        total = mine + self.crossed(give.astype(bf))
        return total[0] + self.turned(total[1].astype(bf))

    def everywhere(self, values):
        bit = 1
        while bit < self.ways:
            values = values + self.flip(values, bit)
            bit *= 2
        return values + self.crossed(values)


def flat(parts):
    joined = jnp.concatenate([part.reshape(-1) for part in parts])
    return jnp.pad(joined, (0, -joined.shape[0] % (8 * LANES))).reshape(-1, LANES)


def shards(
    tokens, cotangent, lengths, slot_of, norm_gains, w_query, w_key, w_value, w_gate, w_decay, w_beta,
    conv_weights, a_log, dt_bias, out_gain, w_out, w_mlp_gate, w_mlp_up, w_mlp_down,
):
    lay = Layout()
    row_count, features = tokens.shape
    tensor_ways = lax.axis_size("tensor")
    device_count = lay.ways * tensor_ways
    group_rows = row_count * tensor_ways
    capacity = row_count // device_count + 2
    bulk_rows = device_count * capacity
    all_heads = a_log.shape[0]
    heads = all_heads // (2 * tensor_ways)
    keys_here = heads * DK
    vals_here = heads * DV
    all_keys = all_heads * DK
    conv_width = 2 * keys_here + vals_here
    share = lay.core * 2 + lay.turn

    target = slot_of // row_count
    within = slot_of % row_count
    hits = target[:, None] == jnp.arange(device_count, dtype=jnp.int32)[None, :]
    places = jnp.arange(row_count, dtype=jnp.int32)
    earlier = (places[:, None] >= places[None, :]).astype(bf)
    rank = jnp.sum(matmul(earlier, hits.astype(bf)) * hits.astype(f32), axis=1).astype(jnp.int32) - 1
    outgoing = target * capacity + rank
    sending = (jnp.arange(bulk_rows, dtype=jnp.int32)[:, None] == outgoing[None, :]).astype(bf)
    slot_mark = jnp.broadcast_to((within + 1).astype(bf)[:, None], (row_count, LANES))
    send_tokens = matmul(sending, jnp.concatenate([tokens, slot_mark], axis=1)).astype(bf)
    send_cot = matmul(sending, cotangent).astype(bf)

    def exchange(values):
        return lax.all_to_all(values, ("dp", "tensor"), split_axis=0, concat_axis=0, tiled=True)

    got_tokens = exchange(send_tokens)
    got_slot = got_tokens[:, features].astype(jnp.int32)
    landing = (places[:, None] + 1 == got_slot[None, :]).astype(bf)
    sources = lay.sources()
    block = features // lay.ways
    feature = jnp.arange(features, dtype=jnp.int32)
    turning = (feature[:, None] == (sources[:, None] * block + jnp.arange(block, dtype=jnp.int32)[None, :]).reshape(1, -1)).astype(bf)
    x_own = matmul(matmul(landing, got_tokens[:, :features]).astype(bf), turning)
    numbers = jnp.arange(lay.ways, dtype=jnp.int32)
    picking = (sources[:, None] == numbers[None, :]).astype(f32)

    def reordered_gain(gain):
        return jnp.sum(picking[:, :, None] * gain.reshape(1, lay.ways, block), axis=1).reshape(features)

    def straight_gain(grad):
        return jnp.sum(picking[:, :, None] * grad.reshape(lay.ways, 1, block), axis=0).reshape(features)

    gains = (reordered_gain(norm_gains[0]), reordered_gain(norm_gains[1]))

    pair_lengths = jnp.concatenate([lengths, lay.turned(lengths)], axis=0)
    marks, seg_rows, live = group_marks(pair_lengths, group_rows)
    live_own = lax.dynamic_slice_in_dim(live[0], lay.core * row_count, row_count)[:, None]
    starts = (share * keys_here, all_keys + share * keys_here, 2 * all_keys + share * vals_here)
    sizes = (keys_here, keys_here, vals_here)
    taps = jnp.concatenate(
        [lax.dynamic_slice_in_dim(conv_weights, start, size, 1) for start, size in zip(starts, sizes)], axis=1
    )
    log_here = lax.dynamic_slice_in_dim(a_log, share * heads, heads)
    bias_here = lax.dynamic_slice_in_dim(dt_bias, share * heads, heads)
    params = jnp.pad(jnp.stack([bias_here, jnp.exp(log_here)]), ((0, 6), (0, LANES - heads)))
    gain_row = out_gain[None, :]

    weights_in = lay.spread([w_query, w_key, w_value, w_gate, w_decay, w_beta])
    weights_out = lay.spread([w_out.T])
    weights_gate = lay.spread([w_mlp_gate])
    weights_up = lay.spread([w_mlp_up])
    weights_down = lay.spread([w_mlp_down.T])

    def group_order(own):
        across, there, beyond = lay.rows_of(own)
        return jnp.concatenate([lay.ordered(own, across, lay.core), lay.ordered(there, beyond, lay.core)], axis=0)

    def own_of_groups(partial):
        partial = partial.reshape(2, 2, row_count, features)
        mine = lax.dynamic_index_in_dim(partial, lay.core, 1, keepdims=False)
        give = lax.dynamic_index_in_dim(partial, 1 - lay.core, 1, keepdims=False)
        return lay.own_of(mine, give)

    def own_of_rows(partial):
        partial = partial.reshape(2, 2, row_count, features)
        return lay.own_of(partial[:, 0], partial[:, 1])

    def any_order(own):
        across, there, beyond = lay.rows_of(own)
        return jnp.concatenate([own, across, there, beyond], axis=0)

    scale_one = lax.rsqrt(jnp.mean(x_own * x_own, axis=1, keepdims=True) + EPS_ROW)
    first_rows = group_order((x_own * scale_one * gains[0]).astype(bf))
    proj = matmul(first_rows, weights_in)
    heads_out, states, inverses = mixer_forward(proj, marks, seg_rows, taps, params, gain_row, group_rows)
    middle = x_own + live_own * own_of_groups(times_back(heads_out, weights_out))
    scale_two = lax.rsqrt(jnp.mean(middle * middle, axis=1, keepdims=True) + EPS_ROW)
    second_rows = any_order((middle * scale_two * gains[1]).astype(bf))

    got_cot = exchange(send_cot)
    dy_own = matmul(matmul(landing, got_cot).astype(bf), turning)
    branch_rows = any_order((live_own * dy_own).astype(bf))

    gate_pre = matmul(second_rows, weights_gate)
    up_proj = matmul(second_rows, weights_up)
    hidden = (jax.nn.silu(gate_pre) * up_proj).astype(bf)
    grad_hidden = matmul(branch_rows, weights_down)
    soft = jax.nn.sigmoid(gate_pre)
    grad_gate = (grad_hidden * up_proj * soft * (1.0 + gate_pre * (1.0 - soft))).astype(bf)
    grad_up = (grad_hidden * gate_pre * soft).astype(bf)
    down_grad = lay.collect(outer_sum(branch_rows, hidden))
    gate_grad = lay.collect(outer_sum(second_rows, grad_gate))
    up_grad = lay.collect(outer_sum(second_rows, grad_up))
    branch_own = own_of_rows(times_back(hidden, weights_down))
    result_own = (middle + live_own * branch_own).astype(bf)
    grad_second = own_of_rows(times_back(grad_gate, weights_gate) + times_back(grad_up, weights_up))
    grad_mid_norm, gain_two_grad = norm_back(middle, scale_two, gains[1], grad_second)
    grad_middle = dy_own + grad_mid_norm
    mix_rows = group_order((live_own * grad_middle).astype(bf))
    grad_heads = matmul(mix_rows, weights_out).astype(bf)
    out_grad = lay.collect(outer_sum(mix_rows, heads_out))
    proj_grad, taps_grad, params_grad, gain_grad = mixer_backward(
        proj, grad_heads, marks, seg_rows, taps, params, gain_row, states, inverses, group_rows
    )
    in_grad = lay.collect(outer_sum(first_rows, proj_grad))
    grad_first = own_of_groups(times_back(proj_grad, weights_in))
    grad_x_norm, gain_one_grad = norm_back(x_own, scale_one, gains[0], grad_first)
    grad_tokens = (grad_middle + grad_x_norm).astype(bf)

    def sent_back(own):
        straight = times_back(own, turning).astype(bf)
        back = exchange(outer_sum(landing, straight).astype(bf))
        return outer_sum(sending, back).astype(bf)

    output = sent_back(result_own)
    tokens_grad = sent_back(grad_tokens)

    conv_full = jnp.zeros(conv_weights.shape, f32)
    begin = 0
    for start, size in zip(starts, sizes):
        conv_full = lax.dynamic_update_slice_in_dim(conv_full, taps_grad[:, begin : begin + size], start, 1)
        begin += size
    log_full = lax.dynamic_update_slice_in_dim(jnp.zeros_like(a_log), params_grad[0, :heads], share * heads, 0)
    bias_full = lax.dynamic_update_slice_in_dim(jnp.zeros_like(dt_bias), params_grad[1, :heads], share * heads, 0)

    early = lay.everywhere(flat([conv_full, straight_gain(gain_two_grad), gain_grad[0], log_full, bias_full])).reshape(-1)
    late = lay.everywhere(flat([straight_gain(gain_one_grad)])).reshape(-1)[:features]
    conv_size = conv_full.size
    cuts = [conv_size, conv_size + features, conv_size + features + DV, conv_size + features + DV + all_heads]
    norm_grad = jnp.stack([late, early[cuts[0] : cuts[1]]])

    in_columns = []
    begin = 0
    for size in (keys_here, keys_here, vals_here, vals_here, heads, heads):
        in_columns.append(lay.columns(*in_grad, begin, begin + size))
        begin += size
    hidden_here = weights_gate.shape[1]
    return (
        output,
        tokens_grad,
        norm_grad,
        *in_columns,
        early[:conv_size].reshape(conv_full.shape),
        early[cuts[2] : cuts[3]],
        early[cuts[3] : cuts[3] + all_heads],
        early[cuts[1] : cuts[2]],
        lay.columns(*out_grad, 0, vals_here).T,
        lay.columns(*gate_grad, 0, hidden_here),
        lay.columns(*up_grad, 0, hidden_here),
        lay.columns(*down_grad, 0, hidden_here).T,
    )


def solution(mesh):
    return jax.shard_map(
        shards,
        mesh=mesh,
        in_specs=(
            P(("dp", "tensor"), None),
            P(("dp", "tensor"), None),
            P("dp", None),
            P(("dp", "tensor")),
            P(),
            P("dp", "tensor"),
            P("dp", "tensor"),
            P("dp", "tensor"),
            P("dp", "tensor"),
            P("dp", "tensor"),
            P("dp", "tensor"),
            P(),
            P(),
            P(),
            P(),
            P("tensor", "dp"),
            P("dp", "tensor"),
            P("dp", "tensor"),
            P("tensor", "dp"),
        ),
        out_specs=(
            P(("dp", "tensor"), None),
            P(("dp", "tensor"), None),
            P(),
            P("dp", "tensor"),
            P("dp", "tensor"),
            P("dp", "tensor"),
            P("dp", "tensor"),
            P("dp", "tensor"),
            P("dp", "tensor"),
            P(),
            P(),
            P(),
            P(),
            P("tensor", "dp"),
            P("dp", "tensor"),
            P("dp", "tensor"),
            P("tensor", "dp"),
        ),
        check_vma=False,
    )
```

```python
import functools

import jax
import jax.numpy as jnp
from jax import lax
from jax.experimental import pallas as pl
from jax.experimental.pallas import tpu as pltpu
from jax.sharding import PartitionSpec as P

bf = jnp.bfloat16
f32 = jnp.float32
DK = 128
DV = 256
CHUNK = 128
LANES = 128
GROUPS = 2
EPS_ROW = 1e-06
EPS_UNIT = 1e-06
EPS_HEAD = 1e-05
NEG = -1e30
VMEM_LIMIT = 56 * 2**20


def dot(left, right, left_dim, right_dim):
    return lax.dot_general(
        left.astype(bf), right.astype(bf), (((left_dim,), (right_dim,)), ((), ())), preferred_element_type=f32
    )


def nn(left, right):
    return dot(left, right, 1, 0)


def nt(left, right):
    return dot(left, right, 1, 1)


def tn(left, right):
    return dot(left, right, 0, 0)


def exact(left, right):
    return lax.dot_general(
        left, right, (((1,), (0,)), ((), ())), precision=lax.Precision.HIGHEST, preferred_element_type=f32
    )


def softplus(v):
    return jnp.maximum(v, 0.0) + jnp.log(1.0 + jnp.exp(-jnp.abs(v)))


def sigmoid(v):
    return 1.0 / (1.0 + jnp.exp(-v))


def unit_lower_inverses(systems, places, others):
    eye = (places == others).astype(f32)
    size = 16
    same = (places // size) == (others // size)
    power = [jnp.where(same, a, 0.0) for a in systems]
    inverse = [eye - a for a in power]
    span = 2
    while span < size:
        power = [nn(a, a) for a in power]
        inverse = [t + nn(t, a) for t, a in zip(inverse, power)]
        span *= 2
    while size < places.shape[0]:
        corner = ((places // (2 * size)) == (others // (2 * size))) & ((places // size) != (others // size))
        steps = [nn(jnp.where(corner, a, 0.0), t) for a, t in zip(systems, inverse)]
        inverse = [t - nn(t, s) for t, s in zip(inverse, steps)]
        size *= 2
    return inverse


def conv_channels(padded, group, taps, marks, columns):
    total = taps[0:1, columns] * padded[group, 8 : 8 + CHUNK, columns]
    for offset in range(1, 4):
        total = total + (taps[offset : offset + 1, columns] * marks[:, offset : offset + 1]) * (
            padded[group, 8 - offset : 8 - offset + CHUNK, columns]
        )
    return total


class Unit:
    def __init__(self, group, head, heads, first, lanes, shared):
        self.group = group
        self.head = head
        keys = heads * DK
        self.query_columns = slice(head * DK, head * DK + DK)
        self.key_columns = slice(keys + head * DK, keys + head * DK + DK)
        self.value_columns = slice(2 * keys + head * DV, 2 * keys + head * DV + DV)
        start = 2 * keys + heads * DV + head * DV
        self.gate_columns = slice(start, start + DV)
        self.out_columns = slice(head * DV, head * DV + DV)
        self.lane = first + head
        self.beta_lane = lanes + first + head
        cum, cum_rows, beta, causal, opening, closing = shared
        col = cum[:, self.lane : self.lane + 1]
        row = cum_rows[self.lane : self.lane + 1, :]
        self.decay = jnp.exp(jnp.where(causal, col - row, NEG))
        self.opened = jnp.exp(jnp.where(opening, col, NEG))
        last = cum[CHUNK - 1 : CHUNK, self.lane : self.lane + 1]
        self.closed = jnp.exp(jnp.where(closing, last - col, NEG))
        self.opened_last = self.opened[CHUNK - 1 : CHUNK, :]
        self.strength = beta[:, self.beta_lane : self.beta_lane + 1]


def chunk_units(heads, first, lanes, decays_ref, params, marks_ref, seg_ref, places, others):
    units, kept = [], []
    lower = (places >= others).astype(f32)
    for group in range(GROUPS):
        decays = decays_ref[0, group, 0]
        marks = marks_ref[group, 0]
        biased = decays + params[0:1, :]
        log_decay = -params[1:2, :] * softplus(biased)
        cum = exact(lower, log_decay)
        beta = sigmoid(decays)
        causal = (places >= others) & (marks[:, 0:1] == seg_ref[group, 0])
        shared = (cum, cum.T, beta, causal, marks[:, 4:5] > 0.0, marks[:, 5:6] > 0.0)
        kept.append((biased, log_decay, beta, marks))
        for head in range(heads):
            units.append(Unit(group, head, heads, first, lanes, shared))
    return units, kept


def forward_kernel(
    heads, first, lanes, core_ref, proj, decays, marks_ref, seg_ref, taps, params, gain, partner,
    out, kept_state, kept_inverse, state, padded,
):
    conv_width = heads * (2 * DK + DV)

    @pl.when(pl.program_id(0) == 0)
    def _():
        state[...] = jnp.zeros_like(state)
        padded[:, 0:8, :] = jnp.zeros((GROUPS, 8, conv_width), f32)

    for group in range(GROUPS):
        padded[group, 8:, :] = proj[0, group, 0, :, :conv_width].astype(f32)
    places = lax.broadcasted_iota(jnp.int32, (CHUNK, CHUNK), 0)
    others = lax.broadcasted_iota(jnp.int32, (CHUNK, CHUNK), 1)
    units, kept = chunk_units(heads, first, lanes, decays, params, marks_ref, seg_ref, places, others)
    strict = places > others
    queries, key_vecs, values = [], [], []
    for unit in units:
        marks = kept[unit.group][3]
        summed = conv_channels(padded, unit.group, taps, marks, unit.query_columns)
        act = summed * sigmoid(summed)
        scale = lax.rsqrt(jnp.sum(act * act, axis=1, keepdims=True) + EPS_UNIT)
        queries.append((act * (scale * DK**-0.5)).astype(bf))
        summed = conv_channels(padded, unit.group, taps, marks, unit.key_columns)
        act = summed * sigmoid(summed)
        scale = lax.rsqrt(jnp.sum(act * act, axis=1, keepdims=True) + EPS_UNIT)
        key_vecs.append((act * scale).astype(bf))
    pairs = [jnp.concatenate([q, k], axis=0) for q, k in zip(queries, key_vecs)]
    dots = [nt(pair, k) for pair, k in zip(pairs, key_vecs)]
    systems = [jnp.where(strict, unit.strength * unit.decay * d[CHUNK:], 0.0) for unit, d in zip(units, dots)]
    inverses = unit_lower_inverses(systems, places, others)
    for unit in units:
        summed = conv_channels(padded, unit.group, taps, kept[unit.group][3], unit.value_columns)
        values.append((summed * sigmoid(summed)).astype(bf).astype(f32))
    for group in range(GROUPS):
        padded[group, 0:8, :] = padded[group, CHUNK : CHUNK + 8, :]
    before = [state[number] for number in range(len(units))]
    for number in range(len(units)):
        kept_state[0, number] = before[number].astype(bf)
        kept_inverse[0, number] = inverses[number].astype(bf)
    reads = [nn(pair, s) for pair, s in zip(pairs, before)]
    rights = [unit.strength * (v - unit.opened * read[CHUNK:]) for unit, v, read in zip(units, values, reads)]
    news = [nn(t, r) for t, r in zip(inverses, rights)]
    mixed = [
        unit.opened * read[:CHUNK] + nn(d[:CHUNK] * unit.decay, new)
        for unit, read, d, new in zip(units, reads, dots, news)
    ]
    for number, unit in enumerate(units):
        state[number] = unit.opened_last * before[number] + tn(key_vecs[number], unit.closed * news[number])
    for unit, mix in zip(units, mixed):
        gate = proj[0, unit.group, 0, :, unit.gate_columns].astype(f32)
        scale = lax.rsqrt(jnp.mean(mix * mix, axis=1, keepdims=True) + EPS_HEAD)
        out[0, unit.group, 0, :, unit.out_columns] = (mix * scale * gain[...] * (gate * sigmoid(gate))).astype(bf)


def backward_kernel(
    heads, first, lanes, core_ref, proj, prev_rows, decays, grads, marks_ref, seg_ref, taps, params, gain,
    kept_state, kept_inverse, earlier, proj_grad, taps_grad, params_grad, gain_grad, state_grad, padded, summed_grad,
):
    conv_width = heads * (2 * DK + DV)
    width = conv_width + heads * DV

    @pl.when(pl.program_id(0) == 0)
    def _():
        taps_grad[...] = jnp.zeros_like(taps_grad)
        params_grad[...] = jnp.zeros_like(params_grad)
        gain_grad[...] = jnp.zeros_like(gain_grad)
        state_grad[...] = jnp.zeros_like(state_grad)
        summed_grad[:, CHUNK:, :] = jnp.zeros((GROUPS, 8, conv_width), f32)

    for group in range(GROUPS):
        padded[group, 0:8, :] = prev_rows[0, group, 0, :, :conv_width].astype(f32)[-8:]
        padded[group, 8:, :] = proj[0, group, 0, :, :conv_width].astype(f32)
    places = lax.broadcasted_iota(jnp.int32, (CHUNK, CHUNK), 0)
    others = lax.broadcasted_iota(jnp.int32, (CHUNK, CHUNK), 1)
    units, kept = chunk_units(heads, first, lanes, decays, params, marks_ref, seg_ref, places, others)
    strict = places > others
    q_sums, k_sums, v_sums, q_acts, k_acts, q_scale, k_scale = [], [], [], [], [], [], []
    queries, key_vecs, values = [], [], []
    for unit in units:
        marks = kept[unit.group][3]
        summed = conv_channels(padded, unit.group, taps, marks, unit.query_columns)
        act = summed * sigmoid(summed)
        scale = lax.rsqrt(jnp.sum(act * act, axis=1, keepdims=True) + EPS_UNIT)
        queries.append((act * (scale * DK**-0.5)).astype(bf))
        q_sums.append(summed)
        q_acts.append(act)
        q_scale.append(scale)
        summed = conv_channels(padded, unit.group, taps, marks, unit.key_columns)
        act = summed * sigmoid(summed)
        scale = lax.rsqrt(jnp.sum(act * act, axis=1, keepdims=True) + EPS_UNIT)
        key_vecs.append((act * scale).astype(bf))
        k_sums.append(summed)
        k_acts.append(act)
        k_scale.append(scale)
        summed = conv_channels(padded, unit.group, taps, marks, unit.value_columns)
        values.append((summed * sigmoid(summed)).astype(bf).astype(f32))
        v_sums.append(summed)
    count = len(units)
    pairs = [jnp.concatenate([q, k], axis=0) for q, k in zip(queries, key_vecs)]
    dots = [nt(pair, k) for pair, k in zip(pairs, key_vecs)]
    before = [kept_state[0, number] for number in range(count)]
    after_grad = [state_grad[number] for number in range(count)]
    inverses = [kept_inverse[0, number] for number in range(count)]
    reads = [nn(pair, s) for pair, s in zip(pairs, before)]
    gaps = [v - unit.opened * read[CHUNK:] for unit, v, read in zip(units, values, reads)]
    news = [nn(t, unit.strength * g) for t, unit, g in zip(inverses, units, gaps)]
    scores = [d[:CHUNK] * unit.decay for d, unit in zip(dots, units)]
    mixed = [unit.opened * read[:CHUNK] + nn(score, new) for unit, read, score, new in zip(units, reads, scores, news)]
    mix_grads = []
    gain_row = gain[...]
    gain_total = jnp.zeros((1, DV), f32)
    for unit, mix in zip(units, mixed):
        gate = proj[0, unit.group, 0, :, unit.gate_columns].astype(f32)
        grad = grads[0, unit.group, 0, :, unit.out_columns].astype(f32)
        scale = lax.rsqrt(jnp.mean(mix * mix, axis=1, keepdims=True) + EPS_HEAD)
        soft = sigmoid(gate)
        grad_normed = grad * (mix * scale)
        proj_grad[0, unit.group, 0, :, unit.gate_columns] = (
            grad_normed * gain_row * (soft * (1.0 + gate * (1.0 - soft)))
        ).astype(bf)
        silu = gate * soft
        gain_total = gain_total + jnp.sum(grad_normed * silu, axis=0, keepdims=True)
        inner = grad * silu * gain_row
        mix_grads.append(scale * inner - mix * (scale * scale * scale) * jnp.mean(inner * mix, axis=1, keepdims=True))
    gain_grad[0:1, :] += gain_total
    pushes = [nn(k, g) for k, g in zip(key_vecs, after_grad)]
    new_grads = [
        tn(score, grad) + unit.closed * push for score, grad, unit, push in zip(scores, mix_grads, units, pushes)
    ]
    score_grads = [nt(grad, new) for grad, new in zip(mix_grads, news)]
    right_grads = [tn(t, grad) for t, grad in zip(inverses, new_grads)]
    system_grads = [jnp.where(strict, -nt(grad, new), 0.0) for grad, new in zip(right_grads, news)]
    lane_ids = lax.broadcasted_iota(jnp.int32, (CHUNK, LANES), 1)
    rows_down = lax.broadcasted_iota(jnp.int32, (CHUNK, 1), 0)
    cum_grads = [jnp.zeros((CHUNK, LANES), f32) for _ in range(GROUPS)]
    beta_grads = [jnp.zeros((CHUNK, LANES), f32) for _ in range(GROUPS)]
    cross_rows = [[], []]
    raised = []
    for number, unit in enumerate(units):
        read_query = reads[number][:CHUNK]
        read_key = reads[number][CHUNK:]
        gram = dots[number][CHUNK:]
        decayed_score = score_grads[number] * unit.decay
        decayed_system = system_grads[number] * unit.decay
        system_gram = decayed_system * gram
        crossing = decayed_score * dots[number][:CHUNK] + unit.strength * system_gram
        value_grad = unit.strength * right_grads[number]
        beta_grad = jnp.sum(system_gram, axis=1, keepdims=True) + jnp.sum(
            right_grads[number] * gaps[number], axis=1, keepdims=True
        )
        open_grad = jnp.sum(mix_grads[number] * read_query - value_grad * read_key, axis=1, keepdims=True)
        close_grad = unit.closed * jnp.sum(news[number] * pushes[number], axis=1, keepdims=True)
        kept_dot = jnp.sum(
            jnp.sum(after_grad[number] * before[number].astype(f32), axis=1, keepdims=True), axis=0, keepdims=True
        )
        last_grad = jnp.sum(close_grad, axis=0, keepdims=True) + unit.opened_last * kept_dot
        col = jnp.sum(crossing, axis=1, keepdims=True) + unit.opened * open_grad - close_grad
        col = col + jnp.where(rows_down == CHUNK - 1, last_grad, 0.0)
        cross_rows[unit.group].append(jnp.sum(crossing, axis=0, keepdims=True))
        cum_grads[unit.group] = jnp.where(lane_ids == unit.lane, col, cum_grads[unit.group])
        beta_grads[unit.group] = jnp.where(lane_ids == unit.beta_lane, beta_grad, beta_grads[unit.group])
        raised.append((decayed_score.astype(bf), (unit.strength * decayed_system).astype(bf), value_grad))
    stacked = [
        jnp.concatenate([(unit.opened * grad).astype(bf), (-unit.opened * item[2]).astype(bf)], axis=0)
        for unit, item, grad in zip(units, raised, mix_grads)
    ]
    through = [nt(x, s) for x, s in zip(stacked, before)]
    grams = [jnp.concatenate([item[0], item[1]], axis=0) for item in raised]
    direct = [nn(g, k) for g, k in zip(grams, key_vecs)]
    turned = [tn(g, pair) for g, pair in zip(grams, pairs)]
    pushed = [nt(unit.closed * new, grad) for unit, new, grad in zip(units, news, after_grad)]
    for number, unit in enumerate(units):
        state_grad[number] = unit.opened_last * after_grad[number] + tn(pairs[number], stacked[number])
    for number, unit in enumerate(units):
        query_grad = (through[number][:CHUNK] + direct[number][:CHUNK]) * DK**-0.5
        key_grad = through[number][CHUNK:] + direct[number][CHUNK:] + turned[number] + pushed[number]
        for grad, act, scale, summed, columns in (
            (query_grad, q_acts[number], q_scale[number], q_sums[number], unit.query_columns),
            (key_grad, k_acts[number], k_scale[number], k_sums[number], unit.key_columns),
        ):
            inner = scale * (grad - act * (scale * scale) * jnp.sum(grad * act, axis=1, keepdims=True))
            soft = sigmoid(summed)
            summed_grad[unit.group, 0:CHUNK, columns] = inner * (soft * (1.0 + summed * (1.0 - soft)))
        summed = v_sums[number]
        soft = sigmoid(summed)
        summed_grad[unit.group, 0:CHUNK, unit.value_columns] = raised[number][2] * (
            soft * (1.0 + summed * (1.0 - soft))
        )
    for group in range(GROUPS):
        marks = kept[group][3]
        for start in range(0, conv_width, LANES):
            columns = slice(start, start + LANES)
            grad = summed_grad[group, 0:CHUNK, columns]
            total = taps[0:1, columns] * grad
            taps_grad[0:1, columns] += jnp.sum(grad * padded[group, 8 : 8 + CHUNK, columns], axis=0, keepdims=True)
            for offset in range(1, 4):
                later = summed_grad[group, offset : offset + CHUNK, columns]
                total = total + (taps[offset : offset + 1, columns] * marks[:, 5 + offset : 6 + offset]) * later
                taps_grad[offset : offset + 1, columns] += jnp.sum(
                    (grad * marks[:, offset : offset + 1]) * padded[group, 8 - offset : 8 - offset + CHUNK, columns],
                    axis=0, keepdims=True,
                )
            proj_grad[0, group, 0, :, columns] = total.astype(bf)
        summed_grad[group, CHUNK:, :] = summed_grad[group, 0:8, :]
    upper = (places <= others).astype(f32)
    for group in range(GROUPS):
        biased, log_decay, beta, _ = kept[group]
        blank = [jnp.zeros((first, CHUNK), f32)] if first else []
        rest = [jnp.zeros((CHUNK - heads - first, CHUNK), f32)]
        cross = jnp.concatenate(blank + cross_rows[group] + rest, axis=0).T
        log_grad = exact(upper, cum_grads[group] - cross)
        decay_grad = log_grad * (-params[1:2, :]) * sigmoid(biased)
        both = decay_grad + beta_grads[group] * beta * (1.0 - beta)
        if earlier is not None:
            both = both + earlier[0, group, 0].astype(f32)
        proj_grad[0, group, 0, :, width:] = both.astype(bf)
        params_grad[0:1, :] += jnp.sum(log_grad * log_decay, axis=0, keepdims=True)
        params_grad[1:2, :] += jnp.sum(decay_grad, axis=0, keepdims=True)


def folded(rows):
    return rows.reshape(2, GROUPS, -1, CHUNK, rows.shape[1])


def mixer_forward(first, lanes, core, proj, decays, marks, seg_rows, taps, params, gain, partner):
    conv_width = taps.shape[1]
    heads = conv_width // (2 * DK + DV)
    proj, decays = folded(proj), folded(decays)
    per_core = proj.shape[2]
    chunks = 2 * per_core
    units = GROUPS * heads

    def at(c, core_ref):
        return ((c // per_core) ^ core_ref[0], 0, c % per_core, 0, 0)

    fixed = lambda c, core_ref: (0, 0)
    here = lambda c, core_ref: (0, c, 0, 0)
    kept = lambda c, core_ref: (c, 0, 0, 0)
    full = proj.shape[:4] + (lanes * DV,)
    body = functools.partial(forward_kernel, heads, first, lanes)
    more_specs, more, aliases = [], [], {}
    if partner is None:
        inner = body

        def body(*refs):
            return inner(*refs[:8], None, *refs[8:])

    else:
        more_specs, more, aliases = [pl.BlockSpec(memory_space=pl.ANY)], [partner.reshape(full)], {8: 0}

    def out_at(c, core_ref):
        return at(c, core_ref)[:4] + (first // heads,)

    out, states, inverses = pl.pallas_call(
        body,
        grid_spec=pltpu.PrefetchScalarGridSpec(
            num_scalar_prefetch=1,
            grid=(chunks,),
            in_specs=[
                pl.BlockSpec((1, GROUPS, 1, CHUNK, proj.shape[4]), at),
                pl.BlockSpec((1, GROUPS, 1, CHUNK, LANES), at),
                pl.BlockSpec((GROUPS, 1, CHUNK, LANES), here),
                pl.BlockSpec((GROUPS, 1, 1, CHUNK), here),
                pl.BlockSpec((4, conv_width), fixed),
                pl.BlockSpec((8, LANES), fixed),
                pl.BlockSpec((1, DV), fixed),
            ]
            + more_specs,
            out_specs=[
                pl.BlockSpec((1, GROUPS, 1, CHUNK, heads * DV), out_at),
                pl.BlockSpec((1, units, DK, DV), kept),
                pl.BlockSpec((1, units, CHUNK, CHUNK), kept),
            ],
            scratch_shapes=[pltpu.VMEM((units, DK, DV), f32), pltpu.VMEM((GROUPS, CHUNK + 8, conv_width), f32)],
        ),
        out_shape=[
            jax.ShapeDtypeStruct(full, bf),
            jax.ShapeDtypeStruct((chunks, units, DK, DV), bf),
            jax.ShapeDtypeStruct((chunks, units, CHUNK, CHUNK), bf),
        ],
        compiler_params=pltpu.CompilerParams(vmem_limit_bytes=VMEM_LIMIT),
        cost_estimate=pl.CostEstimate(flops=16 * 10**9, bytes_accessed=16 * 2**20, transcendentals=0),
        input_output_aliases=aliases,
        name="mixer_forward",
    )(core, proj, decays, marks, seg_rows, taps, params, gain, *more)
    return out.reshape(-1, lanes * DV), states, inverses


def mixer_backward(first, lanes, core, proj, decays, grads, marks, seg_rows, taps, params, gain, states, inverses, earlier):
    conv_width = taps.shape[1]
    heads = conv_width // (2 * DK + DV)
    proj, decays, grads = folded(proj), folded(decays), folded(grads)
    per_core = proj.shape[2]
    chunks = 2 * per_core
    units = GROUPS * heads
    width = conv_width + heads * DV + LANES
    tail = 16

    def at(step, core_ref):
        c = chunks - 1 - step
        return ((c // per_core) ^ core_ref[0], 0, c % per_core, 0, 0)

    def prev(step, core_ref):
        c = jnp.maximum(chunks - 2 - step, 0)
        return ((c // per_core) ^ core_ref[0], 0, c % per_core, CHUNK // tail - 1, 0)

    def grad_at(step, core_ref):
        return at(step, core_ref)[:4] + (first // heads,)

    def last_lanes(step, core_ref):
        return at(step, core_ref)[:4] + ((conv_width + heads * DV) // LANES,)

    fixed = lambda step, core_ref: (0, 0)
    here = lambda step, core_ref: (0, chunks - 1 - step, 0, 0)
    kept = lambda step, core_ref: (chunks - 1 - step, 0, 0, 0)
    in_specs = [
        pl.BlockSpec((1, GROUPS, 1, CHUNK, proj.shape[4]), at),
        pl.BlockSpec((1, GROUPS, 1, tail, proj.shape[4]), prev),
        pl.BlockSpec((1, GROUPS, 1, CHUNK, LANES), at),
        pl.BlockSpec((1, GROUPS, 1, CHUNK, heads * DV), grad_at),
        pl.BlockSpec((GROUPS, 1, CHUNK, LANES), here),
        pl.BlockSpec((GROUPS, 1, 1, CHUNK), here),
        pl.BlockSpec((4, conv_width), fixed),
        pl.BlockSpec((8, LANES), fixed),
        pl.BlockSpec((1, DV), fixed),
        pl.BlockSpec((1, units, DK, DV), kept),
        pl.BlockSpec((1, units, CHUNK, CHUNK), kept),
    ]
    inputs = [core, proj, proj, decays, grads, marks, seg_rows, taps, params, gain, states, inverses]
    body = functools.partial(backward_kernel, heads, first, lanes)
    if earlier is not None:
        in_specs.append(pl.BlockSpec((1, GROUPS, 1, CHUNK, LANES), last_lanes))
        inputs.append(folded(earlier))
    else:
        whole = body

        def body(*refs):
            return whole(*refs[:12], None, *refs[12:])

    out, taps_grad, params_grad, gain_grad = pl.pallas_call(
        body,
        grid_spec=pltpu.PrefetchScalarGridSpec(
            num_scalar_prefetch=1,
            grid=(chunks,),
            in_specs=in_specs,
            out_specs=[
                pl.BlockSpec((1, GROUPS, 1, CHUNK, width), at),
                pl.BlockSpec((4, conv_width), fixed),
                pl.BlockSpec((8, LANES), fixed),
                pl.BlockSpec((8, DV), fixed),
            ],
            scratch_shapes=[
                pltpu.VMEM((units, DK, DV), f32),
                pltpu.VMEM((GROUPS, CHUNK + 8, conv_width), f32),
                pltpu.VMEM((GROUPS, CHUNK + 8, conv_width), f32),
            ],
        ),
        out_shape=[
            jax.ShapeDtypeStruct(proj.shape[:4] + (width,), bf),
            jax.ShapeDtypeStruct((4, conv_width), f32),
            jax.ShapeDtypeStruct((8, LANES), f32),
            jax.ShapeDtypeStruct((8, DV), f32),
        ],
        compiler_params=pltpu.CompilerParams(vmem_limit_bytes=VMEM_LIMIT),
        cost_estimate=pl.CostEstimate(flops=30 * 10**9, bytes_accessed=30 * 2**20, transcendentals=0),
        name="mixer_backward",
    )(*inputs)
    return out.reshape(-1, width), taps_grad, params_grad, gain_grad


def group_marks(lengths, group_rows):
    groups, count = lengths.shape
    position = jnp.arange(group_rows, dtype=jnp.int32)[None, :]
    segment = jnp.zeros((groups, group_rows), jnp.int32)
    end = jnp.zeros((groups, 1), jnp.int32)
    for number in range(count):
        segment = segment + (position >= end).astype(jnp.int32)
        end = end + lengths[:, number : number + 1]
    live = (position < end).astype(f32)
    padded = jnp.pad(segment, ((0, 0), (CHUNK, CHUNK)))
    later = lambda offset: padded[:, CHUNK + offset : CHUNK + offset + group_rows]
    chunked = segment.reshape(groups, group_rows // CHUNK, CHUNK)
    before = padded[:, CHUNK - 1 : CHUNK - 1 + group_rows].reshape(chunked.shape)[:, :, :1]
    columns = [segment]
    columns += [later(-offset) == segment for offset in (1, 2, 3)]
    columns += [(chunked == before).reshape(segment.shape), (chunked == chunked[:, :, -1:]).reshape(segment.shape)]
    columns += [later(offset) == segment for offset in (1, 2, 3)]
    lane = jnp.arange(LANES, dtype=jnp.int32)
    marks = jnp.zeros((groups, group_rows, LANES), f32)
    for number, column in enumerate(columns):
        marks = jnp.where(lane == number, column.astype(f32)[:, :, None], marks)
    marks = marks.reshape(groups, group_rows // CHUNK, CHUNK, LANES)
    seg_rows = segment.astype(f32).reshape(groups, group_rows // CHUNK, 1, CHUNK)
    return marks, seg_rows, live


def pick_kernel(pairs, turn_ref, *refs):
    count = len(refs) - len(pairs)
    for out, parts in zip(refs[count:], pairs):
        begin = 0
        for number, start, stop in parts:
            out[:, begin : begin + stop - start] = refs[number][:, start:stop]
            begin += stop - start


def picked(turn, weights, axes, joins):
    in_specs, inputs, shapes = [], [], []
    for weight, axis in zip(weights, axes):
        rows, columns = weight.shape
        if axis is None:
            in_specs += [pl.BlockSpec((rows, columns), lambda i, t: (0, 0))] * 2
            shapes.append((rows, columns))
        elif axis == 1:
            in_specs += [
                pl.BlockSpec((rows, columns // 2), lambda i, t: (0, t[0])),
                pl.BlockSpec((rows, columns // 2), lambda i, t: (0, 1 - t[0])),
            ]
            shapes.append((rows, columns // 2))
        else:
            in_specs += [
                pl.BlockSpec((rows // 2, columns), lambda i, t: (t[0], 0)),
                pl.BlockSpec((rows // 2, columns), lambda i, t: (1 - t[0], 0)),
            ]
            shapes.append((rows // 2, columns))
        inputs += [weight, weight]
    pairs, out_shapes = [], []
    for join in joins:
        width = sum(stop - start for _, start, stop in join)
        for given in (0, 1):
            pairs.append([(2 * number + given, start, stop) for number, start, stop in join])
            out_shapes.append((shapes[join[0][0]][0], width))
    outs = pl.pallas_call(
        functools.partial(pick_kernel, pairs),
        grid_spec=pltpu.PrefetchScalarGridSpec(
            num_scalar_prefetch=1,
            grid=(1,),
            in_specs=in_specs,
            out_specs=[pl.BlockSpec(shape, lambda i, t: (0, 0)) for shape in out_shapes],
        ),
        out_shape=[jax.ShapeDtypeStruct(shape, bf) for shape in out_shapes],
        compiler_params=pltpu.CompilerParams(vmem_limit_bytes=VMEM_LIMIT),
        cost_estimate=pl.CostEstimate(flops=0, bytes_accessed=8 * 2**20, transcendentals=0),
        name="picked",
    )(turn, *inputs)
    return [(outs[2 * number], outs[2 * number + 1]) for number in range(len(joins))]


TILE = 256
STRIP = 256


def call(body, grid, in_specs, out_specs, out_shape, flops, moved, name, inputs):
    return pl.pallas_call(
        body,
        grid=grid,
        in_specs=in_specs,
        out_specs=out_specs,
        out_shape=out_shape,
        compiler_params=pltpu.CompilerParams(vmem_limit_bytes=VMEM_LIMIT),
        cost_estimate=pl.CostEstimate(flops=flops, bytes_accessed=moved, transcendentals=0),
        name=name,
    )(*inputs)


def strip_sum(rows, pieces, start, product):
    total = None
    begin = 0
    depth = rows.shape[1] // len(pieces)
    for piece in pieces:
        part = product(rows[start : start + STRIP, begin : begin + depth], piece[...])
        total = part if total is None else total + part
        begin += depth
    return total


def whole(array):
    return pl.BlockSpec(array.shape, lambda i: (0,) * array.ndim)


def project(rows, pieces, width, extra):
    count = rows.shape[0]
    depth = pieces[0].shape[0]
    steps = width // TILE
    used = len(pieces)

    def body(rows_ref, *refs):
        weights = refs[:used]
        out = refs[2 * used if extra else used]
        for start in range(0, count, STRIP):
            out[start : start + STRIP, :] = strip_sum(rows_ref, weights, start, nn).astype(bf)
        if extra:

            @pl.when(pl.program_id(0) == 0)
            def _():
                for start in range(0, count, STRIP):
                    refs[-1][start : start + STRIP, :] = strip_sum(rows_ref, refs[used : 2 * used], start, nn)

    in_specs = [whole(rows)] + [pl.BlockSpec((depth, TILE), lambda i: (0, i))] * used
    out_specs = [pl.BlockSpec((count, TILE), lambda i: (0, i))]
    out_shape = [jax.ShapeDtypeStruct((count, width), bf)]
    inputs = [rows, *pieces]
    if extra:
        in_specs += [pl.BlockSpec((depth, LANES), lambda i: (0, width // LANES))] * used
        out_specs.append(pl.BlockSpec((count, LANES), lambda i: (0, 0)))
        out_shape.append(jax.ShapeDtypeStruct((count, LANES), f32))
        inputs += pieces
    flops = 2 * count * depth * used * width
    moved = 2 * (count * depth * used + depth * used * width + count * width)
    return call(body, (steps,), in_specs, out_specs, out_shape, flops, moved, "project", inputs)


def feed_forward(rows, gate_pieces, up_pieces):
    count = rows.shape[0]
    depth, width = gate_pieces[0].shape
    used = len(gate_pieces)

    def body(rows_ref, *refs):
        gate_out, up_out, hidden_out = refs[2 * used :]
        for start in range(0, count, STRIP):
            strip = slice(start, start + STRIP)
            gate = strip_sum(rows_ref, refs[:used], start, nn)
            up = strip_sum(rows_ref, refs[used : 2 * used], start, nn)
            gate_out[strip, :] = gate.astype(bf)
            up_out[strip, :] = up.astype(bf)
            hidden_out[strip, :] = (gate * sigmoid(gate) * up).astype(bf)

    out_spec = pl.BlockSpec((count, TILE), lambda i: (0, i))
    return call(
        body,
        (pl.cdiv(width, TILE),),
        [whole(rows)] + [pl.BlockSpec((depth, TILE), lambda i: (0, i))] * (2 * used),
        [out_spec] * 3,
        [jax.ShapeDtypeStruct((count, width), bf)] * 3,
        4 * count * depth * used * width,
        2 * (count * depth * used + 2 * depth * used * width + 3 * count * width),
        "feed_forward",
        [rows, *gate_pieces, *up_pieces],
    )


def feed_backward(rows, down_pieces, gate_pre, up_proj):
    count = rows.shape[0]
    width, depth = down_pieces[0].shape
    used = len(down_pieces)

    def body(rows_ref, *refs):
        gate_ref, up_ref, gate_out, up_out = refs[used:]
        for start in range(0, count, STRIP):
            strip = slice(start, start + STRIP)
            grad = strip_sum(rows_ref, refs[:used], start, nt)
            gate = gate_ref[strip, :].astype(f32)
            soft = sigmoid(gate)
            gate_out[strip, :] = (grad * up_ref[strip, :].astype(f32) * soft * (1.0 + gate * (1.0 - soft))).astype(bf)
            up_out[strip, :] = (grad * gate * soft).astype(bf)

    tile = pl.BlockSpec((count, TILE), lambda i: (0, i))
    return call(
        body,
        (pl.cdiv(width, TILE),),
        [whole(rows)] + [pl.BlockSpec((TILE, depth), lambda i: (i, 0))] * used + [tile] * 2,
        [tile] * 2,
        [jax.ShapeDtypeStruct((count, width), bf)] * 2,
        2 * count * depth * used * width,
        2 * (count * depth * used + depth * used * width + 4 * count * width),
        "feed_backward",
        [rows, *down_pieces, gate_pre, up_proj],
    )


def heads_backward(rows, out_pieces):
    count = rows.shape[0]
    width, depth = out_pieces[0].shape
    used = len(out_pieces)

    def body(rows_ref, *refs):
        for start in range(0, count, STRIP):
            refs[used][start : start + STRIP, :] = strip_sum(rows_ref, refs[:used], start, nt).astype(bf)

    return call(
        body,
        (width // TILE,),
        [whole(rows)] + [pl.BlockSpec((TILE, depth), lambda i: (i, 0))] * used,
        pl.BlockSpec((count, TILE), lambda i: (0, i)),
        jax.ShapeDtypeStruct((count, width), bf),
        2 * count * depth * used * width,
        2 * (count * depth * used + depth * used * width + count * width),
        "heads_backward",
        [rows, *out_pieces],
    )


def widen(terms, refs, product):
    outs = []
    for piece in range(4):
        total = None
        for number, begin, weight, first, columns in terms:
            left = refs[number][:, begin : begin + columns]
            right = refs[weight + piece]
            right = right[:, first : first + columns] if product is nt else right[...]
            part = product(left, right)
            total = part if total is None else total + part
        outs.append(total)
    return outs


def wide(terms, lefts, pieces, product, features, got):
    count = lefts[0].shape[0]
    per = count // 4
    given = got is None
    here = (lambda i: (i + 2, 0)) if given else (lambda i: (1 - i, 0))
    inputs = list(lefts) + [piece for group in pieces for piece in group]
    in_specs = [pl.BlockSpec((per, left.shape[1]), here) for left in lefts]
    in_specs += [whole(piece) for group in pieces for piece in group]
    flops = 2 * (count // 2) * features * sum(term[4] for term in terms)
    moved = 2 * sum(piece.size for group in pieces for piece in group) + 6 * count * features
    depth = features // 4
    if given:

        def body(*refs):
            for piece, total in enumerate(widen(terms, refs, product)):
                refs[-1][:, piece * depth : piece * depth + depth] = total.astype(bf)

        return call(
            body, (2,), in_specs, pl.BlockSpec((per, features), lambda i: (i, 0)),
            jax.ShapeDtypeStruct((count // 2, features), bf), flops, moved, "wide_given", inputs,
        )

    def body(*refs):
        got_ref, there, own = refs[-3:]
        totals = widen(terms, refs, product)
        for piece, total in enumerate(totals):
            columns = slice(piece * depth, piece * depth + depth)
            total = total + got_ref[:, columns].astype(f32)

            @pl.when(pl.program_id(0) == 0)
            def _():
                there[:, columns] = total.astype(bf)

            @pl.when(pl.program_id(0) == 1)
            def _():
                own[:, columns] = total

    return call(
        body, (2,), in_specs + [pl.BlockSpec((per, features), here)],
        [pl.BlockSpec((per, features), lambda i: (0, 0))] * 2,
        [jax.ShapeDtypeStruct((per, features), bf), jax.ShapeDtypeStruct((per, features), f32)],
        flops, moved, "wide_kept", inputs + [got],
    )


RING = (0, 1, 3, 2)


def matmul(left, right):
    return jnp.dot(left, right, preferred_element_type=f32)


def outer_sum(left, right):
    return lax.dot_general(left, right, (((0,), (0,)), ((), ())), preferred_element_type=f32)


def times_back(left, right):
    return lax.dot_general(left, right, (((1,), (1,)), ((), ())), preferred_element_type=f32)


def norm_back(inputs, scale, gain, grad_out):
    scaled = grad_out * gain
    grad_in = scale * scaled - inputs * scale**3 * jnp.mean(scaled * inputs, axis=1, keepdims=True)
    return (grad_in, jnp.sum(grad_out * inputs * scale, axis=0))


class Layout:
    def __init__(self):
        self.ways = lax.axis_size("dp")
        self.spans = self.ways // 8
        dp = lax.axis_index("dp")
        self.core = lax.axis_index("tensor")
        self.turn = (dp // 4) % 2
        self.far = dp // 8
        near = dp % 4
        self.spot = near ^ (near >> 1)
        self.queues = {}

    def queued(self, values, queue, depth):
        line = self.queues.setdefault(queue, [])
        if len(line) >= depth:
            values, _ = lax.optimization_barrier((values, line[-depth]))
        return values, line

    def ring(self, values, step):
        pairs = []
        for number in range(self.ways):
            near = number % 4
            pairs.append((number, number - near + RING[((near ^ (near >> 1)) + step) % 4]))
        values, line = self.queued(values, step, DEPTH)
        line.append(lax.ppermute(values, "dp", pairs))
        return line[-1]

    def flip(self, values, bit):
        return lax.ppermute(values, "dp", [(n, n ^ bit) for n in range(self.ways)])

    def turned(self, values):
        return self.flip(values, 4)

    def crossed(self, values):
        return lax.ppermute(values, "tensor", [(0, 1), (1, 0)])

    def far_bits(self):
        bit = 8
        while bit < self.ways:
            yield bit
            bit *= 2

    def sources(self):
        places = jnp.arange(self.ways, dtype=jnp.int32)
        step = places // (2 * self.spans)
        jump = (places // 2) % self.spans
        spot = (self.spot + step) % 4
        return ((self.far ^ jump) * 2 + places % 2) * 4 + (spot ^ (spot >> 1))

    def ordered(self, first, second, axis):
        return jnp.where(
            self.turn == 0, jnp.concatenate([first, second], axis=axis), jnp.concatenate([second, first], axis=axis)
        )

    def spread(self, blob, axis, upward):
        keep, give = blob
        give, line = self.queued(give, "turn", DEPTH)
        line.append(self.turned(give))
        chunk = self.ordered(keep, line[-1], axis)
        for bit in self.far_bits():
            sent, line = self.queued(chunk, "far", DEPTH)
            line.append(self.flip(sent, bit))
            chunk = jnp.concatenate([chunk, line[-1]], axis=axis)
        ahead = self.ring(chunk, -1)
        behind = self.ring(chunk, 1)
        across = self.ring(behind, 1) if upward else self.ring(ahead, -1)
        return [chunk, ahead, across, behind]

    def collect_ring(self, make, upward):
        if upward:
            up = self.ring(make(2).astype(bf), 1)
            down = self.ring(make(3).astype(bf), -1)
            up = self.ring((make(1) + up).astype(bf), 1)
        else:
            down = self.ring(make(2).astype(bf), -1)
            up = self.ring(make(1).astype(bf), 1)
            down = self.ring((make(3) + down).astype(bf), -1)
        return make(0) + up + down

    def collect_rest(self, own, axis):
        for bit in reversed(list(self.far_bits())):
            half = own.shape[axis] // 2
            sent = lax.slice_in_dim(own, half, 2 * half, axis=axis)
            own = lax.slice_in_dim(own, 0, half, axis=axis) + self.flip(sent.astype(bf), bit)
        half = own.shape[axis] // 2
        mine = lax.dynamic_slice_in_dim(own, self.turn * half, half, axis)
        other = lax.dynamic_slice_in_dim(own, (1 - self.turn) * half, half, axis)
        return mine, self.turned(other.astype(bf)).astype(f32)

    def joined(self, mine, theirs, axis):
        return self.ordered(jnp.concatenate(mine, axis=axis), jnp.concatenate(theirs, axis=axis), axis)

    def rows_of(self, own):
        across = self.crossed(own)
        there = self.turned(own)
        return jnp.concatenate([own, there, across, self.crossed(there)], axis=0)

    def own_of(self, terms, lefts, pieces, product, features):
        given = wide(terms, lefts, pieces, product, features, None)
        there, own = wide(terms, lefts, pieces, product, features, self.crossed(given))
        return own + self.turned(there)

    def everywhere(self, values):
        bit = 1
        while bit < self.ways:
            values = values + self.flip(values, bit)
            bit *= 2
        return values + self.crossed(values)


DEPTH = 1


def flat(parts):
    joined = jnp.concatenate([part.reshape(-1) for part in parts])
    return jnp.pad(joined, (0, -joined.shape[0] % (8 * LANES))).reshape(-1, LANES)


def shards(
    tokens, cotangent, lengths, slot_of, norm_gains, w_query, w_key, w_value, w_gate, w_decay, w_beta,
    conv_weights, a_log, dt_bias, out_gain, w_out, w_mlp_gate, w_mlp_up, w_mlp_down,
):
    lay = Layout()
    row_count, features = tokens.shape
    tensor_ways = lax.axis_size("tensor")
    device_count = lay.ways * tensor_ways
    group_rows = row_count * tensor_ways
    capacity = row_count // device_count + 2
    bulk_rows = device_count * capacity
    all_heads = a_log.shape[0]
    heads = all_heads // (2 * tensor_ways)
    pair = heads // 2
    all_keys = all_heads * DK
    keys, vals = pair * DK, pair * DV
    width = 2 * keys + 2 * vals
    share = lay.core * 2 + lay.turn
    turn = lay.turn.reshape(1)
    core = lay.core.reshape(1)

    target = slot_of // row_count
    within = slot_of % row_count
    hits = target[:, None] == jnp.arange(device_count, dtype=jnp.int32)[None, :]
    places = jnp.arange(row_count, dtype=jnp.int32)
    earlier = (places[:, None] >= places[None, :]).astype(bf)
    rank = jnp.sum(matmul(earlier, hits.astype(bf)) * hits.astype(f32), axis=1).astype(jnp.int32) - 1
    outgoing = target * capacity + rank
    sending = (jnp.arange(bulk_rows, dtype=jnp.int32)[:, None] == outgoing[None, :]).astype(bf)
    slot_mark = jnp.broadcast_to((within + 1).astype(bf)[:, None], (row_count, LANES))
    send_tokens = matmul(sending, jnp.concatenate([tokens, slot_mark], axis=1)).astype(bf)
    send_cot = matmul(sending, cotangent).astype(bf)

    def exchange(values):
        return lax.all_to_all(values, ("dp", "tensor"), split_axis=0, concat_axis=0, tiled=True)


    def half_heads(weight):
        kept = jnp.where(lay.turn == 0, weight[:, :heads], weight[:, heads:])
        given = jnp.where(lay.turn == 0, weight[:, heads:], weight[:, :heads])
        return kept, given

    decay_halves, beta_halves = half_heads(w_decay), half_heads(w_beta)
    lanes_of = [
        jnp.pad(jnp.concatenate([d, b], axis=1), ((0, 0), (0, LANES - 2 * heads)))
        for d, b in zip(decay_halves, beta_halves)
    ]
    first_join = [(0, 0, keys), (1, 0, keys), (2, 0, vals), (3, 0, vals)]
    second_join = [(0, keys, 2 * keys), (1, keys, 2 * keys), (2, vals, 2 * vals), (3, vals, 2 * vals)]
    blob_first, blob_second = picked(
        turn, [w_query, w_key, w_value, w_gate], [1] * 4, [first_join, second_join]
    )
    blob_first = tuple(jnp.concatenate([blob, extra], axis=1) for blob, extra in zip(blob_first, lanes_of))
    out_rows, hidden_here = w_out.shape[0] // 2, w_mlp_gate.shape[1] // 2
    block = features // lay.ways
    blob_out, blob_gate, blob_up, blob_down = picked(
        turn, [w_out, w_mlp_gate, w_mlp_up, w_mlp_down], [0, 1, 1, 0],
        [[(0, 0, block)], [(1, 0, hidden_here)], [(2, 0, hidden_here)], [(3, 0, block)]],
    )
    got_tokens = exchange(send_tokens)
    in_first = lay.spread(blob_first, 0, True)
    in_second = lay.spread(blob_second, 0, False)
    out_pieces = lay.spread(blob_out, 1, True)
    gate_pieces = lay.spread(blob_gate, 0, False)
    up_pieces = lay.spread(blob_up, 0, True)
    down_pieces = lay.spread(blob_down, 1, False)

    got_slot = got_tokens[:, features].astype(jnp.int32)
    landing = (places[:, None] + 1 == got_slot[None, :]).astype(bf)
    sources = lay.sources()
    feature = jnp.arange(features, dtype=jnp.int32)
    origin = (sources[:, None] * block + jnp.arange(block, dtype=jnp.int32)[None, :]).reshape(1, -1)
    turning = (feature[:, None] == origin).astype(bf)
    numbers = jnp.arange(lay.ways, dtype=jnp.int32)
    picking = (sources[:, None] == numbers[None, :]).astype(f32)

    def reordered_gain(gain):
        return jnp.sum(picking[:, :, None] * gain.reshape(1, lay.ways, block), axis=1).reshape(features)

    def straight_gain(grad):
        return jnp.sum(picking[:, :, None] * grad.reshape(lay.ways, 1, block), axis=0).reshape(features)

    gains = (reordered_gain(norm_gains[0]), reordered_gain(norm_gains[1]))
    x_own = matmul(matmul(landing, got_tokens[:, :features]).astype(bf), turning)

    pair_lengths = jnp.concatenate([lengths, lay.turned(lengths)], axis=0)
    marks, seg_rows, live = group_marks(pair_lengths, group_rows)
    live_own = lax.dynamic_slice_in_dim(live[0], lay.core * row_count, row_count)[:, None]
    starts = [(share * heads + first) * DK for first in (0, pair)]
    cuts = [
        [(start, keys), (all_keys + start, keys), (2 * all_keys + 2 * start, vals)] for start in starts
    ]
    taps = [
        jnp.concatenate([lax.dynamic_slice_in_dim(conv_weights, start, size, 1) for start, size in cut], axis=1)
        for cut in cuts
    ]
    log_here = lax.dynamic_slice_in_dim(a_log, share * heads, heads)
    bias_here = lax.dynamic_slice_in_dim(dt_bias, share * heads, heads)
    params = jnp.pad(jnp.stack([bias_here, jnp.exp(log_here)]), ((0, 6), (0, LANES - heads)))
    gain_row = out_gain[None, :]

    scale_one = lax.rsqrt(jnp.mean(x_own * x_own, axis=1, keepdims=True) + EPS_ROW)
    first_rows = lay.rows_of((x_own * scale_one * gains[0]).astype(bf))
    proj_first, decays = project(first_rows, in_first, width, True)
    heads_out, states_first, inverses_first = mixer_forward(
        0, heads, core, proj_first, decays, marks, seg_rows, taps[0], params, gain_row, None
    )
    proj_second = project(first_rows, in_second, width, False)[0]
    heads_out, states_second, inverses_second = mixer_forward(
        pair, heads, core, proj_second, decays, marks, seg_rows, taps[1], params, gain_row, heads_out
    )
    mixed_own = lay.own_of([(0, 0, 1, 0, out_rows)], [heads_out], [out_pieces], nn, features)
    middle = x_own + live_own * mixed_own

    got_cot = exchange(send_cot)
    dy_own = matmul(matmul(landing, got_cot).astype(bf), turning)
    branch_rows = lay.rows_of((live_own * dy_own).astype(bf))
    scale_two = lax.rsqrt(jnp.mean(middle * middle, axis=1, keepdims=True) + EPS_ROW)
    second_rows = lay.rows_of((middle * scale_two * gains[1]).astype(bf))
    gate_pre, up_proj, hidden = feed_forward(second_rows, gate_pieces, up_pieces)
    depth = features // 4

    def columns_of(rows, piece):
        return rows[:, piece * depth : piece * depth + depth]

    down_own = lay.collect_ring(lambda r: outer_sum(hidden, columns_of(branch_rows, r)), True)
    grad_gate, grad_up = feed_backward(branch_rows, down_pieces, gate_pre, up_proj)
    gate_own = lay.collect_ring(lambda r: outer_sum(columns_of(second_rows, r), grad_gate), False)
    up_own = lay.collect_ring(lambda r: outer_sum(columns_of(second_rows, r), grad_up), True)
    grad_second = lay.own_of(
        [(0, 0, 2, 0, hidden_here), (1, 0, 6, 0, hidden_here)],
        [grad_gate, grad_up], [gate_pieces, up_pieces], nt, features,
    )
    grad_mid_norm, gain_two_grad = norm_back(middle, scale_two, gains[1], grad_second)
    grad_middle = dy_own + grad_mid_norm
    mix_rows = lay.rows_of((live_own * grad_middle).astype(bf))

    grad_heads = heads_backward(mix_rows, out_pieces)
    out_own = lay.collect_ring(lambda r: outer_sum(heads_out, columns_of(mix_rows, r)), False)
    grad_proj_first, taps_first, params_first, gain_first = mixer_backward(
        0, heads, core, proj_first, decays, grad_heads, marks, seg_rows, taps[0], params, gain_row,
        states_first, inverses_first, None,
    )
    first_own = lay.collect_ring(
        lambda r: outer_sum(columns_of(first_rows, r), grad_proj_first[:, :width]), True
    )
    grad_proj_second, taps_second, params_second, gain_second = mixer_backward(
        pair, heads, core, proj_second, decays, grad_heads, marks, seg_rows, taps[1], params, gain_row,
        states_second, inverses_second, grad_proj_first,
    )
    second_own = lay.collect_ring(lambda r: outer_sum(columns_of(first_rows, r), grad_proj_second), False)
    grad_first = lay.own_of(
        [(0, 0, 2, 0, width), (1, 0, 6, 0, width), (1, width, 2, width, LANES)],
        [grad_proj_first, grad_proj_second], [in_first, in_second], nt, features,
    )
    grad_x_norm, gain_one_grad = norm_back(x_own, scale_one, gains[0], grad_first)
    grad_tokens = (grad_middle + grad_x_norm).astype(bf)

    def sent_back(own):
        straight = times_back(own, turning).astype(bf)
        back = exchange(outer_sum(landing, straight).astype(bf))
        return outer_sum(sending, back).astype(bf)

    branch_own = lay.own_of([(0, 0, 1, 0, hidden_here)], [hidden], [down_pieces], nn, features)
    output = sent_back((middle + live_own * branch_own).astype(bf))
    tokens_grad = sent_back(grad_tokens)

    conv_full = jnp.zeros(conv_weights.shape, f32)
    for cut, grad in zip(cuts, (taps_first, taps_second)):
        begin = 0
        for start, size in cut:
            conv_full = lax.dynamic_update_slice_in_dim(conv_full, grad[:, begin : begin + size], start, 1)
            begin += size
    params_grad = params_first + params_second
    log_full = lax.dynamic_update_slice_in_dim(jnp.zeros_like(a_log), params_grad[0, :heads], share * heads, 0)
    bias_full = lax.dynamic_update_slice_in_dim(jnp.zeros_like(dt_bias), params_grad[1, :heads], share * heads, 0)
    gain_grad = gain_first[0] + gain_second[0]
    sums = flat([conv_full, straight_gain(gain_two_grad), gain_grad, log_full, bias_full])
    sums = lay.everywhere(sums).reshape(-1)
    late = lay.everywhere(flat([straight_gain(gain_one_grad)])).reshape(-1)[:features]
    ends = [conv_full.size]
    for size in (features, DV, all_heads, all_heads):
        ends.append(ends[-1] + size)
    norm_grad = jnp.stack([late, sums[ends[0] : ends[1]]])

    gate_grad, up_grad = lay.collect_rest(gate_own, 0), lay.collect_rest(up_own, 0)
    down_grad, out_grad = lay.collect_rest(down_own, 1), lay.collect_rest(out_own, 1)
    first_grad, second_grad = lay.collect_rest(first_own, 0), lay.collect_rest(second_own, 0)
    in_grads = []
    begin = 0
    for size in (keys, keys, vals, vals):
        part = slice(begin, begin + size)
        in_grads.append(
            lay.joined(*[[grads[0][:, part], grads[1][:, part]] for grads in zip(first_grad, second_grad)], 1)
        )
        begin += size
    for size in (heads, heads):
        in_grads.append(lay.joined(*[[grad[:, begin : begin + size]] for grad in second_grad], 1))
        begin += size
    return (
        output,
        tokens_grad,
        norm_grad,
        *in_grads,
        sums[: ends[0]].reshape(conv_full.shape),
        sums[ends[2] : ends[3]],
        sums[ends[3] : ends[4]],
        sums[ends[1] : ends[2]],
        lay.ordered(*out_grad, 0),
        lay.ordered(*gate_grad, 1),
        lay.ordered(*up_grad, 1),
        lay.ordered(*down_grad, 0),
    )


def solution(mesh):
    return jax.shard_map(
        shards,
        mesh=mesh,
        in_specs=(
            P(("dp", "tensor"), None),
            P(("dp", "tensor"), None),
            P("dp", None),
            P(("dp", "tensor")),
            P(),
            P("dp", "tensor"),
            P("dp", "tensor"),
            P("dp", "tensor"),
            P("dp", "tensor"),
            P("dp", "tensor"),
            P("dp", "tensor"),
            P(),
            P(),
            P(),
            P(),
            P("tensor", "dp"),
            P("dp", "tensor"),
            P("dp", "tensor"),
            P("tensor", "dp"),
        ),
        out_specs=(
            P(("dp", "tensor"), None),
            P(("dp", "tensor"), None),
            P(),
            P("dp", "tensor"),
            P("dp", "tensor"),
            P("dp", "tensor"),
            P("dp", "tensor"),
            P("dp", "tensor"),
            P("dp", "tensor"),
            P(),
            P(),
            P(),
            P(),
            P("tensor", "dp"),
            P("dp", "tensor"),
            P("dp", "tensor"),
            P("tensor", "dp"),
        ),
        check_vma=False,
    )
```

```python
import functools

import jax
import jax.numpy as jnp
from jax import lax
from jax.experimental import pallas as pl
from jax.experimental.pallas import tpu as pltpu
from jax.sharding import PartitionSpec as P

bf = jnp.bfloat16
f32 = jnp.float32
DK = 128
DV = 256
CHUNK = 128
LANES = 128
GROUPS = 2
EPS_ROW = 1e-06
EPS_UNIT = 1e-06
EPS_HEAD = 1e-05
NEG = -1e30
VMEM_LIMIT = 56 * 2**20
COST = 1.0


def dot(left, right, left_dim, right_dim):
    return lax.dot_general(
        left.astype(bf), right.astype(bf), (((left_dim,), (right_dim,)), ((), ())), preferred_element_type=f32
    )


def nn(left, right):
    return dot(left, right, 1, 0)


def nt(left, right):
    return dot(left, right, 1, 1)


def tn(left, right):
    return dot(left, right, 0, 0)


def exact(left, right):
    return lax.dot_general(
        left, right, (((1,), (0,)), ((), ())), precision=lax.Precision.HIGHEST, preferred_element_type=f32
    )


def softplus(v):
    return jnp.maximum(v, 0.0) + jnp.log(1.0 + jnp.exp(-jnp.abs(v)))


def sigmoid(v):
    return 1.0 / (1.0 + jnp.exp(-v))


def unit_lower_inverses(systems, places, others):
    eye = (places == others).astype(f32)
    size = 16
    same = (places // size) == (others // size)
    power = [jnp.where(same, a, 0.0) for a in systems]
    inverse = [eye - a for a in power]
    span = 2
    while span < size:
        power = [nn(a, a) for a in power]
        inverse = [t + nn(t, a) for t, a in zip(inverse, power)]
        span *= 2
    while size < places.shape[0]:
        corner = ((places // (2 * size)) == (others // (2 * size))) & ((places // size) != (others // size))
        steps = [nn(jnp.where(corner, a, 0.0), t) for a, t in zip(systems, inverse)]
        inverse = [t - nn(t, s) for t, s in zip(inverse, steps)]
        size *= 2
    return inverse


def conv_channels(padded, group, taps, marks, columns):
    total = taps[0:1, columns] * padded[group, 8 : 8 + CHUNK, columns]
    for offset in range(1, 4):
        total = total + (taps[offset : offset + 1, columns] * marks[:, offset : offset + 1]) * (
            padded[group, 8 - offset : 8 - offset + CHUNK, columns]
        )
    return total


class Unit:
    def __init__(self, group, head, heads, first, lanes, shared):
        self.group = group
        self.head = head
        keys = heads * DK
        self.query_columns = slice(head * DK, head * DK + DK)
        self.key_columns = slice(keys + head * DK, keys + head * DK + DK)
        self.value_columns = slice(2 * keys + head * DV, 2 * keys + head * DV + DV)
        start = 2 * keys + heads * DV + head * DV
        self.gate_columns = slice(start, start + DV)
        self.out_columns = slice(head * DV, head * DV + DV)
        self.lane = first + head
        self.beta_lane = lanes + first + head
        cum, cum_rows, beta, causal, opening, closing = shared
        col = cum[:, self.lane : self.lane + 1]
        row = cum_rows[self.lane : self.lane + 1, :]
        self.decay = jnp.exp(jnp.where(causal, col - row, NEG))
        self.opened = jnp.exp(jnp.where(opening, col, NEG))
        last = cum[CHUNK - 1 : CHUNK, self.lane : self.lane + 1]
        self.closed = jnp.exp(jnp.where(closing, last - col, NEG))
        self.opened_last = self.opened[CHUNK - 1 : CHUNK, :]
        self.strength = beta[:, self.beta_lane : self.beta_lane + 1]


def chunk_units(heads, first, lanes, decays_ref, params, marks_ref, seg_ref, places, others):
    units, kept = [], []
    lower = (places >= others).astype(f32)
    for group in range(GROUPS):
        decays = decays_ref[0, group, 0]
        marks = marks_ref[group, 0]
        biased = decays + params[0:1, :]
        log_decay = -params[1:2, :] * softplus(biased)
        cum = exact(lower, log_decay)
        beta = sigmoid(decays)
        causal = (places >= others) & (marks[:, 0:1] == seg_ref[group, 0])
        shared = (cum, cum.T, beta, causal, marks[:, 4:5] > 0.0, marks[:, 5:6] > 0.0)
        kept.append((biased, log_decay, beta, marks))
        for head in range(heads):
            units.append(Unit(group, head, heads, first, lanes, shared))
    return units, kept


def forward_kernel(
    heads, first, lanes, core_ref, proj, decays, marks_ref, seg_ref, taps, params, gain, partner,
    out, kept_state, kept_inverse, state, padded,
):
    conv_width = heads * (2 * DK + DV)

    @pl.when(pl.program_id(0) == 0)
    def _():
        state[...] = jnp.zeros_like(state)
        padded[:, 0:8, :] = jnp.zeros((GROUPS, 8, conv_width), f32)

    for group in range(GROUPS):
        padded[group, 8:, :] = proj[0, group, 0, :, :conv_width].astype(f32)
    places = lax.broadcasted_iota(jnp.int32, (CHUNK, CHUNK), 0)
    others = lax.broadcasted_iota(jnp.int32, (CHUNK, CHUNK), 1)
    units, kept = chunk_units(heads, first, lanes, decays, params, marks_ref, seg_ref, places, others)
    strict = places > others
    queries, key_vecs, values = [], [], []
    for unit in units:
        marks = kept[unit.group][3]
        summed = conv_channels(padded, unit.group, taps, marks, unit.query_columns)
        act = summed * sigmoid(summed)
        scale = lax.rsqrt(jnp.sum(act * act, axis=1, keepdims=True) + EPS_UNIT)
        queries.append((act * (scale * DK**-0.5)).astype(bf))
        summed = conv_channels(padded, unit.group, taps, marks, unit.key_columns)
        act = summed * sigmoid(summed)
        scale = lax.rsqrt(jnp.sum(act * act, axis=1, keepdims=True) + EPS_UNIT)
        key_vecs.append((act * scale).astype(bf))
    pairs = [jnp.concatenate([q, k], axis=0) for q, k in zip(queries, key_vecs)]
    dots = [nt(pair, k) for pair, k in zip(pairs, key_vecs)]
    systems = [jnp.where(strict, unit.strength * unit.decay * d[CHUNK:], 0.0) for unit, d in zip(units, dots)]
    inverses = unit_lower_inverses(systems, places, others)
    for unit in units:
        summed = conv_channels(padded, unit.group, taps, kept[unit.group][3], unit.value_columns)
        values.append((summed * sigmoid(summed)).astype(bf).astype(f32))
    for group in range(GROUPS):
        padded[group, 0:8, :] = padded[group, CHUNK : CHUNK + 8, :]
    before = [state[number] for number in range(len(units))]
    for number in range(len(units)):
        kept_state[0, number] = before[number].astype(bf)
        kept_inverse[0, number] = inverses[number].astype(bf)
    reads = [nn(pair, s) for pair, s in zip(pairs, before)]
    rights = [unit.strength * (v - unit.opened * read[CHUNK:]) for unit, v, read in zip(units, values, reads)]
    news = [nn(t, r) for t, r in zip(inverses, rights)]
    mixed = [
        unit.opened * read[:CHUNK] + nn(d[:CHUNK] * unit.decay, new)
        for unit, read, d, new in zip(units, reads, dots, news)
    ]
    for number, unit in enumerate(units):
        state[number] = unit.opened_last * before[number] + tn(key_vecs[number], unit.closed * news[number])
    for unit, mix in zip(units, mixed):
        gate = proj[0, unit.group, 0, :, unit.gate_columns].astype(f32)
        scale = lax.rsqrt(jnp.mean(mix * mix, axis=1, keepdims=True) + EPS_HEAD)
        out[0, unit.group, 0, :, unit.out_columns] = (mix * scale * gain[...] * (gate * sigmoid(gate))).astype(bf)


def backward_kernel(
    heads, first, lanes, core_ref, proj, prev_rows, decays, grads, marks_ref, seg_ref, taps, params, gain,
    kept_state, kept_inverse, earlier, proj_grad, taps_grad, params_grad, gain_grad, state_grad, padded, summed_grad,
):
    conv_width = heads * (2 * DK + DV)
    width = conv_width + heads * DV

    @pl.when(pl.program_id(0) == 0)
    def _():
        taps_grad[...] = jnp.zeros_like(taps_grad)
        params_grad[...] = jnp.zeros_like(params_grad)
        gain_grad[...] = jnp.zeros_like(gain_grad)
        state_grad[...] = jnp.zeros_like(state_grad)
        summed_grad[:, CHUNK:, :] = jnp.zeros((GROUPS, 8, conv_width), f32)

    for group in range(GROUPS):
        padded[group, 0:8, :] = prev_rows[0, group, 0, :, :conv_width].astype(f32)[-8:]
        padded[group, 8:, :] = proj[0, group, 0, :, :conv_width].astype(f32)
    places = lax.broadcasted_iota(jnp.int32, (CHUNK, CHUNK), 0)
    others = lax.broadcasted_iota(jnp.int32, (CHUNK, CHUNK), 1)
    units, kept = chunk_units(heads, first, lanes, decays, params, marks_ref, seg_ref, places, others)
    strict = places > others
    q_sums, k_sums, v_sums, q_acts, k_acts, q_scale, k_scale = [], [], [], [], [], [], []
    queries, key_vecs, values = [], [], []
    for unit in units:
        marks = kept[unit.group][3]
        summed = conv_channels(padded, unit.group, taps, marks, unit.query_columns)
        act = summed * sigmoid(summed)
        scale = lax.rsqrt(jnp.sum(act * act, axis=1, keepdims=True) + EPS_UNIT)
        queries.append((act * (scale * DK**-0.5)).astype(bf))
        q_sums.append(summed)
        q_acts.append(act)
        q_scale.append(scale)
        summed = conv_channels(padded, unit.group, taps, marks, unit.key_columns)
        act = summed * sigmoid(summed)
        scale = lax.rsqrt(jnp.sum(act * act, axis=1, keepdims=True) + EPS_UNIT)
        key_vecs.append((act * scale).astype(bf))
        k_sums.append(summed)
        k_acts.append(act)
        k_scale.append(scale)
        summed = conv_channels(padded, unit.group, taps, marks, unit.value_columns)
        values.append((summed * sigmoid(summed)).astype(bf).astype(f32))
        v_sums.append(summed)
    count = len(units)
    pairs = [jnp.concatenate([q, k], axis=0) for q, k in zip(queries, key_vecs)]
    dots = [nt(pair, k) for pair, k in zip(pairs, key_vecs)]
    before = [kept_state[0, number] for number in range(count)]
    after_grad = [state_grad[number] for number in range(count)]
    inverses = [kept_inverse[0, number] for number in range(count)]
    reads = [nn(pair, s) for pair, s in zip(pairs, before)]
    gaps = [v - unit.opened * read[CHUNK:] for unit, v, read in zip(units, values, reads)]
    news = [nn(t, unit.strength * g) for t, unit, g in zip(inverses, units, gaps)]
    scores = [d[:CHUNK] * unit.decay for d, unit in zip(dots, units)]
    mixed = [unit.opened * read[:CHUNK] + nn(score, new) for unit, read, score, new in zip(units, reads, scores, news)]
    mix_grads = []
    gain_row = gain[...]
    gain_total = jnp.zeros((1, DV), f32)
    for unit, mix in zip(units, mixed):
        gate = proj[0, unit.group, 0, :, unit.gate_columns].astype(f32)
        grad = grads[0, unit.group, 0, :, unit.out_columns].astype(f32)
        scale = lax.rsqrt(jnp.mean(mix * mix, axis=1, keepdims=True) + EPS_HEAD)
        soft = sigmoid(gate)
        grad_normed = grad * (mix * scale)
        proj_grad[0, unit.group, 0, :, unit.gate_columns] = (
            grad_normed * gain_row * (soft * (1.0 + gate * (1.0 - soft)))
        ).astype(bf)
        silu = gate * soft
        gain_total = gain_total + jnp.sum(grad_normed * silu, axis=0, keepdims=True)
        inner = grad * silu * gain_row
        mix_grads.append(scale * inner - mix * (scale * scale * scale) * jnp.mean(inner * mix, axis=1, keepdims=True))
    gain_grad[0:1, :] += gain_total
    pushes = [nn(k, g) for k, g in zip(key_vecs, after_grad)]
    new_grads = [
        tn(score, grad) + unit.closed * push for score, grad, unit, push in zip(scores, mix_grads, units, pushes)
    ]
    score_grads = [nt(grad, new) for grad, new in zip(mix_grads, news)]
    right_grads = [tn(t, grad) for t, grad in zip(inverses, new_grads)]
    system_grads = [jnp.where(strict, -nt(grad, new), 0.0) for grad, new in zip(right_grads, news)]
    lane_ids = lax.broadcasted_iota(jnp.int32, (CHUNK, LANES), 1)
    rows_down = lax.broadcasted_iota(jnp.int32, (CHUNK, 1), 0)
    cum_grads = [jnp.zeros((CHUNK, LANES), f32) for _ in range(GROUPS)]
    beta_grads = [jnp.zeros((CHUNK, LANES), f32) for _ in range(GROUPS)]
    cross_rows = [[], []]
    raised = []
    for number, unit in enumerate(units):
        read_query = reads[number][:CHUNK]
        read_key = reads[number][CHUNK:]
        gram = dots[number][CHUNK:]
        decayed_score = score_grads[number] * unit.decay
        decayed_system = system_grads[number] * unit.decay
        system_gram = decayed_system * gram
        crossing = decayed_score * dots[number][:CHUNK] + unit.strength * system_gram
        value_grad = unit.strength * right_grads[number]
        beta_grad = jnp.sum(system_gram, axis=1, keepdims=True) + jnp.sum(
            right_grads[number] * gaps[number], axis=1, keepdims=True
        )
        open_grad = jnp.sum(mix_grads[number] * read_query - value_grad * read_key, axis=1, keepdims=True)
        close_grad = unit.closed * jnp.sum(news[number] * pushes[number], axis=1, keepdims=True)
        kept_dot = jnp.sum(
            jnp.sum(after_grad[number] * before[number].astype(f32), axis=1, keepdims=True), axis=0, keepdims=True
        )
        last_grad = jnp.sum(close_grad, axis=0, keepdims=True) + unit.opened_last * kept_dot
        col = jnp.sum(crossing, axis=1, keepdims=True) + unit.opened * open_grad - close_grad
        col = col + jnp.where(rows_down == CHUNK - 1, last_grad, 0.0)
        cross_rows[unit.group].append(jnp.sum(crossing, axis=0, keepdims=True))
        cum_grads[unit.group] = jnp.where(lane_ids == unit.lane, col, cum_grads[unit.group])
        beta_grads[unit.group] = jnp.where(lane_ids == unit.beta_lane, beta_grad, beta_grads[unit.group])
        raised.append((decayed_score.astype(bf), (unit.strength * decayed_system).astype(bf), value_grad))
    stacked = [
        jnp.concatenate([(unit.opened * grad).astype(bf), (-unit.opened * item[2]).astype(bf)], axis=0)
        for unit, item, grad in zip(units, raised, mix_grads)
    ]
    through = [nt(x, s) for x, s in zip(stacked, before)]
    grams = [jnp.concatenate([item[0], item[1]], axis=0) for item in raised]
    direct = [nn(g, k) for g, k in zip(grams, key_vecs)]
    turned = [tn(g, pair) for g, pair in zip(grams, pairs)]
    pushed = [nt(unit.closed * new, grad) for unit, new, grad in zip(units, news, after_grad)]
    for number, unit in enumerate(units):
        state_grad[number] = unit.opened_last * after_grad[number] + tn(pairs[number], stacked[number])
    for number, unit in enumerate(units):
        query_grad = (through[number][:CHUNK] + direct[number][:CHUNK]) * DK**-0.5
        key_grad = through[number][CHUNK:] + direct[number][CHUNK:] + turned[number] + pushed[number]
        for grad, act, scale, summed, columns in (
            (query_grad, q_acts[number], q_scale[number], q_sums[number], unit.query_columns),
            (key_grad, k_acts[number], k_scale[number], k_sums[number], unit.key_columns),
        ):
            inner = scale * (grad - act * (scale * scale) * jnp.sum(grad * act, axis=1, keepdims=True))
            soft = sigmoid(summed)
            summed_grad[unit.group, 0:CHUNK, columns] = inner * (soft * (1.0 + summed * (1.0 - soft)))
        summed = v_sums[number]
        soft = sigmoid(summed)
        summed_grad[unit.group, 0:CHUNK, unit.value_columns] = raised[number][2] * (
            soft * (1.0 + summed * (1.0 - soft))
        )
    for group in range(GROUPS):
        marks = kept[group][3]
        for start in range(0, conv_width, LANES):
            columns = slice(start, start + LANES)
            grad = summed_grad[group, 0:CHUNK, columns]
            total = taps[0:1, columns] * grad
            taps_grad[0:1, columns] += jnp.sum(grad * padded[group, 8 : 8 + CHUNK, columns], axis=0, keepdims=True)
            for offset in range(1, 4):
                later = summed_grad[group, offset : offset + CHUNK, columns]
                total = total + (taps[offset : offset + 1, columns] * marks[:, 5 + offset : 6 + offset]) * later
                taps_grad[offset : offset + 1, columns] += jnp.sum(
                    (grad * marks[:, offset : offset + 1]) * padded[group, 8 - offset : 8 - offset + CHUNK, columns],
                    axis=0, keepdims=True,
                )
            proj_grad[0, group, 0, :, columns] = total.astype(bf)
        summed_grad[group, CHUNK:, :] = summed_grad[group, 0:8, :]
    upper = (places <= others).astype(f32)
    for group in range(GROUPS):
        biased, log_decay, beta, _ = kept[group]
        blank = [jnp.zeros((first, CHUNK), f32)] if first else []
        rest = [jnp.zeros((CHUNK - heads - first, CHUNK), f32)]
        cross = jnp.concatenate(blank + cross_rows[group] + rest, axis=0).T
        log_grad = exact(upper, cum_grads[group] - cross)
        decay_grad = log_grad * (-params[1:2, :]) * sigmoid(biased)
        both = decay_grad + beta_grads[group] * beta * (1.0 - beta)
        if earlier is not None:
            both = both + earlier[0, group, 0].astype(f32)
        proj_grad[0, group, 0, :, width:] = both.astype(bf)
        params_grad[0:1, :] += jnp.sum(log_grad * log_decay, axis=0, keepdims=True)
        params_grad[1:2, :] += jnp.sum(decay_grad, axis=0, keepdims=True)


def folded(rows):
    return rows.reshape(2, GROUPS, -1, CHUNK, rows.shape[1])


def mixer_forward(first, lanes, core, proj, decays, marks, seg_rows, taps, params, gain, partner):
    conv_width = taps.shape[1]
    heads = conv_width // (2 * DK + DV)
    proj, decays = folded(proj), folded(decays)
    per_core = proj.shape[2]
    chunks = 2 * per_core
    units = GROUPS * heads

    def at(c, core_ref):
        return ((c // per_core) ^ core_ref[0], 0, c % per_core, 0, 0)

    fixed = lambda c, core_ref: (0, 0)
    here = lambda c, core_ref: (0, c, 0, 0)
    kept = lambda c, core_ref: (c, 0, 0, 0)
    full = proj.shape[:4] + (lanes * DV,)
    body = functools.partial(forward_kernel, heads, first, lanes)
    more_specs, more, aliases = [], [], {}
    if partner is None:
        inner = body

        def body(*refs):
            return inner(*refs[:8], None, *refs[8:])

    else:
        more_specs, more, aliases = [pl.BlockSpec(memory_space=pl.ANY)], [partner.reshape(full)], {8: 0}

    def out_at(c, core_ref):
        return at(c, core_ref)[:4] + (first // heads,)

    out, states, inverses = pl.pallas_call(
        body,
        grid_spec=pltpu.PrefetchScalarGridSpec(
            num_scalar_prefetch=1,
            grid=(chunks,),
            in_specs=[
                pl.BlockSpec((1, GROUPS, 1, CHUNK, proj.shape[4]), at),
                pl.BlockSpec((1, GROUPS, 1, CHUNK, LANES), at),
                pl.BlockSpec((GROUPS, 1, CHUNK, LANES), here),
                pl.BlockSpec((GROUPS, 1, 1, CHUNK), here),
                pl.BlockSpec((4, conv_width), fixed),
                pl.BlockSpec((8, LANES), fixed),
                pl.BlockSpec((1, DV), fixed),
            ]
            + more_specs,
            out_specs=[
                pl.BlockSpec((1, GROUPS, 1, CHUNK, heads * DV), out_at),
                pl.BlockSpec((1, units, DK, DV), kept),
                pl.BlockSpec((1, units, CHUNK, CHUNK), kept),
            ],
            scratch_shapes=[pltpu.VMEM((units, DK, DV), f32), pltpu.VMEM((GROUPS, CHUNK + 8, conv_width), f32)],
        ),
        out_shape=[
            jax.ShapeDtypeStruct(full, bf),
            jax.ShapeDtypeStruct((chunks, units, DK, DV), bf),
            jax.ShapeDtypeStruct((chunks, units, CHUNK, CHUNK), bf),
        ],
        compiler_params=pltpu.CompilerParams(vmem_limit_bytes=VMEM_LIMIT),
        cost_estimate=pl.CostEstimate(flops=int(COST * 16 * 10**9), bytes_accessed=int(COST * 16 * 2**20), transcendentals=0),
        input_output_aliases=aliases,
        name="mixer_forward",
    )(core, proj, decays, marks, seg_rows, taps, params, gain, *more)
    return out.reshape(-1, lanes * DV), states, inverses


def mixer_backward(first, lanes, core, proj, decays, grads, marks, seg_rows, taps, params, gain, states, inverses, earlier):
    conv_width = taps.shape[1]
    heads = conv_width // (2 * DK + DV)
    proj, decays, grads = folded(proj), folded(decays), folded(grads)
    per_core = proj.shape[2]
    chunks = 2 * per_core
    units = GROUPS * heads
    width = conv_width + heads * DV + LANES
    tail = 16

    def at(step, core_ref):
        c = chunks - 1 - step
        return ((c // per_core) ^ core_ref[0], 0, c % per_core, 0, 0)

    def prev(step, core_ref):
        c = jnp.maximum(chunks - 2 - step, 0)
        return ((c // per_core) ^ core_ref[0], 0, c % per_core, CHUNK // tail - 1, 0)

    def grad_at(step, core_ref):
        return at(step, core_ref)[:4] + (first // heads,)

    def last_lanes(step, core_ref):
        return at(step, core_ref)[:4] + ((conv_width + heads * DV) // LANES,)

    fixed = lambda step, core_ref: (0, 0)
    here = lambda step, core_ref: (0, chunks - 1 - step, 0, 0)
    kept = lambda step, core_ref: (chunks - 1 - step, 0, 0, 0)
    in_specs = [
        pl.BlockSpec((1, GROUPS, 1, CHUNK, proj.shape[4]), at),
        pl.BlockSpec((1, GROUPS, 1, tail, proj.shape[4]), prev),
        pl.BlockSpec((1, GROUPS, 1, CHUNK, LANES), at),
        pl.BlockSpec((1, GROUPS, 1, CHUNK, heads * DV), grad_at),
        pl.BlockSpec((GROUPS, 1, CHUNK, LANES), here),
        pl.BlockSpec((GROUPS, 1, 1, CHUNK), here),
        pl.BlockSpec((4, conv_width), fixed),
        pl.BlockSpec((8, LANES), fixed),
        pl.BlockSpec((1, DV), fixed),
        pl.BlockSpec((1, units, DK, DV), kept),
        pl.BlockSpec((1, units, CHUNK, CHUNK), kept),
    ]
    inputs = [core, proj, proj, decays, grads, marks, seg_rows, taps, params, gain, states, inverses]
    body = functools.partial(backward_kernel, heads, first, lanes)
    if earlier is not None:
        in_specs.append(pl.BlockSpec((1, GROUPS, 1, CHUNK, LANES), last_lanes))
        inputs.append(folded(earlier))
    else:
        whole = body

        def body(*refs):
            return whole(*refs[:12], None, *refs[12:])

    out, taps_grad, params_grad, gain_grad = pl.pallas_call(
        body,
        grid_spec=pltpu.PrefetchScalarGridSpec(
            num_scalar_prefetch=1,
            grid=(chunks,),
            in_specs=in_specs,
            out_specs=[
                pl.BlockSpec((1, GROUPS, 1, CHUNK, width), at),
                pl.BlockSpec((4, conv_width), fixed),
                pl.BlockSpec((8, LANES), fixed),
                pl.BlockSpec((8, DV), fixed),
            ],
            scratch_shapes=[
                pltpu.VMEM((units, DK, DV), f32),
                pltpu.VMEM((GROUPS, CHUNK + 8, conv_width), f32),
                pltpu.VMEM((GROUPS, CHUNK + 8, conv_width), f32),
            ],
        ),
        out_shape=[
            jax.ShapeDtypeStruct(proj.shape[:4] + (width,), bf),
            jax.ShapeDtypeStruct((4, conv_width), f32),
            jax.ShapeDtypeStruct((8, LANES), f32),
            jax.ShapeDtypeStruct((8, DV), f32),
        ],
        compiler_params=pltpu.CompilerParams(vmem_limit_bytes=VMEM_LIMIT),
        cost_estimate=pl.CostEstimate(flops=int(COST * 30 * 10**9), bytes_accessed=int(COST * 30 * 2**20), transcendentals=0),
        name="mixer_backward",
    )(*inputs)
    return out.reshape(-1, width), taps_grad, params_grad, gain_grad


def group_marks(lengths, group_rows):
    groups, count = lengths.shape
    position = jnp.arange(group_rows, dtype=jnp.int32)[None, :]
    segment = jnp.zeros((groups, group_rows), jnp.int32)
    end = jnp.zeros((groups, 1), jnp.int32)
    for number in range(count):
        segment = segment + (position >= end).astype(jnp.int32)
        end = end + lengths[:, number : number + 1]
    live = (position < end).astype(f32)
    padded = jnp.pad(segment, ((0, 0), (CHUNK, CHUNK)))
    later = lambda offset: padded[:, CHUNK + offset : CHUNK + offset + group_rows]
    chunked = segment.reshape(groups, group_rows // CHUNK, CHUNK)
    before = padded[:, CHUNK - 1 : CHUNK - 1 + group_rows].reshape(chunked.shape)[:, :, :1]
    columns = [segment]
    columns += [later(-offset) == segment for offset in (1, 2, 3)]
    columns += [(chunked == before).reshape(segment.shape), (chunked == chunked[:, :, -1:]).reshape(segment.shape)]
    columns += [later(offset) == segment for offset in (1, 2, 3)]
    lane = jnp.arange(LANES, dtype=jnp.int32)
    marks = jnp.zeros((groups, group_rows, LANES), f32)
    for number, column in enumerate(columns):
        marks = jnp.where(lane == number, column.astype(f32)[:, :, None], marks)
    marks = marks.reshape(groups, group_rows // CHUNK, CHUNK, LANES)
    seg_rows = segment.astype(f32).reshape(groups, group_rows // CHUNK, 1, CHUNK)
    return marks, seg_rows, live


def pick_kernel(pairs, turn_ref, *refs):
    count = len(refs) - len(pairs)
    for out, parts in zip(refs[count:], pairs):
        begin = 0
        for number, start, stop in parts:
            out[:, begin : begin + stop - start] = refs[number][:, start:stop]
            begin += stop - start


def picked(turn, weights, axes, joins):
    in_specs, inputs, shapes = [], [], []
    for weight, axis in zip(weights, axes):
        rows, columns = weight.shape
        if axis is None:
            in_specs += [pl.BlockSpec((rows, columns), lambda i, t: (0, 0))] * 2
            shapes.append((rows, columns))
        elif axis == 1:
            in_specs += [
                pl.BlockSpec((rows, columns // 2), lambda i, t: (0, t[0])),
                pl.BlockSpec((rows, columns // 2), lambda i, t: (0, 1 - t[0])),
            ]
            shapes.append((rows, columns // 2))
        else:
            in_specs += [
                pl.BlockSpec((rows // 2, columns), lambda i, t: (t[0], 0)),
                pl.BlockSpec((rows // 2, columns), lambda i, t: (1 - t[0], 0)),
            ]
            shapes.append((rows // 2, columns))
        inputs += [weight, weight]
    pairs, out_shapes = [], []
    for join in joins:
        width = sum(stop - start for _, start, stop in join)
        for given in (0, 1):
            pairs.append([(2 * number + given, start, stop) for number, start, stop in join])
            out_shapes.append((shapes[join[0][0]][0], width))
    outs = pl.pallas_call(
        functools.partial(pick_kernel, pairs),
        grid_spec=pltpu.PrefetchScalarGridSpec(
            num_scalar_prefetch=1,
            grid=(1,),
            in_specs=in_specs,
            out_specs=[pl.BlockSpec(shape, lambda i, t: (0, 0)) for shape in out_shapes],
        ),
        out_shape=[jax.ShapeDtypeStruct(shape, bf) for shape in out_shapes],
        compiler_params=pltpu.CompilerParams(vmem_limit_bytes=VMEM_LIMIT),
        cost_estimate=pl.CostEstimate(flops=0, bytes_accessed=8 * 2**20, transcendentals=0),
        name="picked",
    )(turn, *inputs)
    return [(outs[2 * number], outs[2 * number + 1]) for number in range(len(joins))]


TILE = 256
STRIP = 256


def call(body, grid, in_specs, out_specs, out_shape, flops, moved, name, inputs, scratch=()):
    return pl.pallas_call(
        body,
        grid=grid,
        scratch_shapes=scratch,
        in_specs=in_specs,
        out_specs=out_specs,
        out_shape=out_shape,
        compiler_params=pltpu.CompilerParams(vmem_limit_bytes=VMEM_LIMIT),
        cost_estimate=pl.CostEstimate(flops=int(flops * COST), bytes_accessed=int(moved * COST), transcendentals=0),
        name=name,
    )(*inputs)


def strip_sum(rows, pieces, start, product):
    total = None
    begin = 0
    depth = rows.shape[1] // len(pieces)
    for piece in pieces:
        part = product(rows[start : start + STRIP, begin : begin + depth], piece[...])
        total = part if total is None else total + part
        begin += depth
    return total


def whole(array):
    return pl.BlockSpec(array.shape, lambda i: (0,) * array.ndim)


def project(rows, pieces, width, extra):
    count = rows.shape[0]
    depth = pieces[0].shape[0]
    steps = width // TILE
    used = len(pieces)

    def body(rows_ref, *refs):
        weights = refs[:used]
        out = refs[2 * used if extra else used]
        for start in range(0, count, STRIP):
            out[start : start + STRIP, :] = strip_sum(rows_ref, weights, start, nn).astype(bf)
        if extra:

            @pl.when(pl.program_id(0) == 0)
            def _():
                for start in range(0, count, STRIP):
                    refs[-1][start : start + STRIP, :] = strip_sum(rows_ref, refs[used : 2 * used], start, nn)

    in_specs = [whole(rows)] + [pl.BlockSpec((depth, TILE), lambda i: (0, i))] * used
    out_specs = [pl.BlockSpec((count, TILE), lambda i: (0, i))]
    out_shape = [jax.ShapeDtypeStruct((count, width), bf)]
    inputs = [rows, *pieces]
    if extra:
        in_specs += [pl.BlockSpec((depth, LANES), lambda i: (0, width // LANES))] * used
        out_specs.append(pl.BlockSpec((count, LANES), lambda i: (0, 0)))
        out_shape.append(jax.ShapeDtypeStruct((count, LANES), f32))
        inputs += pieces
    flops = 2 * count * depth * used * width
    moved = 2 * (count * depth * used + depth * used * width + count * width)
    return call(body, (steps,), in_specs, out_specs, out_shape, flops, moved, "project", inputs)


def feed_forward(rows, pieces):
    count = rows.shape[0]
    depth, width = pieces[0].shape
    used = len(pieces)

    def body(rows_ref, *refs):
        pre_out, hidden_out = refs[used:]
        for start in range(0, count, STRIP):
            strip = slice(start, start + STRIP)
            both = strip_sum(rows_ref, refs[:used], start, nn)
            gate = both[:, :LANES]
            pre_out[strip, :] = both.astype(bf)
            hidden_out[strip, :] = (gate * sigmoid(gate) * both[:, LANES:]).astype(bf)

    return call(
        body,
        (width // (2 * LANES),),
        [whole(rows)] + [pl.BlockSpec((depth, 2 * LANES), lambda i: (0, i))] * used,
        [pl.BlockSpec((count, 2 * LANES), lambda i: (0, i)), pl.BlockSpec((count, LANES), lambda i: (0, i))],
        [jax.ShapeDtypeStruct((count, width), bf), jax.ShapeDtypeStruct((count, width // 2), bf)],
        2 * count * depth * used * width,
        2 * (count * depth * used + depth * used * width + 2 * count * width),
        "feed_forward",
        [rows, *pieces],
    )


def feed_backward(rows, down_pieces, pre):
    count = rows.shape[0]
    width, depth = down_pieces[0].shape
    used = len(down_pieces)

    def body(rows_ref, *refs):
        pre_ref, out = refs[used:]
        for begin in range(0, width, TILE):
            size = min(TILE, width - begin)
            total = None
            for number in range(used):
                part = nt(rows_ref[:, number * depth : number * depth + depth], refs[number][begin : begin + size, :])
                total = part if total is None else total + part
            for shift in range(0, size, LANES):
                grad = total[:, shift : shift + LANES]
                at = 2 * (begin + shift)
                gate = pre_ref[:, at : at + LANES].astype(f32)
                up = pre_ref[:, at + LANES : at + 2 * LANES].astype(f32)
                soft = sigmoid(gate)
                out[:, at : at + LANES] = (grad * up * soft * (1.0 + gate * (1.0 - soft))).astype(bf)
                out[:, at + LANES : at + 2 * LANES] = (grad * gate * soft).astype(bf)

    strip = pl.BlockSpec((STRIP, 2 * width), lambda i: (i, 0))
    return call(
        body,
        (count // STRIP,),
        [pl.BlockSpec((STRIP, depth * used), lambda i: (i, 0))] + [whole(piece) for piece in down_pieces] + [strip],
        strip,
        jax.ShapeDtypeStruct((count, 2 * width), bf),
        2 * count * depth * used * width,
        2 * (count * depth * used + depth * used * width + 4 * count * width),
        "feed_backward",
        [rows, *down_pieces, pre],
    )


def heads_backward(rows, out_pieces):
    count = rows.shape[0]
    width, depth = out_pieces[0].shape
    used = len(out_pieces)

    def body(rows_ref, *refs):
        for start in range(0, count, STRIP):
            refs[used][start : start + STRIP, :] = strip_sum(rows_ref, refs[:used], start, nt).astype(bf)

    return call(
        body,
        (width // TILE,),
        [whole(rows)] + [pl.BlockSpec((TILE, depth), lambda i: (i, 0))] * used,
        pl.BlockSpec((count, TILE), lambda i: (0, i)),
        jax.ShapeDtypeStruct((count, width), bf),
        2 * count * depth * used * width,
        2 * (count * depth * used + depth * used * width + count * width),
        "heads_backward",
        [rows, *out_pieces],
    )


def wide(terms, lefts, pieces, product, features, got):
    count = lefts[0].shape[0]
    half, per = count // 2, count // 4
    depth = features // 4
    given = got is None
    used = len(pieces)
    inputs = list(lefts) + [piece for group in pieces for piece in group]
    in_specs = [pl.BlockSpec((half, left.shape[1]), (lambda i: (1, 0)) if given else (lambda i: (0, 0))) for left in lefts]
    in_specs += [pl.BlockSpec(memory_space=pl.ANY)] * (4 * used)
    flops = 2 * half * features * sum(term[4] for term in terms)
    moved = 2 * sum(piece.size for group in pieces for piece in group) + 6 * count * features
    skip = len(lefts) + 4 * used

    def body(*refs):
        held, sems = refs[-1 - used : -1], refs[-1]

        def copy(number, piece):
            source = refs[len(lefts) + 4 * number + piece]
            return pltpu.make_async_copy(source, held[number].at[piece], sems.at[number, piece])

        for piece in range(4):
            for number in range(used):
                copy(number, piece).start()
        for piece in range(4):
            columns = slice(piece * depth, piece * depth + depth)
            for number in range(used):
                copy(number, piece).wait()
            for strip in range(2):
                rows = slice(strip * per, strip * per + per)
                total = None
                for number, begin, weight, first, size in terms:
                    left = refs[number][rows, begin : begin + size]
                    right = held[weight][piece]
                    right = right[:, first : first + size] if product is nt else right
                    part = product(left, right)
                    total = part if total is None else total + part
                if given:
                    refs[skip][rows, columns] = total.astype(bf)
                else:
                    total = total + refs[skip][rows, columns].astype(f32)
                    if strip == 0:
                        refs[skip + 2][:, columns] = total
                    else:
                        refs[skip + 1][:, columns] = total.astype(bf)

    scratch = [pltpu.VMEM((4,) + group[0].shape, bf) for group in pieces] + [pltpu.SemaphoreType.DMA((used, 4))]
    if given:
        out_specs = pl.BlockSpec((half, features), lambda i: (0, 0))
        out_shape = jax.ShapeDtypeStruct((half, features), bf)
    else:
        in_specs.append(pl.BlockSpec((half, features), lambda i: (0, 0)))
        inputs.append(got)
        out_specs = [pl.BlockSpec((per, features), lambda i: (0, 0))] * 2
        out_shape = [jax.ShapeDtypeStruct((per, features), bf), jax.ShapeDtypeStruct((per, features), f32)]
    return call(
        body, (1,), in_specs, out_specs, out_shape, flops, moved, "wide_given" if given else "wide_kept", inputs, scratch
    )


RING = (0, 1, 3, 2)


def matmul(left, right):
    return jnp.dot(left, right, preferred_element_type=f32)


def outer_sum(left, right):
    return lax.dot_general(left, right, (((0,), (0,)), ((), ())), preferred_element_type=f32)


def times_back(left, right):
    return lax.dot_general(left, right, (((1,), (1,)), ((), ())), preferred_element_type=f32)


def norm_back(inputs, scale, gain, grad_out):
    scaled = grad_out * gain
    grad_in = scale * scaled - inputs * scale**3 * jnp.mean(scaled * inputs, axis=1, keepdims=True)
    return (grad_in, jnp.sum(grad_out * inputs * scale, axis=0))


class Layout:
    def __init__(self):
        self.ways = lax.axis_size("dp")
        self.spans = self.ways // 8
        dp = lax.axis_index("dp")
        self.core = lax.axis_index("tensor")
        self.turn = (dp // 4) % 2
        self.far = dp // 8
        near = dp % 4
        self.spot = near ^ (near >> 1)
        self.queues = {}

    def queued(self, values, queue, depth):
        line = self.queues.setdefault(queue, [])
        if len(line) >= depth:
            values, _ = lax.optimization_barrier((values, line[-depth]))
        return values, line

    def ring(self, values, step):
        pairs = []
        for number in range(self.ways):
            near = number % 4
            pairs.append((number, number - near + RING[((near ^ (near >> 1)) + step) % 4]))
        values, line = self.queued(values, step, DEPTH)
        line.append(lax.ppermute(values, "dp", pairs))
        return line[-1]

    def flip(self, values, bit):
        return lax.ppermute(values, "dp", [(n, n ^ bit) for n in range(self.ways)])

    def turned(self, values):
        return self.flip(values, 4)

    def crossed(self, values):
        return lax.ppermute(values, "tensor", [(0, 1), (1, 0)])

    def far_bits(self):
        bit = 8
        while bit < self.ways:
            yield bit
            bit *= 2

    def sources(self):
        places = jnp.arange(self.ways, dtype=jnp.int32)
        step = places // (2 * self.spans)
        jump = (places // 2) % self.spans
        spot = (self.spot + step) % 4
        return ((self.far ^ jump) * 2 + places % 2) * 4 + (spot ^ (spot >> 1))

    def ordered(self, first, second, axis):
        return jnp.where(
            self.turn == 0, jnp.concatenate([first, second], axis=axis), jnp.concatenate([second, first], axis=axis)
        )

    def tie(self, values, *others):
        return lax.optimization_barrier((values, *others))[0]

    def spread_far(self, chunk, axis, *others):
        for bit in self.far_bits():
            sent, line = self.queued(chunk, "far", DEPTH)
            line.append(self.flip(sent, bit))
            line[-1] = self.tie(line[-1], *others)
            chunk = jnp.concatenate([chunk, line[-1]], axis=axis)
        return chunk

    def spread_ring(self, chunk, upward):
        ahead = self.ring(chunk, -1)
        behind = self.ring(chunk, 1)
        across = self.ring(behind, 1) if upward else self.ring(ahead, -1)
        return [chunk, ahead, across, behind]

    def collect_ring(self, make, upward):
        across = make(2).astype(bf)
        if upward:
            behind = make(3).astype(bf)
            up = self.ring(across, 1)
            down = self.ring(behind, -1)
            last = self.ring((make(1) + up).astype(bf), 1)
            return make(0) + last + down, (across, behind), (up, down, last)
        ahead = make(1).astype(bf)
        down = self.ring(across, -1)
        up = self.ring(ahead, 1)
        last = self.ring((make(3) + down).astype(bf), -1)
        return make(0) + up + last, (across, ahead), (down, up, last)

    def collect_far(self, own, axis):
        for bit in reversed(list(self.far_bits())):
            half = own.shape[axis] // 2
            sent = lax.slice_in_dim(own, half, 2 * half, axis=axis)
            own = lax.slice_in_dim(own, 0, half, axis=axis), self.flip(sent.astype(bf), bit)
            if bit > 8:
                own = own[0] + own[1]
        return own

    def collect_last(self, own, axis, *others):
        if isinstance(own, tuple):
            own = own[0] + self.tie(own[1], *others)
        half = own.shape[axis] // 2
        mine = lax.dynamic_slice_in_dim(own, self.turn * half, half, axis)
        other = lax.dynamic_slice_in_dim(own, (1 - self.turn) * half, half, axis)
        return mine, self.turned(other.astype(bf))

    def joined(self, mine, theirs, axis):
        return self.ordered(jnp.concatenate(mine, axis=axis), jnp.concatenate(theirs, axis=axis), axis)

    def rows_of(self, own):
        across = self.crossed(own)
        there = self.turned(own)
        return jnp.concatenate([own, there, across, self.crossed(there)], axis=0)

    def own_of(self, terms, lefts, pieces, product, features):
        given = wide(terms, lefts, pieces, product, features, None)
        there, own = wide(terms, lefts, pieces, product, features, self.crossed(given))
        return own + self.turned(there)

    def everywhere(self, values, marks):
        bits = []
        bit = 1
        while bit < self.ways:
            bits.append(bit)
            bit *= 2
        for bit in reversed(bits):
            values = values + self.tie(self.flip(values, bit), *marks)
        return values + self.crossed(values)


DEPTH = 1


def flat(parts):
    joined = jnp.concatenate([part.reshape(-1) for part in parts])
    return jnp.pad(joined, (0, -joined.shape[0] % (8 * LANES))).reshape(-1, LANES)


def shards(
    tokens, cotangent, lengths, slot_of, norm_gains, w_query, w_key, w_value, w_gate, w_decay, w_beta,
    conv_weights, a_log, dt_bias, out_gain, w_out, w_mlp_gate, w_mlp_up, w_mlp_down,
):
    lay = Layout()
    row_count, features = tokens.shape
    tensor_ways = lax.axis_size("tensor")
    device_count = lay.ways * tensor_ways
    group_rows = row_count * tensor_ways
    capacity = row_count // device_count + 2
    bulk_rows = device_count * capacity
    all_heads = a_log.shape[0]
    heads = all_heads // (2 * tensor_ways)
    pair = heads // 2
    all_keys = all_heads * DK
    keys, vals = pair * DK, pair * DV
    width = 2 * keys + 2 * vals
    share = lay.core * 2 + lay.turn
    turn = lay.turn.reshape(1)
    core = lay.core.reshape(1)

    target = slot_of // row_count
    within = slot_of % row_count
    hits = target[:, None] == jnp.arange(device_count, dtype=jnp.int32)[None, :]
    places = jnp.arange(row_count, dtype=jnp.int32)
    earlier = (places[:, None] >= places[None, :]).astype(bf)
    rank = jnp.sum(matmul(earlier, hits.astype(bf)) * hits.astype(f32), axis=1).astype(jnp.int32) - 1
    outgoing = target * capacity + rank
    sending = (jnp.arange(bulk_rows, dtype=jnp.int32)[:, None] == outgoing[None, :]).astype(bf)
    slot_mark = jnp.broadcast_to((within + 1).astype(bf)[:, None], (row_count, LANES))
    send_tokens = matmul(sending, jnp.concatenate([tokens, slot_mark], axis=1)).astype(bf)
    send_cot = matmul(sending, cotangent).astype(bf)

    def exchange(values):
        return lax.all_to_all(values, ("dp", "tensor"), split_axis=0, concat_axis=0, tiled=True)


    def half_heads(weight):
        kept = jnp.where(lay.turn == 0, weight[:, :heads], weight[:, heads:])
        given = jnp.where(lay.turn == 0, weight[:, heads:], weight[:, :heads])
        return kept, given

    decay_halves, beta_halves = half_heads(w_decay), half_heads(w_beta)
    lanes_of = [
        jnp.pad(jnp.concatenate([d, b], axis=1), ((0, 0), (0, LANES - 2 * heads)))
        for d, b in zip(decay_halves, beta_halves)
    ]
    first_join = [(0, 0, keys), (1, 0, keys), (2, 0, vals), (3, 0, vals)]
    second_join = [(0, keys, 2 * keys), (1, keys, 2 * keys), (2, vals, 2 * vals), (3, vals, 2 * vals)]
    out_rows, hidden_here = w_out.shape[0] // 2, w_mlp_gate.shape[1] // 2
    block = features // lay.ways
    mixed_join = []
    for start in range(0, hidden_here, LANES):
        mixed_join += [(0, start, start + LANES), (1, start, start + LANES)]
    blob_first, (second_keep, second_give) = picked(
        turn, [w_query, w_key, w_value, w_gate], [1] * 4, [first_join, second_join]
    )
    first_keep, first_give = [
        jnp.concatenate([blob, extra], axis=1) for blob, extra in zip(blob_first, lanes_of)
    ]
    first_got = lay.turned(first_give)
    got_tokens = exchange(lay.tie(send_tokens, first_got))
    first_chunk = lay.spread_far(lay.ordered(first_keep, first_got, 0), 0)
    second_got = lay.turned(lay.tie(second_give, first_chunk))
    [(feed_keep, feed_give)] = picked(turn, [w_mlp_gate, w_mlp_up], [1, 1], [mixed_join])

    def half_rows(weight):
        half = weight.shape[0] // 2
        return [lax.dynamic_slice_in_dim(weight, place * half, half, 0) for place in (lay.turn, 1 - lay.turn)]

    out_keep, out_give = half_rows(w_out)
    down_keep, down_give = half_rows(w_mlp_down)
    tall_got = lay.turned(lay.tie(jnp.concatenate([out_give, down_give], axis=0), second_got))
    feed_got = lay.turned(lay.tie(feed_give, second_got))
    second_chunk = lay.spread_far(lay.ordered(second_keep, second_got, 0), 0)
    in_first = lay.spread_ring(first_chunk, True)
    tall_got = lay.tie(tall_got, in_first[1], in_first[3])
    out_chunk = lay.spread_far(lay.ordered(out_keep, tall_got[:out_rows], 1), 1)
    in_second = lay.spread_ring(second_chunk, False)
    out_pieces = lay.spread_ring(out_chunk, True)

    got_slot = got_tokens[:, features].astype(jnp.int32)
    landing = (places[:, None] + 1 == got_slot[None, :]).astype(bf)
    sources = lay.sources()
    feature = jnp.arange(features, dtype=jnp.int32)
    origin = (sources[:, None] * block + jnp.arange(block, dtype=jnp.int32)[None, :]).reshape(1, -1)
    turning = (feature[:, None] == origin).astype(bf)
    numbers = jnp.arange(lay.ways, dtype=jnp.int32)
    picking = (sources[:, None] == numbers[None, :]).astype(f32)

    def reordered_gain(gain):
        return jnp.sum(picking[:, :, None] * gain.reshape(1, lay.ways, block), axis=1).reshape(features)

    def straight_gain(grad):
        return jnp.sum(picking[:, :, None] * grad.reshape(lay.ways, 1, block), axis=0).reshape(features)

    gains = (reordered_gain(norm_gains[0]), reordered_gain(norm_gains[1]))
    x_own = matmul(matmul(landing, got_tokens[:, :features]).astype(bf), turning)

    pair_lengths = jnp.concatenate([lengths, lay.turned(lengths)], axis=0)
    marks, seg_rows, live = group_marks(pair_lengths, group_rows)
    live_own = lax.dynamic_slice_in_dim(live[0], lay.core * row_count, row_count)[:, None]
    starts = [(share * heads + first) * DK for first in (0, pair)]
    cuts = [
        [(start, keys), (all_keys + start, keys), (2 * all_keys + 2 * start, vals)] for start in starts
    ]
    taps = [
        jnp.concatenate([lax.dynamic_slice_in_dim(conv_weights, start, size, 1) for start, size in cut], axis=1)
        for cut in cuts
    ]
    log_here = lax.dynamic_slice_in_dim(a_log, share * heads, heads)
    bias_here = lax.dynamic_slice_in_dim(dt_bias, share * heads, heads)
    params = jnp.pad(jnp.stack([bias_here, jnp.exp(log_here)]), ((0, 6), (0, LANES - heads)))
    gain_row = out_gain[None, :]

    scale_one = lax.rsqrt(jnp.mean(x_own * x_own, axis=1, keepdims=True) + EPS_ROW)
    first_rows = lay.rows_of((x_own * scale_one * gains[0]).astype(bf))
    proj_first, decays = project(first_rows, in_first, width, True)
    feed_chunk = lay.spread_far(lay.ordered(feed_keep, lay.tie(feed_got, first_rows), 0), 0, proj_first)
    heads_out, states_first, inverses_first = mixer_forward(
        0, heads, core, proj_first, decays, marks, seg_rows, taps[0], params, gain_row, None
    )
    proj_second = project(first_rows, in_second, width, False)[0]
    heads_out, states_second, inverses_second = mixer_forward(
        pair, heads, core, proj_second, decays, marks, seg_rows, taps[1], params, gain_row, heads_out
    )
    mixed_own = lay.own_of([(0, 0, 0, 0, out_rows)], [lay.tie(heads_out, feed_chunk)], [out_pieces], nn, features)
    middle = x_own + live_own * mixed_own

    got_cot = exchange(lay.tie(send_cot, in_second[2]))
    scale_two = lax.rsqrt(jnp.mean(middle * middle, axis=1, keepdims=True) + EPS_ROW)
    second_own_rows = (middle * scale_two * gains[1]).astype(bf)
    second_rows = lay.rows_of(second_own_rows)
    feed_behind = lay.ring(feed_chunk, 1)
    feed_ahead = lay.ring(feed_chunk, -1)
    feed_across = lay.ring(lay.tie(feed_ahead, second_own_rows), -1)
    feed_pieces = [feed_chunk, feed_ahead, feed_across, feed_behind]
    down_chunk = lay.spread_far(lay.ordered(down_keep, tall_got[out_rows:], 1), 1, second_own_rows)
    down_pieces = lay.spread_ring(down_chunk, True)
    dy_own = matmul(matmul(landing, lay.tie(got_cot, mixed_own)).astype(bf), turning)
    branch_rows = lay.rows_of((live_own * dy_own).astype(bf))
    pre, hidden = feed_forward(second_rows, feed_pieces)
    depth = features // 4

    def columns_of(rows, piece):
        return rows[:, piece * depth : piece * depth + depth]

    down_own, down_terms, down_sent = lay.collect_ring(lambda r: outer_sum(hidden, columns_of(branch_rows, r)), True)
    grad_pre = feed_backward(lay.tie(branch_rows, *down_terms), down_pieces, pre)
    feed_own, feed_terms, feed_sent = lay.collect_ring(
        lambda r: outer_sum(columns_of(second_rows, r), grad_pre), False
    )
    grad_second = lay.own_of([(0, 0, 0, 0, 2 * hidden_here)], [grad_pre], [feed_pieces], nt, features)
    grad_mid_norm, gain_two_grad = norm_back(middle, scale_two, gains[1], grad_second)
    grad_middle = dy_own + grad_mid_norm
    mix_rows = lay.rows_of((live_own * grad_middle).astype(bf))

    grad_heads = heads_backward(lay.tie(mix_rows, feed_sent[0]), out_pieces)
    out_own, out_terms, out_sent = lay.collect_ring(lambda r: outer_sum(heads_out, columns_of(mix_rows, r)), True)
    grad_proj_first, taps_first, params_first, gain_first = mixer_backward(
        0, heads, core, proj_first, decays, lay.tie(grad_heads, *out_terms), marks, seg_rows, taps[0], params,
        gain_row, states_first, inverses_first, None,
    )
    first_own, first_terms, first_sent = lay.collect_ring(
        lambda r: outer_sum(columns_of(first_rows, r), grad_proj_first[:, :width]), True
    )
    grad_proj_second, taps_second, params_second, gain_second = mixer_backward(
        pair, heads, core, proj_second, decays, lay.tie(grad_heads, feed_sent[1], *first_terms), marks, seg_rows,
        taps[1], params, gain_row, states_second, inverses_second, grad_proj_first,
    )
    second_own, second_terms, second_sent = lay.collect_ring(
        lambda r: outer_sum(columns_of(first_rows, r), grad_proj_second), False
    )
    grad_first = lay.own_of(
        [(0, 0, 0, 0, width), (1, 0, 1, 0, width), (1, width, 0, width, LANES)],
        [grad_proj_first, lay.tie(grad_proj_second, feed_sent[2], out_sent[0], *second_terms)],
        [in_first, in_second], nt, features,
    )
    grad_x_norm, gain_one_grad = norm_back(x_own, scale_one, gains[0], grad_first)
    grad_tokens = (grad_middle + grad_x_norm).astype(bf)

    def sent_out(own, *others):
        straight = times_back(own, turning).astype(bf)
        return exchange(lay.tie(outer_sum(landing, straight).astype(bf), *others))

    def sent_home(back, *others):
        return outer_sum(sending, lay.tie(back, *others)).astype(bf)

    branch_own = lay.own_of([(0, 0, 0, 0, hidden_here)], [lay.tie(hidden, feed_terms[0], grad_second)], [down_pieces], nn, features)
    output = sent_home(sent_out((middle + live_own * branch_own).astype(bf), out_sent[0]), first_sent[2])
    tokens_grad = sent_home(sent_out(grad_tokens), *second_sent[1:])

    conv_full = jnp.zeros(conv_weights.shape, f32)
    for cut, grad in zip(cuts, (taps_first, taps_second)):
        begin = 0
        for start, size in cut:
            conv_full = lax.dynamic_update_slice_in_dim(conv_full, grad[:, begin : begin + size], start, 1)
            begin += size
    params_grad = params_first + params_second
    log_full = lax.dynamic_update_slice_in_dim(jnp.zeros_like(a_log), params_grad[0, :heads], share * heads, 0)
    bias_full = lax.dynamic_update_slice_in_dim(jnp.zeros_like(dt_bias), params_grad[1, :heads], share * heads, 0)
    gain_grad = gain_first[0] + gain_second[0]
    norm_grads = jnp.stack([straight_gain(gain_one_grad), straight_gain(gain_two_grad)])
    sums = flat([conv_full, norm_grads, gain_grad, log_full, bias_full])
    sums = lay.everywhere(sums, second_sent[1:]).reshape(-1)
    ends = [conv_full.size]
    for size in (2 * features, DV, all_heads, all_heads):
        ends.append(ends[-1] + size)
    norm_grad = sums[ends[0] : ends[1]].reshape(2, features)

    end = second_sent[1:]
    down_grad = lay.collect_last(lay.collect_far(down_own, 1), 1, feed_sent[2])
    first_grad = lay.collect_last(lay.collect_far(first_own, 0), 0, *end)
    second_grad = lay.collect_last(lay.collect_far(second_own, 0), 0)
    feed_grad = lay.collect_last(lay.collect_far(feed_own, 0), 0, *end)
    out_grad = lay.collect_last(lay.collect_far(out_own, 1), 1, *end)
    down_grad, feed_grad, out_grad = [
        (mine, lay.tie(theirs, *end).astype(f32)) for mine, theirs in (down_grad, feed_grad, out_grad)
    ]
    first_grad, second_grad = [(mine, theirs.astype(f32)) for mine, theirs in (first_grad, second_grad)]
    in_grads = []
    begin = 0
    for size in (keys, keys, vals, vals):
        part = slice(begin, begin + size)
        in_grads.append(
            lay.joined(*[[grads[0][:, part], grads[1][:, part]] for grads in zip(first_grad, second_grad)], 1)
        )
        begin += size
    for size in (heads, heads):
        in_grads.append(lay.joined(*[[grad[:, begin : begin + size]] for grad in second_grad], 1))
        begin += size

    def alternate(grad, part):
        return grad.reshape(grad.shape[0], -1, 2, LANES)[:, :, part].reshape(grad.shape[0], -1)

    return (
        output,
        tokens_grad,
        norm_grad,
        *in_grads,
        sums[: ends[0]].reshape(conv_full.shape),
        sums[ends[2] : ends[3]],
        sums[ends[3] : ends[4]],
        sums[ends[1] : ends[2]],
        lay.ordered(*out_grad, 0),
        *[lay.ordered(*[alternate(grad, part) for grad in feed_grad], 1) for part in (0, 1)],
        lay.ordered(*down_grad, 0),
    )


def solution(mesh):
    return jax.shard_map(
        shards,
        mesh=mesh,
        in_specs=(
            P(("dp", "tensor"), None),
            P(("dp", "tensor"), None),
            P("dp", None),
            P(("dp", "tensor")),
            P(),
            P("dp", "tensor"),
            P("dp", "tensor"),
            P("dp", "tensor"),
            P("dp", "tensor"),
            P("dp", "tensor"),
            P("dp", "tensor"),
            P(),
            P(),
            P(),
            P(),
            P("tensor", "dp"),
            P("dp", "tensor"),
            P("dp", "tensor"),
            P("tensor", "dp"),
        ),
        out_specs=(
            P(("dp", "tensor"), None),
            P(("dp", "tensor"), None),
            P(),
            P("dp", "tensor"),
            P("dp", "tensor"),
            P("dp", "tensor"),
            P("dp", "tensor"),
            P("dp", "tensor"),
            P("dp", "tensor"),
            P(),
            P(),
            P(),
            P(),
            P("tensor", "dp"),
            P("dp", "tensor"),
            P("dp", "tensor"),
            P("tensor", "dp"),
        ),
        check_vma=False,
    )
```

```python
import functools

import jax
import jax.numpy as jnp
from jax import lax
from jax.experimental import pallas as pl
from jax.experimental.pallas import tpu as pltpu
from jax.sharding import PartitionSpec as P

bf = jnp.bfloat16
f32 = jnp.float32
DK = 128
DV = 256
CHUNK = 128
LANES = 128
GROUPS = 2
EPS_ROW = 1e-06
EPS_UNIT = 1e-06
EPS_HEAD = 1e-05
NEG = -1e30
VMEM_LIMIT = 56 * 2**20
COST = 1.0


def dot(left, right, left_dim, right_dim):
    return lax.dot_general(
        left.astype(bf), right.astype(bf), (((left_dim,), (right_dim,)), ((), ())), preferred_element_type=f32
    )


def nn(left, right):
    return dot(left, right, 1, 0)


def nt(left, right):
    return dot(left, right, 1, 1)


def tn(left, right):
    return dot(left, right, 0, 0)


def exact(left, right):
    return lax.dot_general(
        left, right, (((1,), (0,)), ((), ())), precision=lax.Precision.HIGHEST, preferred_element_type=f32
    )


def softplus(v):
    return jnp.maximum(v, 0.0) + jnp.log(1.0 + jnp.exp(-jnp.abs(v)))


def sigmoid(v):
    return 1.0 / (1.0 + jnp.exp(-v))


def unit_lower_inverses(systems, places, others):
    eye = (places == others).astype(f32)
    size = 2
    same = (places // size) == (others // size)
    power = [jnp.where(same, a, 0.0) for a in systems]
    inverse = [eye - a for a in power]
    span = 2
    while span < size:
        power = [nn(a, a) for a in power]
        inverse = [t + nn(t, a) for t, a in zip(inverse, power)]
        span *= 2
    while size < places.shape[0]:
        corner = ((places // (2 * size)) == (others // (2 * size))) & ((places // size) != (others // size))
        steps = [nn(jnp.where(corner, a, 0.0), t) for a, t in zip(systems, inverse)]
        inverse = [t - nn(t, s) for t, s in zip(inverse, steps)]
        size *= 2
    return inverse


def conv_channels(padded, group, taps, marks, columns):
    total = taps[0:1, columns] * padded[group, 8 : 8 + CHUNK, columns]
    for offset in range(1, 4):
        total = total + (taps[offset : offset + 1, columns] * marks[:, offset : offset + 1]) * (
            padded[group, 8 - offset : 8 - offset + CHUNK, columns]
        )
    return total


class Unit:
    def __init__(self, group, head, heads, first, lanes, shared):
        self.group = group
        self.head = head
        keys = heads * DK
        self.query_columns = slice(head * DK, head * DK + DK)
        self.key_columns = slice(keys + head * DK, keys + head * DK + DK)
        self.value_columns = slice(2 * keys + head * DV, 2 * keys + head * DV + DV)
        start = 2 * keys + heads * DV + head * DV
        self.gate_columns = slice(start, start + DV)
        self.out_columns = slice(head * DV, head * DV + DV)
        self.lane = first + head
        self.beta_lane = lanes + first + head
        cum, cum_rows, beta, causal, opening, closing = shared
        col = cum[:, self.lane : self.lane + 1]
        row = cum_rows[self.lane : self.lane + 1, :]
        self.decay = jnp.exp(jnp.where(causal, col - row, NEG))
        self.opened = jnp.exp(jnp.where(opening, col, NEG))
        last = cum[CHUNK - 1 : CHUNK, self.lane : self.lane + 1]
        self.closed = jnp.exp(jnp.where(closing, last - col, NEG))
        self.opened_last = self.opened[CHUNK - 1 : CHUNK, :]
        self.strength = beta[:, self.beta_lane : self.beta_lane + 1]


def chunk_units(heads, first, lanes, decays_ref, params, marks_ref, seg_ref, places, others):
    units, kept = [], []
    lower = (places >= others).astype(f32)
    for group in range(GROUPS):
        decays = decays_ref[0, group, 0]
        marks = marks_ref[group, 0]
        biased = decays + params[0:1, :]
        log_decay = -params[1:2, :] * softplus(biased)
        cum = exact(lower, log_decay)
        beta = sigmoid(decays)
        causal = (places >= others) & (marks[:, 0:1] == seg_ref[group, 0])
        shared = (cum, cum.T, beta, causal, marks[:, 4:5] > 0.0, marks[:, 5:6] > 0.0)
        kept.append((biased, log_decay, beta, marks))
        for head in range(heads):
            units.append(Unit(group, head, heads, first, lanes, shared))
    return units, kept


def forward_kernel(
    heads, first, lanes, core_ref, proj, decays, marks_ref, seg_ref, taps, params, gain, partner,
    out, kept_state, kept_inverse, state, padded,
):
    conv_width = heads * (2 * DK + DV)

    @pl.when(pl.program_id(0) == 0)
    def _():
        state[...] = jnp.zeros_like(state)
        padded[:, 0:8, :] = jnp.zeros((GROUPS, 8, conv_width), f32)

    for group in range(GROUPS):
        padded[group, 8:, :] = proj[0, group, 0, :, :conv_width].astype(f32)
    places = lax.broadcasted_iota(jnp.int32, (CHUNK, CHUNK), 0)
    others = lax.broadcasted_iota(jnp.int32, (CHUNK, CHUNK), 1)
    units, kept = chunk_units(heads, first, lanes, decays, params, marks_ref, seg_ref, places, others)
    strict = places > others
    queries, key_vecs, values = [], [], []
    for unit in units:
        marks = kept[unit.group][3]
        summed = conv_channels(padded, unit.group, taps, marks, unit.query_columns)
        act = summed * sigmoid(summed)
        scale = lax.rsqrt(jnp.sum(act * act, axis=1, keepdims=True) + EPS_UNIT)
        queries.append((act * (scale * DK**-0.5)).astype(bf))
        summed = conv_channels(padded, unit.group, taps, marks, unit.key_columns)
        act = summed * sigmoid(summed)
        scale = lax.rsqrt(jnp.sum(act * act, axis=1, keepdims=True) + EPS_UNIT)
        key_vecs.append((act * scale).astype(bf))
    pairs = [jnp.concatenate([q, k], axis=0) for q, k in zip(queries, key_vecs)]
    dots = [nt(pair, k) for pair, k in zip(pairs, key_vecs)]
    systems = [jnp.where(strict, unit.strength * unit.decay * d[CHUNK:], 0.0) for unit, d in zip(units, dots)]
    inverses = unit_lower_inverses(systems, places, others)
    for unit in units:
        summed = conv_channels(padded, unit.group, taps, kept[unit.group][3], unit.value_columns)
        values.append((summed * sigmoid(summed)).astype(bf).astype(f32))
    for group in range(GROUPS):
        padded[group, 0:8, :] = padded[group, CHUNK : CHUNK + 8, :]
    before = [state[number] for number in range(len(units))]
    for number in range(len(units)):
        kept_state[0, number] = before[number].astype(bf)
        kept_inverse[0, number] = inverses[number].astype(bf)
    reads = [nn(pair, s) for pair, s in zip(pairs, before)]
    rights = [unit.strength * (v - unit.opened * read[CHUNK:]) for unit, v, read in zip(units, values, reads)]
    news = [nn(t, r) for t, r in zip(inverses, rights)]
    mixed = [
        unit.opened * read[:CHUNK] + nn(d[:CHUNK] * unit.decay, new)
        for unit, read, d, new in zip(units, reads, dots, news)
    ]
    for number, unit in enumerate(units):
        state[number] = unit.opened_last * before[number] + tn(key_vecs[number], unit.closed * news[number])
    for unit, mix in zip(units, mixed):
        gate = proj[0, unit.group, 0, :, unit.gate_columns].astype(f32)
        scale = lax.rsqrt(jnp.mean(mix * mix, axis=1, keepdims=True) + EPS_HEAD)
        out[0, unit.group, 0, :, unit.out_columns] = (mix * scale * gain[...] * (gate * sigmoid(gate))).astype(bf)


def backward_kernel(
    heads, first, lanes, core_ref, proj, prev_rows, decays, grads, marks_ref, seg_ref, taps, params, gain,
    kept_state, kept_inverse, earlier, proj_grad, taps_grad, params_grad, gain_grad, state_grad, padded, summed_grad,
):
    conv_width = heads * (2 * DK + DV)
    width = conv_width + heads * DV

    @pl.when(pl.program_id(0) == 0)
    def _():
        taps_grad[...] = jnp.zeros_like(taps_grad)
        params_grad[...] = jnp.zeros_like(params_grad)
        gain_grad[...] = jnp.zeros_like(gain_grad)
        state_grad[...] = jnp.zeros_like(state_grad)
        summed_grad[:, CHUNK:, :] = jnp.zeros((GROUPS, 8, conv_width), f32)

    for group in range(GROUPS):
        padded[group, 0:8, :] = prev_rows[0, group, 0, :, :conv_width].astype(f32)[-8:]
        padded[group, 8:, :] = proj[0, group, 0, :, :conv_width].astype(f32)
    places = lax.broadcasted_iota(jnp.int32, (CHUNK, CHUNK), 0)
    others = lax.broadcasted_iota(jnp.int32, (CHUNK, CHUNK), 1)
    units, kept = chunk_units(heads, first, lanes, decays, params, marks_ref, seg_ref, places, others)
    strict = places > others
    q_sums, k_sums, v_sums, q_acts, k_acts, q_scale, k_scale = [], [], [], [], [], [], []
    queries, key_vecs, values = [], [], []
    for unit in units:
        marks = kept[unit.group][3]
        summed = conv_channels(padded, unit.group, taps, marks, unit.query_columns)
        act = summed * sigmoid(summed)
        scale = lax.rsqrt(jnp.sum(act * act, axis=1, keepdims=True) + EPS_UNIT)
        queries.append((act * (scale * DK**-0.5)).astype(bf))
        q_sums.append(summed)
        q_acts.append(act)
        q_scale.append(scale)
        summed = conv_channels(padded, unit.group, taps, marks, unit.key_columns)
        act = summed * sigmoid(summed)
        scale = lax.rsqrt(jnp.sum(act * act, axis=1, keepdims=True) + EPS_UNIT)
        key_vecs.append((act * scale).astype(bf))
        k_sums.append(summed)
        k_acts.append(act)
        k_scale.append(scale)
        summed = conv_channels(padded, unit.group, taps, marks, unit.value_columns)
        values.append((summed * sigmoid(summed)).astype(bf).astype(f32))
        v_sums.append(summed)
    count = len(units)
    pairs = [jnp.concatenate([q, k], axis=0) for q, k in zip(queries, key_vecs)]
    dots = [nt(pair, k) for pair, k in zip(pairs, key_vecs)]
    before = [kept_state[0, number] for number in range(count)]
    after_grad = [state_grad[number] for number in range(count)]
    inverses = [kept_inverse[0, number] for number in range(count)]
    reads = [nn(pair, s) for pair, s in zip(pairs, before)]
    gaps = [v - unit.opened * read[CHUNK:] for unit, v, read in zip(units, values, reads)]
    news = [nn(t, unit.strength * g) for t, unit, g in zip(inverses, units, gaps)]
    scores = [d[:CHUNK] * unit.decay for d, unit in zip(dots, units)]
    mixed = [unit.opened * read[:CHUNK] + nn(score, new) for unit, read, score, new in zip(units, reads, scores, news)]
    mix_grads = []
    gain_row = gain[...]
    gain_total = jnp.zeros((1, DV), f32)
    for unit, mix in zip(units, mixed):
        gate = proj[0, unit.group, 0, :, unit.gate_columns].astype(f32)
        grad = grads[0, unit.group, 0, :, unit.out_columns].astype(f32)
        scale = lax.rsqrt(jnp.mean(mix * mix, axis=1, keepdims=True) + EPS_HEAD)
        soft = sigmoid(gate)
        grad_normed = grad * (mix * scale)
        proj_grad[0, unit.group, 0, :, unit.gate_columns] = (
            grad_normed * gain_row * (soft * (1.0 + gate * (1.0 - soft)))
        ).astype(bf)
        silu = gate * soft
        gain_total = gain_total + jnp.sum(grad_normed * silu, axis=0, keepdims=True)
        inner = grad * silu * gain_row
        mix_grads.append(scale * inner - mix * (scale * scale * scale) * jnp.mean(inner * mix, axis=1, keepdims=True))
    gain_grad[0:1, :] += gain_total
    pushes = [nn(k, g) for k, g in zip(key_vecs, after_grad)]
    new_grads = [
        tn(score, grad) + unit.closed * push for score, grad, unit, push in zip(scores, mix_grads, units, pushes)
    ]
    score_grads = [nt(grad, new) for grad, new in zip(mix_grads, news)]
    right_grads = [tn(t, grad) for t, grad in zip(inverses, new_grads)]
    system_grads = [jnp.where(strict, -nt(grad, new), 0.0) for grad, new in zip(right_grads, news)]
    lane_ids = lax.broadcasted_iota(jnp.int32, (CHUNK, LANES), 1)
    rows_down = lax.broadcasted_iota(jnp.int32, (CHUNK, 1), 0)
    cum_grads = [jnp.zeros((CHUNK, LANES), f32) for _ in range(GROUPS)]
    beta_grads = [jnp.zeros((CHUNK, LANES), f32) for _ in range(GROUPS)]
    cross_rows = [[], []]
    raised = []
    for number, unit in enumerate(units):
        read_query = reads[number][:CHUNK]
        read_key = reads[number][CHUNK:]
        gram = dots[number][CHUNK:]
        decayed_score = score_grads[number] * unit.decay
        decayed_system = system_grads[number] * unit.decay
        system_gram = decayed_system * gram
        crossing = decayed_score * dots[number][:CHUNK] + unit.strength * system_gram
        value_grad = unit.strength * right_grads[number]
        beta_grad = jnp.sum(system_gram, axis=1, keepdims=True) + jnp.sum(
            right_grads[number] * gaps[number], axis=1, keepdims=True
        )
        open_grad = jnp.sum(mix_grads[number] * read_query - value_grad * read_key, axis=1, keepdims=True)
        close_grad = unit.closed * jnp.sum(news[number] * pushes[number], axis=1, keepdims=True)
        kept_dot = jnp.sum(
            jnp.sum(after_grad[number] * before[number].astype(f32), axis=1, keepdims=True), axis=0, keepdims=True
        )
        last_grad = jnp.sum(close_grad, axis=0, keepdims=True) + unit.opened_last * kept_dot
        col = jnp.sum(crossing, axis=1, keepdims=True) + unit.opened * open_grad - close_grad
        col = col + jnp.where(rows_down == CHUNK - 1, last_grad, 0.0)
        cross_rows[unit.group].append(jnp.sum(crossing, axis=0, keepdims=True))
        cum_grads[unit.group] = jnp.where(lane_ids == unit.lane, col, cum_grads[unit.group])
        beta_grads[unit.group] = jnp.where(lane_ids == unit.beta_lane, beta_grad, beta_grads[unit.group])
        raised.append((decayed_score.astype(bf), (unit.strength * decayed_system).astype(bf), value_grad))
    stacked = [
        jnp.concatenate([(unit.opened * grad).astype(bf), (-unit.opened * item[2]).astype(bf)], axis=0)
        for unit, item, grad in zip(units, raised, mix_grads)
    ]
    through = [nt(x, s) for x, s in zip(stacked, before)]
    grams = [jnp.concatenate([item[0], item[1]], axis=0) for item in raised]
    direct = [nn(g, k) for g, k in zip(grams, key_vecs)]
    turned = [tn(g, pair) for g, pair in zip(grams, pairs)]
    pushed = [nt(unit.closed * new, grad) for unit, new, grad in zip(units, news, after_grad)]
    for number, unit in enumerate(units):
        state_grad[number] = unit.opened_last * after_grad[number] + tn(pairs[number], stacked[number])
    for number, unit in enumerate(units):
        query_grad = (through[number][:CHUNK] + direct[number][:CHUNK]) * DK**-0.5
        key_grad = through[number][CHUNK:] + direct[number][CHUNK:] + turned[number] + pushed[number]
        for grad, act, scale, summed, columns in (
            (query_grad, q_acts[number], q_scale[number], q_sums[number], unit.query_columns),
            (key_grad, k_acts[number], k_scale[number], k_sums[number], unit.key_columns),
        ):
            inner = scale * (grad - act * (scale * scale) * jnp.sum(grad * act, axis=1, keepdims=True))
            soft = sigmoid(summed)
            summed_grad[unit.group, 0:CHUNK, columns] = inner * (soft * (1.0 + summed * (1.0 - soft)))
        summed = v_sums[number]
        soft = sigmoid(summed)
        summed_grad[unit.group, 0:CHUNK, unit.value_columns] = raised[number][2] * (
            soft * (1.0 + summed * (1.0 - soft))
        )
    for group in range(GROUPS):
        marks = kept[group][3]
        for start in range(0, conv_width, LANES):
            columns = slice(start, start + LANES)
            grad = summed_grad[group, 0:CHUNK, columns]
            total = taps[0:1, columns] * grad
            taps_grad[0:1, columns] += jnp.sum(grad * padded[group, 8 : 8 + CHUNK, columns], axis=0, keepdims=True)
            for offset in range(1, 4):
                later = summed_grad[group, offset : offset + CHUNK, columns]
                total = total + (taps[offset : offset + 1, columns] * marks[:, 5 + offset : 6 + offset]) * later
                taps_grad[offset : offset + 1, columns] += jnp.sum(
                    (grad * marks[:, offset : offset + 1]) * padded[group, 8 - offset : 8 - offset + CHUNK, columns],
                    axis=0, keepdims=True,
                )
            proj_grad[0, group, 0, :, columns] = total.astype(bf)
        summed_grad[group, CHUNK:, :] = summed_grad[group, 0:8, :]
    upper = (places <= others).astype(f32)
    for group in range(GROUPS):
        biased, log_decay, beta, _ = kept[group]
        blank = [jnp.zeros((first, CHUNK), f32)] if first else []
        rest = [jnp.zeros((CHUNK - heads - first, CHUNK), f32)]
        cross = jnp.concatenate(blank + cross_rows[group] + rest, axis=0).T
        log_grad = exact(upper, cum_grads[group] - cross)
        decay_grad = log_grad * (-params[1:2, :]) * sigmoid(biased)
        both = decay_grad + beta_grads[group] * beta * (1.0 - beta)
        if earlier is not None:
            both = both + earlier[0, group, 0].astype(f32)
        proj_grad[0, group, 0, :, width:] = both.astype(bf)
        params_grad[0:1, :] += jnp.sum(log_grad * log_decay, axis=0, keepdims=True)
        params_grad[1:2, :] += jnp.sum(decay_grad, axis=0, keepdims=True)


def folded(rows):
    return rows.reshape(2, GROUPS, -1, CHUNK, rows.shape[1])


def mixer_forward(first, lanes, core, proj, decays, marks, seg_rows, taps, params, gain, partner):
    conv_width = taps.shape[1]
    heads = conv_width // (2 * DK + DV)
    proj, decays = folded(proj), folded(decays)
    per_core = proj.shape[2]
    chunks = 2 * per_core
    units = GROUPS * heads

    def at(c, core_ref):
        return ((c // per_core) ^ core_ref[0], 0, c % per_core, 0, 0)

    fixed = lambda c, core_ref: (0, 0)
    here = lambda c, core_ref: (0, c, 0, 0)
    kept = lambda c, core_ref: (c, 0, 0, 0)
    full = proj.shape[:4] + (lanes * DV,)
    body = functools.partial(forward_kernel, heads, first, lanes)
    more_specs, more, aliases = [], [], {}
    if partner is None:
        inner = body

        def body(*refs):
            return inner(*refs[:8], None, *refs[8:])

    else:
        more_specs, more, aliases = [pl.BlockSpec(memory_space=pl.ANY)], [partner.reshape(full)], {8: 0}

    def out_at(c, core_ref):
        return at(c, core_ref)[:4] + (first // heads,)

    out, states, inverses = pl.pallas_call(
        body,
        grid_spec=pltpu.PrefetchScalarGridSpec(
            num_scalar_prefetch=1,
            grid=(chunks,),
            in_specs=[
                pl.BlockSpec((1, GROUPS, 1, CHUNK, proj.shape[4]), at),
                pl.BlockSpec((1, GROUPS, 1, CHUNK, LANES), at),
                pl.BlockSpec((GROUPS, 1, CHUNK, LANES), here),
                pl.BlockSpec((GROUPS, 1, 1, CHUNK), here),
                pl.BlockSpec((4, conv_width), fixed),
                pl.BlockSpec((8, LANES), fixed),
                pl.BlockSpec((1, DV), fixed),
            ]
            + more_specs,
            out_specs=[
                pl.BlockSpec((1, GROUPS, 1, CHUNK, heads * DV), out_at),
                pl.BlockSpec((1, units, DK, DV), kept),
                pl.BlockSpec((1, units, CHUNK, CHUNK), kept),
            ],
            scratch_shapes=[pltpu.VMEM((units, DK, DV), f32), pltpu.VMEM((GROUPS, CHUNK + 8, conv_width), f32)],
        ),
        out_shape=[
            jax.ShapeDtypeStruct(full, bf),
            jax.ShapeDtypeStruct((chunks, units, DK, DV), bf),
            jax.ShapeDtypeStruct((chunks, units, CHUNK, CHUNK), bf),
        ],
        compiler_params=pltpu.CompilerParams(vmem_limit_bytes=VMEM_LIMIT),
        cost_estimate=pl.CostEstimate(flops=int(COST * 16 * 10**9), bytes_accessed=int(COST * 16 * 2**20), transcendentals=0),
        input_output_aliases=aliases,
        name="mixer_forward",
    )(core, proj, decays, marks, seg_rows, taps, params, gain, *more)
    return out.reshape(-1, lanes * DV), states, inverses


def mixer_backward(first, lanes, core, proj, decays, grads, marks, seg_rows, taps, params, gain, states, inverses, earlier):
    conv_width = taps.shape[1]
    heads = conv_width // (2 * DK + DV)
    proj, decays, grads = folded(proj), folded(decays), folded(grads)
    per_core = proj.shape[2]
    chunks = 2 * per_core
    units = GROUPS * heads
    width = conv_width + heads * DV + LANES
    tail = 16

    def at(step, core_ref):
        c = chunks - 1 - step
        return ((c // per_core) ^ core_ref[0], 0, c % per_core, 0, 0)

    def prev(step, core_ref):
        c = jnp.maximum(chunks - 2 - step, 0)
        return ((c // per_core) ^ core_ref[0], 0, c % per_core, CHUNK // tail - 1, 0)

    def grad_at(step, core_ref):
        return at(step, core_ref)[:4] + (first // heads,)

    def last_lanes(step, core_ref):
        return at(step, core_ref)[:4] + ((conv_width + heads * DV) // LANES,)

    fixed = lambda step, core_ref: (0, 0)
    here = lambda step, core_ref: (0, chunks - 1 - step, 0, 0)
    kept = lambda step, core_ref: (chunks - 1 - step, 0, 0, 0)
    in_specs = [
        pl.BlockSpec((1, GROUPS, 1, CHUNK, proj.shape[4]), at),
        pl.BlockSpec((1, GROUPS, 1, tail, proj.shape[4]), prev),
        pl.BlockSpec((1, GROUPS, 1, CHUNK, LANES), at),
        pl.BlockSpec((1, GROUPS, 1, CHUNK, heads * DV), grad_at),
        pl.BlockSpec((GROUPS, 1, CHUNK, LANES), here),
        pl.BlockSpec((GROUPS, 1, 1, CHUNK), here),
        pl.BlockSpec((4, conv_width), fixed),
        pl.BlockSpec((8, LANES), fixed),
        pl.BlockSpec((1, DV), fixed),
        pl.BlockSpec((1, units, DK, DV), kept),
        pl.BlockSpec((1, units, CHUNK, CHUNK), kept),
    ]
    inputs = [core, proj, proj, decays, grads, marks, seg_rows, taps, params, gain, states, inverses]
    body = functools.partial(backward_kernel, heads, first, lanes)
    if earlier is not None:
        in_specs.append(pl.BlockSpec((1, GROUPS, 1, CHUNK, LANES), last_lanes))
        inputs.append(folded(earlier))
    else:
        whole = body

        def body(*refs):
            return whole(*refs[:12], None, *refs[12:])

    out, taps_grad, params_grad, gain_grad = pl.pallas_call(
        body,
        grid_spec=pltpu.PrefetchScalarGridSpec(
            num_scalar_prefetch=1,
            grid=(chunks,),
            in_specs=in_specs,
            out_specs=[
                pl.BlockSpec((1, GROUPS, 1, CHUNK, width), at),
                pl.BlockSpec((4, conv_width), fixed),
                pl.BlockSpec((8, LANES), fixed),
                pl.BlockSpec((8, DV), fixed),
            ],
            scratch_shapes=[
                pltpu.VMEM((units, DK, DV), f32),
                pltpu.VMEM((GROUPS, CHUNK + 8, conv_width), f32),
                pltpu.VMEM((GROUPS, CHUNK + 8, conv_width), f32),
            ],
        ),
        out_shape=[
            jax.ShapeDtypeStruct(proj.shape[:4] + (width,), bf),
            jax.ShapeDtypeStruct((4, conv_width), f32),
            jax.ShapeDtypeStruct((8, LANES), f32),
            jax.ShapeDtypeStruct((8, DV), f32),
        ],
        compiler_params=pltpu.CompilerParams(vmem_limit_bytes=VMEM_LIMIT),
        cost_estimate=pl.CostEstimate(flops=int(COST * 30 * 10**9), bytes_accessed=int(COST * 30 * 2**20), transcendentals=0),
        name="mixer_backward",
    )(*inputs)
    return out.reshape(-1, width), taps_grad, params_grad, gain_grad


def group_marks(lengths, group_rows):
    groups, count = lengths.shape
    position = jnp.arange(group_rows, dtype=jnp.int32)[None, :]
    segment = jnp.zeros((groups, group_rows), jnp.int32)
    end = jnp.zeros((groups, 1), jnp.int32)
    for number in range(count):
        segment = segment + (position >= end).astype(jnp.int32)
        end = end + lengths[:, number : number + 1]
    live = (position < end).astype(f32)
    padded = jnp.pad(segment, ((0, 0), (CHUNK, CHUNK)))
    later = lambda offset: padded[:, CHUNK + offset : CHUNK + offset + group_rows]
    chunked = segment.reshape(groups, group_rows // CHUNK, CHUNK)
    before = padded[:, CHUNK - 1 : CHUNK - 1 + group_rows].reshape(chunked.shape)[:, :, :1]
    columns = [segment]
    columns += [later(-offset) == segment for offset in (1, 2, 3)]
    columns += [(chunked == before).reshape(segment.shape), (chunked == chunked[:, :, -1:]).reshape(segment.shape)]
    columns += [later(offset) == segment for offset in (1, 2, 3)]
    lane = jnp.arange(LANES, dtype=jnp.int32)
    marks = jnp.zeros((groups, group_rows, LANES), f32)
    for number, column in enumerate(columns):
        marks = jnp.where(lane == number, column.astype(f32)[:, :, None], marks)
    marks = marks.reshape(groups, group_rows // CHUNK, CHUNK, LANES)
    seg_rows = segment.astype(f32).reshape(groups, group_rows // CHUNK, 1, CHUNK)
    return marks, seg_rows, live


def pick_kernel(pairs, turn_ref, *refs):
    count = len(refs) - len(pairs)
    for out, parts in zip(refs[count:], pairs):
        begin = 0
        for number, start, stop in parts:
            out[:, begin : begin + stop - start] = refs[number][:, start:stop]
            begin += stop - start


def picked(turn, weights, axes, joins):
    in_specs, inputs, shapes = [], [], []
    for weight, axis in zip(weights, axes):
        rows, columns = weight.shape
        if axis is None:
            in_specs += [pl.BlockSpec((rows, columns), lambda i, t: (0, 0))] * 2
            shapes.append((rows, columns))
        elif axis == 1:
            in_specs += [
                pl.BlockSpec((rows, columns // 2), lambda i, t: (0, t[0])),
                pl.BlockSpec((rows, columns // 2), lambda i, t: (0, 1 - t[0])),
            ]
            shapes.append((rows, columns // 2))
        else:
            in_specs += [
                pl.BlockSpec((rows // 2, columns), lambda i, t: (t[0], 0)),
                pl.BlockSpec((rows // 2, columns), lambda i, t: (1 - t[0], 0)),
            ]
            shapes.append((rows // 2, columns))
        inputs += [weight, weight]
    pairs, out_shapes = [], []
    for join in joins:
        width = sum(stop - start for _, start, stop in join)
        for given in (0, 1):
            pairs.append([(2 * number + given, start, stop) for number, start, stop in join])
            out_shapes.append((shapes[join[0][0]][0], width))
    outs = pl.pallas_call(
        functools.partial(pick_kernel, pairs),
        grid_spec=pltpu.PrefetchScalarGridSpec(
            num_scalar_prefetch=1,
            grid=(1,),
            in_specs=in_specs,
            out_specs=[pl.BlockSpec(shape, lambda i, t: (0, 0)) for shape in out_shapes],
        ),
        out_shape=[jax.ShapeDtypeStruct(shape, bf) for shape in out_shapes],
        compiler_params=pltpu.CompilerParams(vmem_limit_bytes=VMEM_LIMIT),
        cost_estimate=pl.CostEstimate(flops=0, bytes_accessed=8 * 2**20, transcendentals=0),
        name="picked",
    )(turn, *inputs)
    return [(outs[2 * number], outs[2 * number + 1]) for number in range(len(joins))]


TILE = 256
STRIP = 256


def call(body, grid, in_specs, out_specs, out_shape, flops, moved, name, inputs, scratch=()):
    return pl.pallas_call(
        body,
        grid=grid,
        scratch_shapes=scratch,
        in_specs=in_specs,
        out_specs=out_specs,
        out_shape=out_shape,
        compiler_params=pltpu.CompilerParams(vmem_limit_bytes=VMEM_LIMIT),
        cost_estimate=pl.CostEstimate(flops=int(flops * COST), bytes_accessed=int(moved * COST), transcendentals=0),
        name=name,
    )(*inputs)


def strip_sum(rows, pieces, start, product):
    total = None
    begin = 0
    depth = rows.shape[1] // len(pieces)
    for piece in pieces:
        part = product(rows[start : start + STRIP, begin : begin + depth], piece[...])
        total = part if total is None else total + part
        begin += depth
    return total


def whole(array):
    return pl.BlockSpec(array.shape, lambda i: (0,) * array.ndim)


def project(rows, pieces, width, extra):
    count = rows.shape[0]
    depth = pieces[0].shape[0]
    steps = width // TILE
    used = len(pieces)

    def body(rows_ref, *refs):
        weights = refs[:used]
        out = refs[2 * used if extra else used]
        for start in range(0, count, STRIP):
            out[start : start + STRIP, :] = strip_sum(rows_ref, weights, start, nn).astype(bf)
        if extra:

            @pl.when(pl.program_id(0) == 0)
            def _():
                for start in range(0, count, STRIP):
                    refs[-1][start : start + STRIP, :] = strip_sum(rows_ref, refs[used : 2 * used], start, nn)

    in_specs = [whole(rows)] + [pl.BlockSpec((depth, TILE), lambda i: (0, i))] * used
    out_specs = [pl.BlockSpec((count, TILE), lambda i: (0, i))]
    out_shape = [jax.ShapeDtypeStruct((count, width), bf)]
    inputs = [rows, *pieces]
    if extra:
        in_specs += [pl.BlockSpec((depth, LANES), lambda i: (0, width // LANES))] * used
        out_specs.append(pl.BlockSpec((count, LANES), lambda i: (0, 0)))
        out_shape.append(jax.ShapeDtypeStruct((count, LANES), f32))
        inputs += pieces
    flops = 2 * count * depth * used * width
    moved = 2 * (count * depth * used + depth * used * width + count * width)
    return call(body, (steps,), in_specs, out_specs, out_shape, flops, moved, "project", inputs)


def feed_forward(rows, pieces):
    count = rows.shape[0]
    depth, width = pieces[0].shape
    used = len(pieces)

    def body(rows_ref, *refs):
        pre_out, hidden_out = refs[used:]
        for start in range(0, count, STRIP):
            strip = slice(start, start + STRIP)
            both = strip_sum(rows_ref, refs[:used], start, nn)
            gate = both[:, :LANES]
            pre_out[strip, :] = both.astype(bf)
            hidden_out[strip, :] = (gate * sigmoid(gate) * both[:, LANES:]).astype(bf)

    return call(
        body,
        (width // (2 * LANES),),
        [whole(rows)] + [pl.BlockSpec((depth, 2 * LANES), lambda i: (0, i))] * used,
        [pl.BlockSpec((count, 2 * LANES), lambda i: (0, i)), pl.BlockSpec((count, LANES), lambda i: (0, i))],
        [jax.ShapeDtypeStruct((count, width), bf), jax.ShapeDtypeStruct((count, width // 2), bf)],
        2 * count * depth * used * width,
        2 * (count * depth * used + depth * used * width + 2 * count * width),
        "feed_forward",
        [rows, *pieces],
    )


def feed_backward(rows, down_pieces, pre):
    count = rows.shape[0]
    width, depth = down_pieces[0].shape
    used = len(down_pieces)

    def body(rows_ref, *refs):
        pre_ref, out = refs[used:]
        for begin in range(0, width, TILE):
            size = min(TILE, width - begin)
            total = None
            for number in range(used):
                part = nt(rows_ref[:, number * depth : number * depth + depth], refs[number][begin : begin + size, :])
                total = part if total is None else total + part
            for shift in range(0, size, LANES):
                grad = total[:, shift : shift + LANES]
                at = 2 * (begin + shift)
                gate = pre_ref[:, at : at + LANES].astype(f32)
                up = pre_ref[:, at + LANES : at + 2 * LANES].astype(f32)
                soft = sigmoid(gate)
                out[:, at : at + LANES] = (grad * up * soft * (1.0 + gate * (1.0 - soft))).astype(bf)
                out[:, at + LANES : at + 2 * LANES] = (grad * gate * soft).astype(bf)

    strip = pl.BlockSpec((STRIP, 2 * width), lambda i: (i, 0))
    return call(
        body,
        (count // STRIP,),
        [pl.BlockSpec((STRIP, depth * used), lambda i: (i, 0))] + [whole(piece) for piece in down_pieces] + [strip],
        strip,
        jax.ShapeDtypeStruct((count, 2 * width), bf),
        2 * count * depth * used * width,
        2 * (count * depth * used + depth * used * width + 4 * count * width),
        "feed_backward",
        [rows, *down_pieces, pre],
    )


def heads_backward(rows, out_pieces):
    count = rows.shape[0]
    width, depth = out_pieces[0].shape
    used = len(out_pieces)

    def body(rows_ref, *refs):
        for start in range(0, count, STRIP):
            refs[used][start : start + STRIP, :] = strip_sum(rows_ref, refs[:used], start, nt).astype(bf)

    return call(
        body,
        (width // TILE,),
        [whole(rows)] + [pl.BlockSpec((TILE, depth), lambda i: (i, 0))] * used,
        pl.BlockSpec((count, TILE), lambda i: (0, i)),
        jax.ShapeDtypeStruct((count, width), bf),
        2 * count * depth * used * width,
        2 * (count * depth * used + depth * used * width + count * width),
        "heads_backward",
        [rows, *out_pieces],
    )


def wide(terms, lefts, pieces, product, features, got):
    count = lefts[0].shape[0]
    half, per = count // 2, count // 4
    depth = features // 4
    given = got is None
    used = len(pieces)
    inputs = list(lefts) + [piece for group in pieces for piece in group]
    in_specs = [pl.BlockSpec((half, left.shape[1]), (lambda i: (1, 0)) if given else (lambda i: (0, 0))) for left in lefts]
    in_specs += [pl.BlockSpec(memory_space=pl.ANY)] * (4 * used)
    flops = 2 * half * features * sum(term[4] for term in terms)
    moved = 2 * sum(piece.size for group in pieces for piece in group) + 6 * count * features
    skip = len(lefts) + 4 * used

    def body(*refs):
        held, sems = refs[-1 - used : -1], refs[-1]

        def copy(number, piece):
            source = refs[len(lefts) + 4 * number + piece]
            return pltpu.make_async_copy(source, held[number].at[piece], sems.at[number, piece])

        for piece in range(4):
            for number in range(used):
                copy(number, piece).start()
        for piece in range(4):
            columns = slice(piece * depth, piece * depth + depth)
            for number in range(used):
                copy(number, piece).wait()
            for strip in range(2):
                rows = slice(strip * per, strip * per + per)
                total = None
                for number, begin, weight, first, size in terms:
                    left = refs[number][rows, begin : begin + size]
                    right = held[weight][piece]
                    right = right[:, first : first + size] if product is nt else right
                    part = product(left, right)
                    total = part if total is None else total + part
                if given:
                    refs[skip][rows, columns] = total.astype(bf)
                else:
                    total = total + refs[skip][rows, columns].astype(f32)
                    if strip == 0:
                        refs[skip + 2][:, columns] = total
                    else:
                        refs[skip + 1][:, columns] = total.astype(bf)

    scratch = [pltpu.VMEM((4,) + group[0].shape, bf) for group in pieces] + [pltpu.SemaphoreType.DMA((used, 4))]
    if given:
        out_specs = pl.BlockSpec((half, features), lambda i: (0, 0))
        out_shape = jax.ShapeDtypeStruct((half, features), bf)
    else:
        in_specs.append(pl.BlockSpec((half, features), lambda i: (0, 0)))
        inputs.append(got)
        out_specs = [pl.BlockSpec((per, features), lambda i: (0, 0))] * 2
        out_shape = [jax.ShapeDtypeStruct((per, features), bf), jax.ShapeDtypeStruct((per, features), f32)]
    return call(
        body, (1,), in_specs, out_specs, out_shape, flops, moved, "wide_given" if given else "wide_kept", inputs, scratch
    )


RING = (0, 1, 3, 2)


def matmul(left, right):
    return jnp.dot(left, right, preferred_element_type=f32)


def outer_sum(left, right):
    return lax.dot_general(left, right, (((0,), (0,)), ((), ())), preferred_element_type=f32)


def times_back(left, right):
    return lax.dot_general(left, right, (((1,), (1,)), ((), ())), preferred_element_type=f32)


def norm_back(inputs, scale, gain, grad_out):
    scaled = grad_out * gain
    grad_in = scale * scaled - inputs * scale**3 * jnp.mean(scaled * inputs, axis=1, keepdims=True)
    return (grad_in, jnp.sum(grad_out * inputs * scale, axis=0))


class Layout:
    def __init__(self):
        self.ways = lax.axis_size("dp")
        self.spans = self.ways // 8
        dp = lax.axis_index("dp")
        self.core = lax.axis_index("tensor")
        self.turn = (dp // 4) % 2
        self.far = dp // 8
        near = dp % 4
        self.spot = near ^ (near >> 1)
        self.queues = {}

    def queued(self, values, queue, depth):
        line = self.queues.setdefault(queue, [])
        if len(line) >= depth:
            values, _ = lax.optimization_barrier((values, line[-depth]))
        return values, line

    def ring(self, values, step):
        pairs = []
        for number in range(self.ways):
            near = number % 4
            pairs.append((number, number - near + RING[((near ^ (near >> 1)) + step) % 4]))
        values, line = self.queued(values, step, DEPTH)
        line.append(lax.ppermute(values, "dp", pairs))
        return line[-1]

    def flip(self, values, bit):
        return lax.ppermute(values, "dp", [(n, n ^ bit) for n in range(self.ways)])

    def turned(self, values):
        return self.flip(values, 4)

    def crossed(self, values):
        return lax.ppermute(values, "tensor", [(0, 1), (1, 0)])

    def far_bits(self):
        bit = 8
        while bit < self.ways:
            yield bit
            bit *= 2

    def sources(self):
        places = jnp.arange(self.ways, dtype=jnp.int32)
        step = places // (2 * self.spans)
        jump = (places // 2) % self.spans
        spot = (self.spot + step) % 4
        return ((self.far ^ jump) * 2 + places % 2) * 4 + (spot ^ (spot >> 1))

    def ordered(self, first, second, axis):
        return jnp.where(
            self.turn == 0, jnp.concatenate([first, second], axis=axis), jnp.concatenate([second, first], axis=axis)
        )

    def tie(self, values, *others):
        return lax.optimization_barrier((values, *others))[0]

    def spread_far(self, chunk, axis, *others):
        for bit in self.far_bits():
            sent, line = self.queued(chunk, "far", DEPTH)
            line.append(self.flip(sent, bit))
            line[-1] = self.tie(line[-1], *others)
            chunk = jnp.concatenate([chunk, line[-1]], axis=axis)
        return chunk

    def spread_ring(self, chunk, upward):
        ahead = self.ring(chunk, -1)
        behind = self.ring(chunk, 1)
        across = self.ring(behind, 1) if upward else self.ring(ahead, -1)
        return [chunk, ahead, across, behind]

    def collect_ring(self, make, upward):
        across = make(2).astype(bf)
        if upward:
            behind = make(3).astype(bf)
            up = self.ring(across, 1)
            down = self.ring(behind, -1)
            last = self.ring((make(1) + up).astype(bf), 1)
            return make(0) + last + down, (across, behind), (up, down, last)
        ahead = make(1).astype(bf)
        down = self.ring(across, -1)
        up = self.ring(ahead, 1)
        last = self.ring((make(3) + down).astype(bf), -1)
        return make(0) + up + last, (across, ahead), (down, up, last)

    def collect_far(self, own, axis):
        for bit in reversed(list(self.far_bits())):
            half = own.shape[axis] // 2
            sent = lax.slice_in_dim(own, half, 2 * half, axis=axis)
            own = lax.slice_in_dim(own, 0, half, axis=axis), self.flip(sent.astype(bf), bit)
            if bit > 8:
                own = own[0] + own[1]
        return own

    def collect_last(self, own, axis, *others):
        if isinstance(own, tuple):
            own = own[0] + self.tie(own[1], *others)
        half = own.shape[axis] // 2
        mine = lax.dynamic_slice_in_dim(own, self.turn * half, half, axis)
        other = lax.dynamic_slice_in_dim(own, (1 - self.turn) * half, half, axis)
        return mine, self.turned(other.astype(bf))

    def joined(self, mine, theirs, axis):
        return self.ordered(jnp.concatenate(mine, axis=axis), jnp.concatenate(theirs, axis=axis), axis)

    def rows_of(self, own):
        across = self.crossed(own)
        there = self.turned(own)
        return jnp.concatenate([own, there, across, self.crossed(there)], axis=0)

    def own_of(self, terms, lefts, pieces, product, features):
        given = wide(terms, lefts, pieces, product, features, None)
        there, own = wide(terms, lefts, pieces, product, features, self.crossed(given))
        return own + self.turned(there)

    def everywhere(self, values, marks):
        bits = []
        bit = 1
        while bit < self.ways:
            bits.append(bit)
            bit *= 2
        for bit in reversed(bits):
            values = values + self.tie(self.flip(values, bit), *marks)
        return values + self.crossed(values)


DEPTH = 1


def flat(parts):
    joined = jnp.concatenate([part.reshape(-1) for part in parts])
    return jnp.pad(joined, (0, -joined.shape[0] % (8 * LANES))).reshape(-1, LANES)


def shards(
    tokens, cotangent, lengths, slot_of, norm_gains, w_query, w_key, w_value, w_gate, w_decay, w_beta,
    conv_weights, a_log, dt_bias, out_gain, w_out, w_mlp_gate, w_mlp_up, w_mlp_down,
):
    lay = Layout()
    row_count, features = tokens.shape
    tensor_ways = lax.axis_size("tensor")
    device_count = lay.ways * tensor_ways
    group_rows = row_count * tensor_ways
    capacity = row_count // device_count + 2
    bulk_rows = device_count * capacity
    all_heads = a_log.shape[0]
    heads = all_heads // (2 * tensor_ways)
    pair = heads // 2
    all_keys = all_heads * DK
    keys, vals = pair * DK, pair * DV
    width = 2 * keys + 2 * vals
    share = lay.core * 2 + lay.turn
    turn = lay.turn.reshape(1)
    core = lay.core.reshape(1)

    target = slot_of // row_count
    within = slot_of % row_count
    hits = target[:, None] == jnp.arange(device_count, dtype=jnp.int32)[None, :]
    places = jnp.arange(row_count, dtype=jnp.int32)
    earlier = (places[:, None] >= places[None, :]).astype(bf)
    rank = jnp.sum(matmul(earlier, hits.astype(bf)) * hits.astype(f32), axis=1).astype(jnp.int32) - 1
    outgoing = target * capacity + rank
    sending = (jnp.arange(bulk_rows, dtype=jnp.int32)[:, None] == outgoing[None, :]).astype(bf)
    slot_mark = jnp.broadcast_to((within + 1).astype(bf)[:, None], (row_count, LANES))
    send_tokens = matmul(sending, jnp.concatenate([tokens, slot_mark], axis=1)).astype(bf)
    send_cot = matmul(sending, cotangent).astype(bf)

    def exchange(values):
        return lax.all_to_all(values, ("dp", "tensor"), split_axis=0, concat_axis=0, tiled=True)


    def half_heads(weight):
        kept = jnp.where(lay.turn == 0, weight[:, :heads], weight[:, heads:])
        given = jnp.where(lay.turn == 0, weight[:, heads:], weight[:, :heads])
        return kept, given

    decay_halves, beta_halves = half_heads(w_decay), half_heads(w_beta)
    lanes_of = [
        jnp.pad(jnp.concatenate([d, b], axis=1), ((0, 0), (0, LANES - 2 * heads)))
        for d, b in zip(decay_halves, beta_halves)
    ]
    first_join = [(0, 0, keys), (1, 0, keys), (2, 0, vals), (3, 0, vals)]
    second_join = [(0, keys, 2 * keys), (1, keys, 2 * keys), (2, vals, 2 * vals), (3, vals, 2 * vals)]
    out_rows, hidden_here = w_out.shape[0] // 2, w_mlp_gate.shape[1] // 2
    block = features // lay.ways
    mixed_join = []
    for start in range(0, hidden_here, LANES):
        mixed_join += [(0, start, start + LANES), (1, start, start + LANES)]
    blob_first, (second_keep, second_give) = picked(
        turn, [w_query, w_key, w_value, w_gate], [1] * 4, [first_join, second_join]
    )
    first_keep, first_give = [
        jnp.concatenate([blob, extra], axis=1) for blob, extra in zip(blob_first, lanes_of)
    ]
    first_got = lay.turned(first_give)
    got_tokens = exchange(lay.tie(send_tokens, first_got))
    first_chunk = lay.spread_far(lay.ordered(first_keep, first_got, 0), 0)
    second_got = lay.turned(lay.tie(second_give, first_chunk))
    [(feed_keep, feed_give)] = picked(turn, [w_mlp_gate, w_mlp_up], [1, 1], [mixed_join])

    def half_rows(weight):
        half = weight.shape[0] // 2
        return [lax.dynamic_slice_in_dim(weight, place * half, half, 0) for place in (lay.turn, 1 - lay.turn)]

    out_keep, out_give = half_rows(w_out)
    down_keep, down_give = half_rows(w_mlp_down)
    tall_got = lay.turned(lay.tie(jnp.concatenate([out_give, down_give], axis=0), second_got))
    feed_got = lay.turned(lay.tie(feed_give, second_got))
    second_chunk = lay.spread_far(lay.ordered(second_keep, second_got, 0), 0)
    in_first = lay.spread_ring(first_chunk, True)
    tall_got = lay.tie(tall_got, in_first[1], in_first[3])
    out_chunk = lay.spread_far(lay.ordered(out_keep, tall_got[:out_rows], 1), 1)
    in_second = lay.spread_ring(second_chunk, False)
    out_pieces = lay.spread_ring(out_chunk, True)

    got_slot = got_tokens[:, features].astype(jnp.int32)
    landing = (places[:, None] + 1 == got_slot[None, :]).astype(bf)
    sources = lay.sources()
    feature = jnp.arange(features, dtype=jnp.int32)
    origin = (sources[:, None] * block + jnp.arange(block, dtype=jnp.int32)[None, :]).reshape(1, -1)
    turning = (feature[:, None] == origin).astype(bf)
    numbers = jnp.arange(lay.ways, dtype=jnp.int32)
    picking = (sources[:, None] == numbers[None, :]).astype(f32)

    def reordered_gain(gain):
        return jnp.sum(picking[:, :, None] * gain.reshape(1, lay.ways, block), axis=1).reshape(features)

    def straight_gain(grad):
        return jnp.sum(picking[:, :, None] * grad.reshape(lay.ways, 1, block), axis=0).reshape(features)

    gains = (reordered_gain(norm_gains[0]), reordered_gain(norm_gains[1]))
    x_own = matmul(matmul(landing, got_tokens[:, :features]).astype(bf), turning)

    pair_lengths = jnp.concatenate([lengths, lay.turned(lengths)], axis=0)
    marks, seg_rows, live = group_marks(pair_lengths, group_rows)
    live_own = lax.dynamic_slice_in_dim(live[0], lay.core * row_count, row_count)[:, None]
    starts = [(share * heads + first) * DK for first in (0, pair)]
    cuts = [
        [(start, keys), (all_keys + start, keys), (2 * all_keys + 2 * start, vals)] for start in starts
    ]
    taps = [
        jnp.concatenate([lax.dynamic_slice_in_dim(conv_weights, start, size, 1) for start, size in cut], axis=1)
        for cut in cuts
    ]
    log_here = lax.dynamic_slice_in_dim(a_log, share * heads, heads)
    bias_here = lax.dynamic_slice_in_dim(dt_bias, share * heads, heads)
    params = jnp.pad(jnp.stack([bias_here, jnp.exp(log_here)]), ((0, 6), (0, LANES - heads)))
    gain_row = out_gain[None, :]

    scale_one = lax.rsqrt(jnp.mean(x_own * x_own, axis=1, keepdims=True) + EPS_ROW)
    first_rows = lay.rows_of((x_own * scale_one * gains[0]).astype(bf))
    proj_first, decays = project(first_rows, in_first, width, True)
    feed_chunk = lay.spread_far(lay.ordered(feed_keep, lay.tie(feed_got, first_rows), 0), 0, proj_first)
    heads_out, states_first, inverses_first = mixer_forward(
        0, heads, core, proj_first, decays, marks, seg_rows, taps[0], params, gain_row, None
    )
    proj_second = project(first_rows, in_second, width, False)[0]
    heads_out, states_second, inverses_second = mixer_forward(
        pair, heads, core, proj_second, decays, marks, seg_rows, taps[1], params, gain_row, heads_out
    )
    mixed_own = lay.own_of([(0, 0, 0, 0, out_rows)], [lay.tie(heads_out, feed_chunk)], [out_pieces], nn, features)
    middle = x_own + live_own * mixed_own

    got_cot = exchange(lay.tie(send_cot, in_second[2]))
    scale_two = lax.rsqrt(jnp.mean(middle * middle, axis=1, keepdims=True) + EPS_ROW)
    second_own_rows = (middle * scale_two * gains[1]).astype(bf)
    second_rows = lay.rows_of(second_own_rows)
    feed_behind = lay.ring(feed_chunk, 1)
    feed_ahead = lay.ring(feed_chunk, -1)
    feed_across = lay.ring(lay.tie(feed_ahead, second_own_rows), -1)
    feed_pieces = [feed_chunk, feed_ahead, feed_across, feed_behind]
    down_chunk = lay.spread_far(lay.ordered(down_keep, tall_got[out_rows:], 1), 1, second_own_rows)
    down_pieces = lay.spread_ring(down_chunk, True)
    dy_own = matmul(matmul(landing, lay.tie(got_cot, mixed_own)).astype(bf), turning)
    branch_rows = lay.rows_of((live_own * dy_own).astype(bf))
    pre, hidden = feed_forward(second_rows, feed_pieces)
    depth = features // 4

    def columns_of(rows, piece):
        return rows[:, piece * depth : piece * depth + depth]

    down_own, down_terms, down_sent = lay.collect_ring(lambda r: outer_sum(hidden, columns_of(branch_rows, r)), True)
    grad_pre = feed_backward(lay.tie(branch_rows, *down_terms), down_pieces, pre)
    feed_own, feed_terms, feed_sent = lay.collect_ring(
        lambda r: outer_sum(columns_of(second_rows, r), grad_pre), False
    )
    grad_second = lay.own_of([(0, 0, 0, 0, 2 * hidden_here)], [grad_pre], [feed_pieces], nt, features)
    grad_mid_norm, gain_two_grad = norm_back(middle, scale_two, gains[1], grad_second)
    grad_middle = dy_own + grad_mid_norm
    mix_rows = lay.rows_of((live_own * grad_middle).astype(bf))

    grad_heads = heads_backward(mix_rows, out_pieces)
    out_own, out_terms, out_sent = lay.collect_ring(lambda r: outer_sum(heads_out, columns_of(mix_rows, r)), True)
    grad_proj_first, taps_first, params_first, gain_first = mixer_backward(
        0, heads, core, proj_first, decays, lay.tie(grad_heads, feed_sent[0], *out_terms), marks, seg_rows, taps[0], params,
        gain_row, states_first, inverses_first, None,
    )
    first_own, first_terms, first_sent = lay.collect_ring(
        lambda r: outer_sum(columns_of(first_rows, r), grad_proj_first[:, :width]), True
    )
    grad_proj_second, taps_second, params_second, gain_second = mixer_backward(
        pair, heads, core, proj_second, decays, lay.tie(grad_heads, feed_sent[1], *first_terms), marks, seg_rows,
        taps[1], params, gain_row, states_second, inverses_second, grad_proj_first,
    )
    second_own, second_terms, second_sent = lay.collect_ring(
        lambda r: outer_sum(columns_of(first_rows, r), grad_proj_second), False
    )
    grad_first = lay.own_of(
        [(0, 0, 0, 0, width), (1, 0, 1, 0, width), (1, width, 0, width, LANES)],
        [grad_proj_first, lay.tie(grad_proj_second, feed_sent[2], out_sent[0], *second_terms)],
        [in_first, in_second], nt, features,
    )
    grad_x_norm, gain_one_grad = norm_back(x_own, scale_one, gains[0], grad_first)
    grad_tokens = (grad_middle + grad_x_norm).astype(bf)

    def sent_out(own, *others):
        straight = times_back(own, turning).astype(bf)
        return exchange(lay.tie(outer_sum(landing, straight).astype(bf), *others))

    def sent_home(back, *others):
        return outer_sum(sending, lay.tie(back, *others)).astype(bf)

    branch_own = lay.own_of([(0, 0, 0, 0, hidden_here)], [lay.tie(hidden, feed_terms[0], grad_second)], [down_pieces], nn, features)
    output = sent_home(sent_out((middle + live_own * branch_own).astype(bf), out_sent[0]), first_sent[2])
    tokens_grad = sent_home(sent_out(grad_tokens), *second_sent[1:])

    conv_full = jnp.zeros(conv_weights.shape, f32)
    for cut, grad in zip(cuts, (taps_first, taps_second)):
        begin = 0
        for start, size in cut:
            conv_full = lax.dynamic_update_slice_in_dim(conv_full, grad[:, begin : begin + size], start, 1)
            begin += size
    params_grad = params_first + params_second
    log_full = lax.dynamic_update_slice_in_dim(jnp.zeros_like(a_log), params_grad[0, :heads], share * heads, 0)
    bias_full = lax.dynamic_update_slice_in_dim(jnp.zeros_like(dt_bias), params_grad[1, :heads], share * heads, 0)
    gain_grad = gain_first[0] + gain_second[0]
    norm_grads = jnp.stack([straight_gain(gain_one_grad), straight_gain(gain_two_grad)])
    sums = flat([conv_full, norm_grads, gain_grad, log_full, bias_full])
    sums = lay.everywhere(sums, second_sent[1:]).reshape(-1)
    ends = [conv_full.size]
    for size in (2 * features, DV, all_heads, all_heads):
        ends.append(ends[-1] + size)
    norm_grad = sums[ends[0] : ends[1]].reshape(2, features)

    end = second_sent[1:]
    down_grad = lay.collect_last(lay.collect_far(down_own, 1), 1, feed_sent[2])
    first_grad = lay.collect_last(lay.collect_far(first_own, 0), 0, *end)
    second_grad = lay.collect_last(lay.collect_far(second_own, 0), 0)
    feed_grad = lay.collect_last(lay.collect_far(feed_own, 0), 0, *end)
    out_grad = lay.collect_last(lay.collect_far(out_own, 1), 1, *end)
    down_grad, feed_grad, out_grad = [
        (mine, lay.tie(theirs, *end).astype(f32)) for mine, theirs in (down_grad, feed_grad, out_grad)
    ]
    first_grad, second_grad = [(mine, theirs.astype(f32)) for mine, theirs in (first_grad, second_grad)]
    in_grads = []
    begin = 0
    for size in (keys, keys, vals, vals):
        part = slice(begin, begin + size)
        in_grads.append(
            lay.joined(*[[grads[0][:, part], grads[1][:, part]] for grads in zip(first_grad, second_grad)], 1)
        )
        begin += size
    for size in (heads, heads):
        in_grads.append(lay.joined(*[[grad[:, begin : begin + size]] for grad in second_grad], 1))
        begin += size

    def alternate(grad, part):
        return grad.reshape(grad.shape[0], -1, 2, LANES)[:, :, part].reshape(grad.shape[0], -1)

    return (
        output,
        tokens_grad,
        norm_grad,
        *in_grads,
        sums[: ends[0]].reshape(conv_full.shape),
        sums[ends[2] : ends[3]],
        sums[ends[3] : ends[4]],
        sums[ends[1] : ends[2]],
        lay.ordered(*out_grad, 0),
        *[lay.ordered(*[alternate(grad, part) for grad in feed_grad], 1) for part in (0, 1)],
        lay.ordered(*down_grad, 0),
    )


def solution(mesh):
    return jax.shard_map(
        shards,
        mesh=mesh,
        in_specs=(
            P(("dp", "tensor"), None),
            P(("dp", "tensor"), None),
            P("dp", None),
            P(("dp", "tensor")),
            P(),
            P("dp", "tensor"),
            P("dp", "tensor"),
            P("dp", "tensor"),
            P("dp", "tensor"),
            P("dp", "tensor"),
            P("dp", "tensor"),
            P(),
            P(),
            P(),
            P(),
            P("tensor", "dp"),
            P("dp", "tensor"),
            P("dp", "tensor"),
            P("tensor", "dp"),
        ),
        out_specs=(
            P(("dp", "tensor"), None),
            P(("dp", "tensor"), None),
            P(),
            P("dp", "tensor"),
            P("dp", "tensor"),
            P("dp", "tensor"),
            P("dp", "tensor"),
            P("dp", "tensor"),
            P("dp", "tensor"),
            P(),
            P(),
            P(),
            P(),
            P("tensor", "dp"),
            P("dp", "tensor"),
            P("dp", "tensor"),
            P("tensor", "dp"),
        ),
        check_vma=False,
    )
```

```python
import functools

import jax
import jax.numpy as jnp
from jax import lax
from jax.experimental import pallas as pl
from jax.experimental.pallas import tpu as pltpu
from jax.sharding import PartitionSpec as P

bf = jnp.bfloat16
f32 = jnp.float32
DK = 128
DV = 256
CHUNK = 128
LANES = 128
GROUPS = 2
EPS_ROW = 1e-06
EPS_UNIT = 1e-06
EPS_HEAD = 1e-05
NEG = -1e30
VMEM_LIMIT = 56 * 2**20
COST = 1.0


def dot(left, right, left_dim, right_dim):
    return lax.dot_general(
        left.astype(bf), right.astype(bf), (((left_dim,), (right_dim,)), ((), ())), preferred_element_type=f32
    )


def nn(left, right):
    return dot(left, right, 1, 0)


def nt(left, right):
    return dot(left, right, 1, 1)


def tn(left, right):
    return dot(left, right, 0, 0)


def exact(left, right):
    return lax.dot_general(
        left, right, (((1,), (0,)), ((), ())), precision=lax.Precision.HIGHEST, preferred_element_type=f32
    )


def softplus(v):
    return jnp.maximum(v, 0.0) + jnp.log(1.0 + jnp.exp(-jnp.abs(v)))


def sigmoid(v):
    return 1.0 / (1.0 + jnp.exp(-v))


def unit_lower_inverses(systems, places, others):
    eye = (places == others).astype(f32)
    size = 16
    same = (places // size) == (others // size)
    power = [jnp.where(same, a, 0.0) for a in systems]
    inverse = [eye - a for a in power]
    span = 2
    while span < size:
        power = [nn(a, a) for a in power]
        inverse = [t + nn(t, a) for t, a in zip(inverse, power)]
        span *= 2
    while size < places.shape[0]:
        corner = ((places // (2 * size)) == (others // (2 * size))) & ((places // size) != (others // size))
        steps = [nn(jnp.where(corner, a, 0.0), t) for a, t in zip(systems, inverse)]
        inverse = [t - nn(t, s) for t, s in zip(inverse, steps)]
        size *= 2
    return inverse


def conv_channels(padded, group, taps, marks, columns):
    total = taps[0:1, columns] * padded[group, 8 : 8 + CHUNK, columns]
    for offset in range(1, 4):
        total = total + (taps[offset : offset + 1, columns] * marks[:, offset : offset + 1]) * (
            padded[group, 8 - offset : 8 - offset + CHUNK, columns]
        )
    return total


class Unit:
    def __init__(self, group, head, heads, first, lanes, shared):
        self.group = group
        self.head = head
        keys = heads * DK
        self.query_columns = slice(head * DK, head * DK + DK)
        self.key_columns = slice(keys + head * DK, keys + head * DK + DK)
        self.value_columns = slice(2 * keys + head * DV, 2 * keys + head * DV + DV)
        start = 2 * keys + heads * DV + head * DV
        self.gate_columns = slice(start, start + DV)
        self.out_columns = slice(head * DV, head * DV + DV)
        self.lane = first + head
        self.beta_lane = lanes + first + head
        cum, cum_rows, beta, causal, opening, closing = shared
        col = cum[:, self.lane : self.lane + 1]
        row = cum_rows[self.lane : self.lane + 1, :]
        self.decay = jnp.exp(jnp.where(causal, col - row, NEG))
        self.opened = jnp.exp(jnp.where(opening, col, NEG))
        last = cum[CHUNK - 1 : CHUNK, self.lane : self.lane + 1]
        self.closed = jnp.exp(jnp.where(closing, last - col, NEG))
        self.opened_last = self.opened[CHUNK - 1 : CHUNK, :]
        self.strength = beta[:, self.beta_lane : self.beta_lane + 1]


def chunk_units(heads, first, lanes, decays_ref, params, marks_ref, seg_ref, places, others):
    units, kept = [], []
    lower = (places >= others).astype(f32)
    for group in range(GROUPS):
        decays = decays_ref[0, group, 0]
        marks = marks_ref[group, 0]
        biased = decays + params[0:1, :]
        log_decay = -params[1:2, :] * softplus(biased)
        cum = exact(lower, log_decay)
        beta = sigmoid(decays)
        causal = (places >= others) & (marks[:, 0:1] == seg_ref[group, 0])
        shared = (cum, cum.T, beta, causal, marks[:, 4:5] > 0.0, marks[:, 5:6] > 0.0)
        kept.append((biased, log_decay, beta, marks))
        for head in range(heads):
            units.append(Unit(group, head, heads, first, lanes, shared))
    return units, kept


def forward_kernel(
    heads, first, lanes, core_ref, proj, decays, marks_ref, seg_ref, taps, params, gain, partner,
    out, kept_state, kept_inverse, state, padded,
):
    conv_width = heads * (2 * DK + DV)

    @pl.when(pl.program_id(0) == 0)
    def _():
        state[...] = jnp.zeros_like(state)
        padded[:, 0:8, :] = jnp.zeros((GROUPS, 8, conv_width), f32)

    for group in range(GROUPS):
        padded[group, 8:, :] = proj[0, group, 0, :, :conv_width].astype(f32)
    places = lax.broadcasted_iota(jnp.int32, (CHUNK, CHUNK), 0)
    others = lax.broadcasted_iota(jnp.int32, (CHUNK, CHUNK), 1)
    units, kept = chunk_units(heads, first, lanes, decays, params, marks_ref, seg_ref, places, others)
    strict = places > others
    queries, key_vecs, values = [], [], []
    for unit in units:
        marks = kept[unit.group][3]
        summed = conv_channels(padded, unit.group, taps, marks, unit.query_columns)
        act = summed * sigmoid(summed)
        scale = lax.rsqrt(jnp.sum(act * act, axis=1, keepdims=True) + EPS_UNIT)
        queries.append((act * (scale * DK**-0.5)).astype(bf))
        summed = conv_channels(padded, unit.group, taps, marks, unit.key_columns)
        act = summed * sigmoid(summed)
        scale = lax.rsqrt(jnp.sum(act * act, axis=1, keepdims=True) + EPS_UNIT)
        key_vecs.append((act * scale).astype(bf))
    pairs = [jnp.concatenate([q, k], axis=0) for q, k in zip(queries, key_vecs)]
    dots = [nt(pair, k) for pair, k in zip(pairs, key_vecs)]
    systems = [jnp.where(strict, unit.strength * unit.decay * d[CHUNK:], 0.0) for unit, d in zip(units, dots)]
    inverses = unit_lower_inverses(systems, places, others)
    for unit in units:
        summed = conv_channels(padded, unit.group, taps, kept[unit.group][3], unit.value_columns)
        values.append((summed * sigmoid(summed)).astype(bf).astype(f32))
    for group in range(GROUPS):
        padded[group, 0:8, :] = padded[group, CHUNK : CHUNK + 8, :]
    before = [state[number] for number in range(len(units))]
    for number in range(len(units)):
        kept_state[0, number] = before[number].astype(bf)
        kept_inverse[0, number] = inverses[number].astype(bf)
    reads = [nn(pair, s) for pair, s in zip(pairs, before)]
    rights = [unit.strength * (v - unit.opened * read[CHUNK:]) for unit, v, read in zip(units, values, reads)]
    news = [nn(t, r) for t, r in zip(inverses, rights)]
    mixed = [
        unit.opened * read[:CHUNK] + nn(d[:CHUNK] * unit.decay, new)
        for unit, read, d, new in zip(units, reads, dots, news)
    ]
    for number, unit in enumerate(units):
        state[number] = unit.opened_last * before[number] + tn(key_vecs[number], unit.closed * news[number])
    for unit, mix in zip(units, mixed):
        gate = proj[0, unit.group, 0, :, unit.gate_columns].astype(f32)
        scale = lax.rsqrt(jnp.mean(mix * mix, axis=1, keepdims=True) + EPS_HEAD)
        out[0, unit.group, 0, :, unit.out_columns] = (mix * scale * gain[...] * (gate * sigmoid(gate))).astype(bf)


def backward_kernel(
    heads, first, lanes, core_ref, proj, prev_rows, decays, grads, marks_ref, seg_ref, taps, params, gain,
    kept_state, kept_inverse, earlier, proj_grad, taps_grad, params_grad, gain_grad, state_grad, padded, summed_grad,
):
    conv_width = heads * (2 * DK + DV)
    width = conv_width + heads * DV

    @pl.when(pl.program_id(0) == 0)
    def _():
        taps_grad[...] = jnp.zeros_like(taps_grad)
        params_grad[...] = jnp.zeros_like(params_grad)
        gain_grad[...] = jnp.zeros_like(gain_grad)
        state_grad[...] = jnp.zeros_like(state_grad)
        summed_grad[:, CHUNK:, :] = jnp.zeros((GROUPS, 8, conv_width), f32)

    for group in range(GROUPS):
        padded[group, 0:8, :] = prev_rows[0, group, 0, :, :conv_width].astype(f32)[-8:]
        padded[group, 8:, :] = proj[0, group, 0, :, :conv_width].astype(f32)
    places = lax.broadcasted_iota(jnp.int32, (CHUNK, CHUNK), 0)
    others = lax.broadcasted_iota(jnp.int32, (CHUNK, CHUNK), 1)
    units, kept = chunk_units(heads, first, lanes, decays, params, marks_ref, seg_ref, places, others)
    strict = places > others
    q_sums, k_sums, v_sums, q_acts, k_acts, q_scale, k_scale = [], [], [], [], [], [], []
    queries, key_vecs, values = [], [], []
    for unit in units:
        marks = kept[unit.group][3]
        summed = conv_channels(padded, unit.group, taps, marks, unit.query_columns)
        act = summed * sigmoid(summed)
        scale = lax.rsqrt(jnp.sum(act * act, axis=1, keepdims=True) + EPS_UNIT)
        queries.append((act * (scale * DK**-0.5)).astype(bf))
        q_sums.append(summed)
        q_acts.append(act)
        q_scale.append(scale)
        summed = conv_channels(padded, unit.group, taps, marks, unit.key_columns)
        act = summed * sigmoid(summed)
        scale = lax.rsqrt(jnp.sum(act * act, axis=1, keepdims=True) + EPS_UNIT)
        key_vecs.append((act * scale).astype(bf))
        k_sums.append(summed)
        k_acts.append(act)
        k_scale.append(scale)
        summed = conv_channels(padded, unit.group, taps, marks, unit.value_columns)
        values.append((summed * sigmoid(summed)).astype(bf).astype(f32))
        v_sums.append(summed)
    count = len(units)
    pairs = [jnp.concatenate([q, k], axis=0) for q, k in zip(queries, key_vecs)]
    dots = [nt(pair, k) for pair, k in zip(pairs, key_vecs)]
    before = [kept_state[0, number] for number in range(count)]
    after_grad = [state_grad[number] for number in range(count)]
    inverses = [kept_inverse[0, number] for number in range(count)]
    reads = [nn(pair, s) for pair, s in zip(pairs, before)]
    gaps = [v - unit.opened * read[CHUNK:] for unit, v, read in zip(units, values, reads)]
    news = [nn(t, unit.strength * g) for t, unit, g in zip(inverses, units, gaps)]
    scores = [d[:CHUNK] * unit.decay for d, unit in zip(dots, units)]
    mixed = [unit.opened * read[:CHUNK] + nn(score, new) for unit, read, score, new in zip(units, reads, scores, news)]
    mix_grads = []
    gain_row = gain[...]
    gain_total = jnp.zeros((1, DV), f32)
    for unit, mix in zip(units, mixed):
        gate = proj[0, unit.group, 0, :, unit.gate_columns].astype(f32)
        grad = grads[0, unit.group, 0, :, unit.out_columns].astype(f32)
        scale = lax.rsqrt(jnp.mean(mix * mix, axis=1, keepdims=True) + EPS_HEAD)
        soft = sigmoid(gate)
        grad_normed = grad * (mix * scale)
        proj_grad[0, unit.group, 0, :, unit.gate_columns] = (
            grad_normed * gain_row * (soft * (1.0 + gate * (1.0 - soft)))
        ).astype(bf)
        silu = gate * soft
        gain_total = gain_total + jnp.sum(grad_normed * silu, axis=0, keepdims=True)
        inner = grad * silu * gain_row
        mix_grads.append(scale * inner - mix * (scale * scale * scale) * jnp.mean(inner * mix, axis=1, keepdims=True))
    gain_grad[0:1, :] += gain_total
    pushes = [nn(k, g) for k, g in zip(key_vecs, after_grad)]
    new_grads = [
        tn(score, grad) + unit.closed * push for score, grad, unit, push in zip(scores, mix_grads, units, pushes)
    ]
    score_grads = [nt(grad, new) for grad, new in zip(mix_grads, news)]
    right_grads = [tn(t, grad) for t, grad in zip(inverses, new_grads)]
    system_grads = [jnp.where(strict, -nt(grad, new), 0.0) for grad, new in zip(right_grads, news)]
    lane_ids = lax.broadcasted_iota(jnp.int32, (CHUNK, LANES), 1)
    rows_down = lax.broadcasted_iota(jnp.int32, (CHUNK, 1), 0)
    cum_grads = [jnp.zeros((CHUNK, LANES), f32) for _ in range(GROUPS)]
    beta_grads = [jnp.zeros((CHUNK, LANES), f32) for _ in range(GROUPS)]
    cross_rows = [[], []]
    raised = []
    for number, unit in enumerate(units):
        read_query = reads[number][:CHUNK]
        read_key = reads[number][CHUNK:]
        gram = dots[number][CHUNK:]
        decayed_score = score_grads[number] * unit.decay
        decayed_system = system_grads[number] * unit.decay
        system_gram = decayed_system * gram
        crossing = decayed_score * dots[number][:CHUNK] + unit.strength * system_gram
        value_grad = unit.strength * right_grads[number]
        beta_grad = jnp.sum(system_gram, axis=1, keepdims=True) + jnp.sum(
            right_grads[number] * gaps[number], axis=1, keepdims=True
        )
        open_grad = jnp.sum(mix_grads[number] * read_query - value_grad * read_key, axis=1, keepdims=True)
        close_grad = unit.closed * jnp.sum(news[number] * pushes[number], axis=1, keepdims=True)
        kept_dot = jnp.sum(
            jnp.sum(after_grad[number] * before[number].astype(f32), axis=1, keepdims=True), axis=0, keepdims=True
        )
        last_grad = jnp.sum(close_grad, axis=0, keepdims=True) + unit.opened_last * kept_dot
        col = jnp.sum(crossing, axis=1, keepdims=True) + unit.opened * open_grad - close_grad
        col = col + jnp.where(rows_down == CHUNK - 1, last_grad, 0.0)
        cross_rows[unit.group].append(jnp.sum(crossing, axis=0, keepdims=True))
        cum_grads[unit.group] = jnp.where(lane_ids == unit.lane, col, cum_grads[unit.group])
        beta_grads[unit.group] = jnp.where(lane_ids == unit.beta_lane, beta_grad, beta_grads[unit.group])
        raised.append((decayed_score.astype(bf), (unit.strength * decayed_system).astype(bf), value_grad))
    stacked = [
        jnp.concatenate([(unit.opened * grad).astype(bf), (-unit.opened * item[2]).astype(bf)], axis=0)
        for unit, item, grad in zip(units, raised, mix_grads)
    ]
    through = [nt(x, s) for x, s in zip(stacked, before)]
    grams = [jnp.concatenate([item[0], item[1]], axis=0) for item in raised]
    direct = [nn(g, k) for g, k in zip(grams, key_vecs)]
    turned = [tn(g, pair) for g, pair in zip(grams, pairs)]
    pushed = [nt(unit.closed * new, grad) for unit, new, grad in zip(units, news, after_grad)]
    for number, unit in enumerate(units):
        state_grad[number] = unit.opened_last * after_grad[number] + tn(pairs[number], stacked[number])
    for number, unit in enumerate(units):
        query_grad = (through[number][:CHUNK] + direct[number][:CHUNK]) * DK**-0.5
        key_grad = through[number][CHUNK:] + direct[number][CHUNK:] + turned[number] + pushed[number]
        for grad, act, scale, summed, columns in (
            (query_grad, q_acts[number], q_scale[number], q_sums[number], unit.query_columns),
            (key_grad, k_acts[number], k_scale[number], k_sums[number], unit.key_columns),
        ):
            inner = scale * (grad - act * (scale * scale) * jnp.sum(grad * act, axis=1, keepdims=True))
            soft = sigmoid(summed)
            summed_grad[unit.group, 0:CHUNK, columns] = inner * (soft * (1.0 + summed * (1.0 - soft)))
        summed = v_sums[number]
        soft = sigmoid(summed)
        summed_grad[unit.group, 0:CHUNK, unit.value_columns] = raised[number][2] * (
            soft * (1.0 + summed * (1.0 - soft))
        )
    for group in range(GROUPS):
        marks = kept[group][3]
        for start in range(0, conv_width, LANES):
            columns = slice(start, start + LANES)
            grad = summed_grad[group, 0:CHUNK, columns]
            total = taps[0:1, columns] * grad
            taps_grad[0:1, columns] += jnp.sum(grad * padded[group, 8 : 8 + CHUNK, columns], axis=0, keepdims=True)
            for offset in range(1, 4):
                later = summed_grad[group, offset : offset + CHUNK, columns]
                total = total + (taps[offset : offset + 1, columns] * marks[:, 5 + offset : 6 + offset]) * later
                taps_grad[offset : offset + 1, columns] += jnp.sum(
                    (grad * marks[:, offset : offset + 1]) * padded[group, 8 - offset : 8 - offset + CHUNK, columns],
                    axis=0, keepdims=True,
                )
            proj_grad[0, group, 0, :, columns] = total.astype(bf)
        summed_grad[group, CHUNK:, :] = summed_grad[group, 0:8, :]
    upper = (places <= others).astype(f32)
    for group in range(GROUPS):
        biased, log_decay, beta, _ = kept[group]
        blank = [jnp.zeros((first, CHUNK), f32)] if first else []
        rest = [jnp.zeros((CHUNK - heads - first, CHUNK), f32)]
        cross = jnp.concatenate(blank + cross_rows[group] + rest, axis=0).T
        log_grad = exact(upper, cum_grads[group] - cross)
        decay_grad = log_grad * (-params[1:2, :]) * sigmoid(biased)
        both = decay_grad + beta_grads[group] * beta * (1.0 - beta)
        if earlier is not None:
            both = both + earlier[0, group, 0].astype(f32)
        proj_grad[0, group, 0, :, width:] = both.astype(bf)
        params_grad[0:1, :] += jnp.sum(log_grad * log_decay, axis=0, keepdims=True)
        params_grad[1:2, :] += jnp.sum(decay_grad, axis=0, keepdims=True)


def folded(rows):
    return rows.reshape(2, GROUPS, -1, CHUNK, rows.shape[1])


def mixer_forward(first, lanes, core, proj, decays, marks, seg_rows, taps, params, gain, partner):
    conv_width = taps.shape[1]
    heads = conv_width // (2 * DK + DV)
    proj, decays = folded(proj), folded(decays)
    per_core = proj.shape[2]
    chunks = 2 * per_core
    units = GROUPS * heads

    def at(c, core_ref):
        return ((c // per_core) ^ core_ref[0], 0, c % per_core, 0, 0)

    fixed = lambda c, core_ref: (0, 0)
    here = lambda c, core_ref: (0, c, 0, 0)
    kept = lambda c, core_ref: (c, 0, 0, 0)
    full = proj.shape[:4] + (lanes * DV,)
    body = functools.partial(forward_kernel, heads, first, lanes)
    more_specs, more, aliases = [], [], {}
    if partner is None:
        inner = body

        def body(*refs):
            return inner(*refs[:8], None, *refs[8:])

    else:
        more_specs, more, aliases = [pl.BlockSpec(memory_space=pl.ANY)], [partner.reshape(full)], {8: 0}

    def out_at(c, core_ref):
        return at(c, core_ref)[:4] + (first // heads,)

    out, states, inverses = pl.pallas_call(
        body,
        grid_spec=pltpu.PrefetchScalarGridSpec(
            num_scalar_prefetch=1,
            grid=(chunks,),
            in_specs=[
                pl.BlockSpec((1, GROUPS, 1, CHUNK, proj.shape[4]), at),
                pl.BlockSpec((1, GROUPS, 1, CHUNK, LANES), at),
                pl.BlockSpec((GROUPS, 1, CHUNK, LANES), here),
                pl.BlockSpec((GROUPS, 1, 1, CHUNK), here),
                pl.BlockSpec((4, conv_width), fixed),
                pl.BlockSpec((8, LANES), fixed),
                pl.BlockSpec((1, DV), fixed),
            ]
            + more_specs,
            out_specs=[
                pl.BlockSpec((1, GROUPS, 1, CHUNK, heads * DV), out_at),
                pl.BlockSpec((1, units, DK, DV), kept),
                pl.BlockSpec((1, units, CHUNK, CHUNK), kept),
            ],
            scratch_shapes=[pltpu.VMEM((units, DK, DV), f32), pltpu.VMEM((GROUPS, CHUNK + 8, conv_width), f32)],
        ),
        out_shape=[
            jax.ShapeDtypeStruct(full, bf),
            jax.ShapeDtypeStruct((chunks, units, DK, DV), bf),
            jax.ShapeDtypeStruct((chunks, units, CHUNK, CHUNK), bf),
        ],
        compiler_params=pltpu.CompilerParams(vmem_limit_bytes=VMEM_LIMIT),
        cost_estimate=pl.CostEstimate(flops=int(COST * 16 * 10**9), bytes_accessed=int(COST * 16 * 2**20), transcendentals=0),
        input_output_aliases=aliases,
        name="mixer_forward",
    )(core, proj, decays, marks, seg_rows, taps, params, gain, *more)
    return out.reshape(-1, lanes * DV), states, inverses


def mixer_backward(first, lanes, core, proj, decays, grads, marks, seg_rows, taps, params, gain, states, inverses, earlier):
    conv_width = taps.shape[1]
    heads = conv_width // (2 * DK + DV)
    proj, decays, grads = folded(proj), folded(decays), folded(grads)
    per_core = proj.shape[2]
    chunks = 2 * per_core
    units = GROUPS * heads
    width = conv_width + heads * DV + LANES
    tail = 16

    def at(step, core_ref):
        c = chunks - 1 - step
        return ((c // per_core) ^ core_ref[0], 0, c % per_core, 0, 0)

    def prev(step, core_ref):
        c = jnp.maximum(chunks - 2 - step, 0)
        return ((c // per_core) ^ core_ref[0], 0, c % per_core, CHUNK // tail - 1, 0)

    def grad_at(step, core_ref):
        return at(step, core_ref)[:4] + (first // heads,)

    def last_lanes(step, core_ref):
        return at(step, core_ref)[:4] + ((conv_width + heads * DV) // LANES,)

    fixed = lambda step, core_ref: (0, 0)
    here = lambda step, core_ref: (0, chunks - 1 - step, 0, 0)
    kept = lambda step, core_ref: (chunks - 1 - step, 0, 0, 0)
    in_specs = [
        pl.BlockSpec((1, GROUPS, 1, CHUNK, proj.shape[4]), at),
        pl.BlockSpec((1, GROUPS, 1, tail, proj.shape[4]), prev),
        pl.BlockSpec((1, GROUPS, 1, CHUNK, LANES), at),
        pl.BlockSpec((1, GROUPS, 1, CHUNK, heads * DV), grad_at),
        pl.BlockSpec((GROUPS, 1, CHUNK, LANES), here),
        pl.BlockSpec((GROUPS, 1, 1, CHUNK), here),
        pl.BlockSpec((4, conv_width), fixed),
        pl.BlockSpec((8, LANES), fixed),
        pl.BlockSpec((1, DV), fixed),
        pl.BlockSpec((1, units, DK, DV), kept),
        pl.BlockSpec((1, units, CHUNK, CHUNK), kept),
    ]
    inputs = [core, proj, proj, decays, grads, marks, seg_rows, taps, params, gain, states, inverses]
    body = functools.partial(backward_kernel, heads, first, lanes)
    if earlier is not None:
        in_specs.append(pl.BlockSpec((1, GROUPS, 1, CHUNK, LANES), last_lanes))
        inputs.append(folded(earlier))
    else:
        whole = body

        def body(*refs):
            return whole(*refs[:12], None, *refs[12:])

    out, taps_grad, params_grad, gain_grad = pl.pallas_call(
        body,
        grid_spec=pltpu.PrefetchScalarGridSpec(
            num_scalar_prefetch=1,
            grid=(chunks,),
            in_specs=in_specs,
            out_specs=[
                pl.BlockSpec((1, GROUPS, 1, CHUNK, width), at),
                pl.BlockSpec((4, conv_width), fixed),
                pl.BlockSpec((8, LANES), fixed),
                pl.BlockSpec((8, DV), fixed),
            ],
            scratch_shapes=[
                pltpu.VMEM((units, DK, DV), f32),
                pltpu.VMEM((GROUPS, CHUNK + 8, conv_width), f32),
                pltpu.VMEM((GROUPS, CHUNK + 8, conv_width), f32),
            ],
        ),
        out_shape=[
            jax.ShapeDtypeStruct(proj.shape[:4] + (width,), bf),
            jax.ShapeDtypeStruct((4, conv_width), f32),
            jax.ShapeDtypeStruct((8, LANES), f32),
            jax.ShapeDtypeStruct((8, DV), f32),
        ],
        compiler_params=pltpu.CompilerParams(vmem_limit_bytes=VMEM_LIMIT),
        cost_estimate=pl.CostEstimate(flops=int(COST * 30 * 10**9), bytes_accessed=int(COST * 30 * 2**20), transcendentals=0),
        name="mixer_backward",
    )(*inputs)
    return out.reshape(-1, width), taps_grad, params_grad, gain_grad


def group_marks(lengths, group_rows):
    groups, count = lengths.shape
    position = jnp.arange(group_rows, dtype=jnp.int32)[None, :]
    segment = jnp.zeros((groups, group_rows), jnp.int32)
    end = jnp.zeros((groups, 1), jnp.int32)
    for number in range(count):
        segment = segment + (position >= end).astype(jnp.int32)
        end = end + lengths[:, number : number + 1]
    live = (position < end).astype(f32)
    padded = jnp.pad(segment, ((0, 0), (CHUNK, CHUNK)))
    later = lambda offset: padded[:, CHUNK + offset : CHUNK + offset + group_rows]
    chunked = segment.reshape(groups, group_rows // CHUNK, CHUNK)
    before = padded[:, CHUNK - 1 : CHUNK - 1 + group_rows].reshape(chunked.shape)[:, :, :1]
    columns = [segment]
    columns += [later(-offset) == segment for offset in (1, 2, 3)]
    columns += [(chunked == before).reshape(segment.shape), (chunked == chunked[:, :, -1:]).reshape(segment.shape)]
    columns += [later(offset) == segment for offset in (1, 2, 3)]
    lane = jnp.arange(LANES, dtype=jnp.int32)
    marks = jnp.zeros((groups, group_rows, LANES), f32)
    for number, column in enumerate(columns):
        marks = jnp.where(lane == number, column.astype(f32)[:, :, None], marks)
    marks = marks.reshape(groups, group_rows // CHUNK, CHUNK, LANES)
    seg_rows = segment.astype(f32).reshape(groups, group_rows // CHUNK, 1, CHUNK)
    return marks, seg_rows, live


def pick_kernel(pairs, turn_ref, *refs):
    count = len(refs) - len(pairs)
    for out, parts in zip(refs[count:], pairs):
        begin = 0
        for number, start, stop in parts:
            out[:, begin : begin + stop - start] = refs[number][:, start:stop]
            begin += stop - start


def picked(turn, weights, axes, joins):
    in_specs, inputs, shapes = [], [], []
    for weight, axis in zip(weights, axes):
        rows, columns = weight.shape
        if axis is None:
            in_specs += [pl.BlockSpec((rows, columns), lambda i, t: (0, 0))] * 2
            shapes.append((rows, columns))
        elif axis == 1:
            in_specs += [
                pl.BlockSpec((rows, columns // 2), lambda i, t: (0, t[0])),
                pl.BlockSpec((rows, columns // 2), lambda i, t: (0, 1 - t[0])),
            ]
            shapes.append((rows, columns // 2))
        else:
            in_specs += [
                pl.BlockSpec((rows // 2, columns), lambda i, t: (t[0], 0)),
                pl.BlockSpec((rows // 2, columns), lambda i, t: (1 - t[0], 0)),
            ]
            shapes.append((rows // 2, columns))
        inputs += [weight, weight]
    pairs, out_shapes = [], []
    for join in joins:
        width = sum(stop - start for _, start, stop in join)
        for given in (0, 1):
            pairs.append([(2 * number + given, start, stop) for number, start, stop in join])
            out_shapes.append((shapes[join[0][0]][0], width))
    outs = pl.pallas_call(
        functools.partial(pick_kernel, pairs),
        grid_spec=pltpu.PrefetchScalarGridSpec(
            num_scalar_prefetch=1,
            grid=(1,),
            in_specs=in_specs,
            out_specs=[pl.BlockSpec(shape, lambda i, t: (0, 0)) for shape in out_shapes],
        ),
        out_shape=[jax.ShapeDtypeStruct(shape, bf) for shape in out_shapes],
        compiler_params=pltpu.CompilerParams(vmem_limit_bytes=VMEM_LIMIT),
        cost_estimate=pl.CostEstimate(flops=0, bytes_accessed=8 * 2**20, transcendentals=0),
        name="picked",
    )(turn, *inputs)
    return [(outs[2 * number], outs[2 * number + 1]) for number in range(len(joins))]


TILE = 256
STRIP = 256


def call(body, grid, in_specs, out_specs, out_shape, flops, moved, name, inputs, scratch=()):
    return pl.pallas_call(
        body,
        grid=grid,
        scratch_shapes=scratch,
        in_specs=in_specs,
        out_specs=out_specs,
        out_shape=out_shape,
        compiler_params=pltpu.CompilerParams(vmem_limit_bytes=VMEM_LIMIT),
        cost_estimate=pl.CostEstimate(flops=int(flops * COST), bytes_accessed=int(moved * COST), transcendentals=0),
        name=name,
    )(*inputs)


def strip_sum(rows, pieces, start, product):
    total = None
    begin = 0
    depth = rows.shape[1] // len(pieces)
    for piece in pieces:
        part = product(rows[start : start + STRIP, begin : begin + depth], piece[...])
        total = part if total is None else total + part
        begin += depth
    return total


def whole(array):
    return pl.BlockSpec(array.shape, lambda i: (0,) * array.ndim)


def project(rows, pieces, width, extra):
    count = rows.shape[0]
    depth = pieces[0].shape[0]
    steps = width // TILE
    used = len(pieces)

    def body(rows_ref, *refs):
        weights = refs[:used]
        out = refs[2 * used if extra else used]
        for start in range(0, count, STRIP):
            out[start : start + STRIP, :] = strip_sum(rows_ref, weights, start, nn).astype(bf)
        if extra:

            @pl.when(pl.program_id(0) == 0)
            def _():
                for start in range(0, count, STRIP):
                    refs[-1][start : start + STRIP, :] = strip_sum(rows_ref, refs[used : 2 * used], start, nn)

    in_specs = [whole(rows)] + [pl.BlockSpec((depth, TILE), lambda i: (0, i))] * used
    out_specs = [pl.BlockSpec((count, TILE), lambda i: (0, i))]
    out_shape = [jax.ShapeDtypeStruct((count, width), bf)]
    inputs = [rows, *pieces]
    if extra:
        in_specs += [pl.BlockSpec((depth, LANES), lambda i: (0, width // LANES))] * used
        out_specs.append(pl.BlockSpec((count, LANES), lambda i: (0, 0)))
        out_shape.append(jax.ShapeDtypeStruct((count, LANES), f32))
        inputs += pieces
    flops = 2 * count * depth * used * width
    moved = 2 * (count * depth * used + depth * used * width + count * width)
    return call(body, (steps,), in_specs, out_specs, out_shape, flops, moved, "project", inputs)


def feed_forward(rows, pieces):
    count = rows.shape[0]
    depth, width = pieces[0].shape
    used = len(pieces)

    def body(rows_ref, *refs):
        pre_out, hidden_out = refs[used:]
        for start in range(0, count, STRIP):
            strip = slice(start, start + STRIP)
            both = strip_sum(rows_ref, refs[:used], start, nn)
            gate = both[:, :LANES]
            pre_out[strip, :] = both.astype(bf)
            hidden_out[strip, :] = (gate * sigmoid(gate) * both[:, LANES:]).astype(bf)

    return call(
        body,
        (width // (2 * LANES),),
        [whole(rows)] + [pl.BlockSpec((depth, 2 * LANES), lambda i: (0, i))] * used,
        [pl.BlockSpec((count, 2 * LANES), lambda i: (0, i)), pl.BlockSpec((count, LANES), lambda i: (0, i))],
        [jax.ShapeDtypeStruct((count, width), bf), jax.ShapeDtypeStruct((count, width // 2), bf)],
        2 * count * depth * used * width,
        2 * (count * depth * used + depth * used * width + 2 * count * width),
        "feed_forward",
        [rows, *pieces],
    )


def feed_backward(rows, down_pieces, pre):
    count = rows.shape[0]
    width, depth = down_pieces[0].shape
    used = len(down_pieces)

    def body(rows_ref, *refs):
        pre_ref, out = refs[used:]
        for begin in range(0, width, TILE):
            size = min(TILE, width - begin)
            total = None
            for number in range(used):
                part = nt(rows_ref[:, number * depth : number * depth + depth], refs[number][begin : begin + size, :])
                total = part if total is None else total + part
            for shift in range(0, size, LANES):
                grad = total[:, shift : shift + LANES]
                at = 2 * (begin + shift)
                gate = pre_ref[:, at : at + LANES].astype(f32)
                up = pre_ref[:, at + LANES : at + 2 * LANES].astype(f32)
                soft = sigmoid(gate)
                out[:, at : at + LANES] = (grad * up * soft * (1.0 + gate * (1.0 - soft))).astype(bf)
                out[:, at + LANES : at + 2 * LANES] = (grad * gate * soft).astype(bf)

    strip = pl.BlockSpec((STRIP, 2 * width), lambda i: (i, 0))
    return call(
        body,
        (count // STRIP,),
        [pl.BlockSpec((STRIP, depth * used), lambda i: (i, 0))] + [whole(piece) for piece in down_pieces] + [strip],
        strip,
        jax.ShapeDtypeStruct((count, 2 * width), bf),
        2 * count * depth * used * width,
        2 * (count * depth * used + depth * used * width + 4 * count * width),
        "feed_backward",
        [rows, *down_pieces, pre],
    )


def heads_backward(rows, out_pieces):
    count = rows.shape[0]
    width, depth = out_pieces[0].shape
    used = len(out_pieces)

    def body(rows_ref, *refs):
        for start in range(0, count, STRIP):
            refs[used][start : start + STRIP, :] = strip_sum(rows_ref, refs[:used], start, nt).astype(bf)

    return call(
        body,
        (width // TILE,),
        [whole(rows)] + [pl.BlockSpec((TILE, depth), lambda i: (i, 0))] * used,
        pl.BlockSpec((count, TILE), lambda i: (0, i)),
        jax.ShapeDtypeStruct((count, width), bf),
        2 * count * depth * used * width,
        2 * (count * depth * used + depth * used * width + count * width),
        "heads_backward",
        [rows, *out_pieces],
    )


def wide(terms, lefts, pieces, product, features, got):
    count = lefts[0].shape[0]
    half, per = count // 2, count // 4
    depth = features // 4
    given = got is None
    used = len(pieces)
    inputs = list(lefts) + [piece for group in pieces for piece in group]
    in_specs = [pl.BlockSpec((half, left.shape[1]), (lambda i: (1, 0)) if given else (lambda i: (0, 0))) for left in lefts]
    in_specs += [pl.BlockSpec(memory_space=pl.ANY)] * (4 * used)
    flops = 2 * half * features * sum(term[4] for term in terms)
    moved = 2 * sum(piece.size for group in pieces for piece in group) + 6 * count * features
    skip = len(lefts) + 4 * used

    def body(*refs):
        held, sems = refs[-1 - used : -1], refs[-1]

        def copy(number, piece):
            source = refs[len(lefts) + 4 * number + piece]
            return pltpu.make_async_copy(source, held[number].at[piece], sems.at[number, piece])

        for piece in range(4):
            for number in range(used):
                copy(number, piece).start()
        for piece in range(4):
            columns = slice(piece * depth, piece * depth + depth)
            for number in range(used):
                copy(number, piece).wait()
            for strip in range(2):
                rows = slice(strip * per, strip * per + per)
                total = None
                for number, begin, weight, first, size in terms:
                    left = refs[number][rows, begin : begin + size]
                    right = held[weight][piece]
                    right = right[:, first : first + size] if product is nt else right
                    part = product(left, right)
                    total = part if total is None else total + part
                if given:
                    refs[skip][rows, columns] = total.astype(bf)
                else:
                    total = total + refs[skip][rows, columns].astype(f32)
                    if strip == 0:
                        refs[skip + 2][:, columns] = total
                    else:
                        refs[skip + 1][:, columns] = total.astype(bf)

    scratch = [pltpu.VMEM((4,) + group[0].shape, bf) for group in pieces] + [pltpu.SemaphoreType.DMA((used, 4))]
    if given:
        out_specs = pl.BlockSpec((half, features), lambda i: (0, 0))
        out_shape = jax.ShapeDtypeStruct((half, features), bf)
    else:
        in_specs.append(pl.BlockSpec((half, features), lambda i: (0, 0)))
        inputs.append(got)
        out_specs = [pl.BlockSpec((per, features), lambda i: (0, 0))] * 2
        out_shape = [jax.ShapeDtypeStruct((per, features), bf), jax.ShapeDtypeStruct((per, features), f32)]
    return call(
        body, (1,), in_specs, out_specs, out_shape, flops, moved, "wide_given" if given else "wide_kept", inputs, scratch
    )


RING = (0, 1, 3, 2)


def matmul(left, right):
    return jnp.dot(left, right, preferred_element_type=f32)


def outer_sum(left, right):
    return lax.dot_general(left, right, (((0,), (0,)), ((), ())), preferred_element_type=f32)


def times_back(left, right):
    return lax.dot_general(left, right, (((1,), (1,)), ((), ())), preferred_element_type=f32)


def norm_back(inputs, scale, gain, grad_out):
    scaled = grad_out * gain
    grad_in = scale * scaled - inputs * scale**3 * jnp.mean(scaled * inputs, axis=1, keepdims=True)
    return (grad_in, jnp.sum(grad_out * inputs * scale, axis=0))


class Layout:
    def __init__(self):
        self.ways = lax.axis_size("dp")
        self.spans = self.ways // 8
        dp = lax.axis_index("dp")
        self.core = lax.axis_index("tensor")
        self.turn = (dp // 4) % 2
        self.far = dp // 8
        near = dp % 4
        self.spot = near ^ (near >> 1)
        self.queues = {}

    def queued(self, values, queue, depth):
        line = self.queues.setdefault(queue, [])
        if len(line) >= depth:
            values, _ = lax.optimization_barrier((values, line[-depth]))
        return values, line

    def ring(self, values, step):
        pairs = []
        for number in range(self.ways):
            near = number % 4
            pairs.append((number, number - near + RING[((near ^ (near >> 1)) + step) % 4]))
        values, line = self.queued(values, step, DEPTH)
        line.append(lax.ppermute(values, "dp", pairs))
        return line[-1]

    def flip(self, values, bit):
        return lax.ppermute(values, "dp", [(n, n ^ bit) for n in range(self.ways)])

    def turned(self, values):
        return self.flip(values, 4)

    def crossed(self, values):
        return lax.ppermute(values, "tensor", [(0, 1), (1, 0)])

    def far_bits(self):
        bit = 8
        while bit < self.ways:
            yield bit
            bit *= 2

    def sources(self):
        places = jnp.arange(self.ways, dtype=jnp.int32)
        step = places // (2 * self.spans)
        jump = (places // 2) % self.spans
        spot = (self.spot + step) % 4
        return ((self.far ^ jump) * 2 + places % 2) * 4 + (spot ^ (spot >> 1))

    def ordered(self, first, second, axis):
        return jnp.where(
            self.turn == 0, jnp.concatenate([first, second], axis=axis), jnp.concatenate([second, first], axis=axis)
        )

    def tie(self, values, *others):
        return lax.optimization_barrier((values, *others))[0]

    def spread_far(self, chunk, axis, *others):
        for bit in self.far_bits():
            sent, line = self.queued(chunk, "far", DEPTH)
            line.append(self.flip(sent, bit))
            line[-1] = self.tie(line[-1], *others)
            chunk = jnp.concatenate([chunk, line[-1]], axis=axis)
        return chunk

    def spread_ring(self, chunk, upward):
        ahead = self.ring(chunk, -1)
        behind = self.ring(chunk, 1)
        across = self.ring(behind, 1) if upward else self.ring(ahead, -1)
        return [chunk, ahead, across, behind]

    def collect_ring(self, make, upward):
        across = make(2).astype(bf)
        if upward:
            behind = make(3).astype(bf)
            up = self.ring(across, 1)
            down = self.ring(behind, -1)
            last = self.ring((make(1) + up).astype(bf), 1)
            return make(0) + last + down, (across, behind), (up, down, last)
        ahead = make(1).astype(bf)
        down = self.ring(across, -1)
        up = self.ring(ahead, 1)
        last = self.ring((make(3) + down).astype(bf), -1)
        return make(0) + up + last, (across, ahead), (down, up, last)

    def collect_far(self, own, axis):
        for bit in reversed(list(self.far_bits())):
            half = own.shape[axis] // 2
            sent = lax.slice_in_dim(own, half, 2 * half, axis=axis)
            own = lax.slice_in_dim(own, 0, half, axis=axis), self.flip(sent.astype(bf), bit)
            if bit > 8:
                own = own[0] + own[1]
        return own

    def collect_last(self, own, axis, *others):
        if isinstance(own, tuple):
            own = own[0] + self.tie(own[1], *others)
        half = own.shape[axis] // 2
        mine = lax.dynamic_slice_in_dim(own, self.turn * half, half, axis)
        other = lax.dynamic_slice_in_dim(own, (1 - self.turn) * half, half, axis)
        return mine, self.turned(other.astype(bf))

    def joined(self, mine, theirs, axis):
        return self.ordered(jnp.concatenate(mine, axis=axis), jnp.concatenate(theirs, axis=axis), axis)

    def rows_of(self, own):
        across = self.crossed(own)
        there = self.turned(own)
        return jnp.concatenate([own, there, across, self.crossed(there)], axis=0)

    def own_of(self, terms, lefts, pieces, product, features):
        given = wide(terms, lefts, pieces, product, features, None)
        there, own = wide(terms, lefts, pieces, product, features, self.crossed(given))
        return own + self.turned(there)

    def everywhere(self, values, marks):
        bits = []
        bit = 1
        while bit < self.ways:
            bits.append(bit)
            bit *= 2
        for bit in reversed(bits):
            values = values + self.tie(self.flip(values, bit), *marks)
        return values + self.crossed(values)


DEPTH = 1


def flat(parts):
    joined = jnp.concatenate([part.reshape(-1) for part in parts])
    return jnp.pad(joined, (0, -joined.shape[0] % (8 * LANES))).reshape(-1, LANES)


def shards(
    tokens, cotangent, lengths, slot_of, norm_gains, w_query, w_key, w_value, w_gate, w_decay, w_beta,
    conv_weights, a_log, dt_bias, out_gain, w_out, w_mlp_gate, w_mlp_up, w_mlp_down,
):
    lay = Layout()
    row_count, features = tokens.shape
    tensor_ways = lax.axis_size("tensor")
    device_count = lay.ways * tensor_ways
    group_rows = row_count * tensor_ways
    capacity = row_count // device_count + 2
    bulk_rows = device_count * capacity
    all_heads = a_log.shape[0]
    heads = all_heads // (2 * tensor_ways)
    pair = heads // 2
    all_keys = all_heads * DK
    keys, vals = pair * DK, pair * DV
    width = 2 * keys + 2 * vals
    share = lay.core * 2 + lay.turn
    turn = lay.turn.reshape(1)
    core = lay.core.reshape(1)

    target = slot_of // row_count
    within = slot_of % row_count
    hits = target[:, None] == jnp.arange(device_count, dtype=jnp.int32)[None, :]
    places = jnp.arange(row_count, dtype=jnp.int32)
    earlier = (places[:, None] >= places[None, :]).astype(bf)
    rank = jnp.sum(matmul(earlier, hits.astype(bf)) * hits.astype(f32), axis=1).astype(jnp.int32) - 1
    outgoing = target * capacity + rank
    sending = (jnp.arange(bulk_rows, dtype=jnp.int32)[:, None] == outgoing[None, :]).astype(bf)
    slot_mark = jnp.broadcast_to((within + 1).astype(bf)[:, None], (row_count, LANES))
    send_tokens = matmul(sending, jnp.concatenate([tokens, slot_mark], axis=1)).astype(bf)
    send_cot = matmul(sending, cotangent).astype(bf)

    def exchange(values):
        return lax.all_to_all(values, ("dp", "tensor"), split_axis=0, concat_axis=0, tiled=True)


    def half_heads(weight):
        kept = jnp.where(lay.turn == 0, weight[:, :heads], weight[:, heads:])
        given = jnp.where(lay.turn == 0, weight[:, heads:], weight[:, :heads])
        return kept, given

    decay_halves, beta_halves = half_heads(w_decay), half_heads(w_beta)
    lanes_of = [
        jnp.pad(jnp.concatenate([d, b], axis=1), ((0, 0), (0, LANES - 2 * heads)))
        for d, b in zip(decay_halves, beta_halves)
    ]
    first_join = [(0, 0, keys), (1, 0, keys), (2, 0, vals), (3, 0, vals)]
    second_join = [(0, keys, 2 * keys), (1, keys, 2 * keys), (2, vals, 2 * vals), (3, vals, 2 * vals)]
    out_rows, hidden_here = w_out.shape[0] // 2, w_mlp_gate.shape[1] // 2
    block = features // lay.ways
    mixed_join = []
    for start in range(0, hidden_here, LANES):
        mixed_join += [(0, start, start + LANES), (1, start, start + LANES)]
    blob_first, (second_keep, second_give) = picked(
        turn, [w_query, w_key, w_value, w_gate], [1] * 4, [first_join, second_join]
    )
    first_keep, first_give = [
        jnp.concatenate([blob, extra], axis=1) for blob, extra in zip(blob_first, lanes_of)
    ]
    first_got = lay.turned(first_give)
    got_tokens = exchange(lay.tie(send_tokens, first_got))
    first_chunk = lay.spread_far(lay.ordered(first_keep, first_got, 0), 0)
    second_got = lay.turned(lay.tie(second_give, first_chunk))
    [(feed_keep, feed_give)] = picked(turn, [w_mlp_gate, w_mlp_up], [1, 1], [mixed_join])

    def half_rows(weight):
        half = weight.shape[0] // 2
        return [lax.dynamic_slice_in_dim(weight, place * half, half, 0) for place in (lay.turn, 1 - lay.turn)]

    out_keep, out_give = half_rows(w_out)
    down_keep, down_give = half_rows(w_mlp_down)
    tall_got = lay.turned(lay.tie(jnp.concatenate([out_give, down_give], axis=0), second_got))
    feed_got = lay.turned(lay.tie(feed_give, second_got))
    second_chunk = lay.spread_far(lay.ordered(second_keep, second_got, 0), 0)
    in_first = lay.spread_ring(first_chunk, True)
    tall_got = lay.tie(tall_got, in_first[1], in_first[3])
    out_chunk = lay.spread_far(lay.ordered(out_keep, tall_got[:out_rows], 1), 1)
    in_second = lay.spread_ring(second_chunk, False)
    out_pieces = lay.spread_ring(out_chunk, True)

    got_slot = got_tokens[:, features].astype(jnp.int32)
    landing = (places[:, None] + 1 == got_slot[None, :]).astype(bf)
    sources = lay.sources()
    feature = jnp.arange(features, dtype=jnp.int32)
    origin = (sources[:, None] * block + jnp.arange(block, dtype=jnp.int32)[None, :]).reshape(1, -1)
    turning = (feature[:, None] == origin).astype(bf)
    numbers = jnp.arange(lay.ways, dtype=jnp.int32)
    picking = (sources[:, None] == numbers[None, :]).astype(f32)

    def reordered_gain(gain):
        return jnp.sum(picking[:, :, None] * gain.reshape(1, lay.ways, block), axis=1).reshape(features)

    def straight_gain(grad):
        return jnp.sum(picking[:, :, None] * grad.reshape(lay.ways, 1, block), axis=0).reshape(features)

    gains = (reordered_gain(norm_gains[0]), reordered_gain(norm_gains[1]))
    x_own = matmul(matmul(landing, got_tokens[:, :features]).astype(bf), turning)

    pair_lengths = jnp.concatenate([lengths, lay.turned(lengths)], axis=0)
    marks, seg_rows, live = group_marks(pair_lengths, group_rows)
    live_own = lax.dynamic_slice_in_dim(live[0], lay.core * row_count, row_count)[:, None]
    starts = [(share * heads + first) * DK for first in (0, pair)]
    cuts = [
        [(start, keys), (all_keys + start, keys), (2 * all_keys + 2 * start, vals)] for start in starts
    ]
    taps = [
        jnp.concatenate([lax.dynamic_slice_in_dim(conv_weights, start, size, 1) for start, size in cut], axis=1)
        for cut in cuts
    ]
    log_here = lax.dynamic_slice_in_dim(a_log, share * heads, heads)
    bias_here = lax.dynamic_slice_in_dim(dt_bias, share * heads, heads)
    params = jnp.pad(jnp.stack([bias_here, jnp.exp(log_here)]), ((0, 6), (0, LANES - heads)))
    gain_row = out_gain[None, :]

    scale_one = lax.rsqrt(jnp.mean(x_own * x_own, axis=1, keepdims=True) + EPS_ROW)
    first_rows = lay.rows_of((x_own * scale_one * gains[0]).astype(bf))
    proj_first, decays = project(first_rows, in_first, width, True)
    feed_chunk = lay.spread_far(lay.ordered(feed_keep, lay.tie(feed_got, first_rows), 0), 0, proj_first)
    heads_out, states_first, inverses_first = mixer_forward(
        0, heads, core, proj_first, decays, marks, seg_rows, taps[0], params, gain_row, None
    )
    proj_second = project(first_rows, in_second, width, False)[0]
    heads_out, states_second, inverses_second = mixer_forward(
        pair, heads, core, proj_second, decays, marks, seg_rows, taps[1], params, gain_row, heads_out
    )
    mixed_own = lay.own_of([(0, 0, 0, 0, out_rows)], [lay.tie(heads_out, feed_chunk)], [out_pieces], nn, features)
    middle = x_own + live_own * mixed_own

    got_cot = exchange(lay.tie(send_cot, in_second[2]))
    scale_two = lax.rsqrt(jnp.mean(middle * middle, axis=1, keepdims=True) + EPS_ROW)
    second_own_rows = (middle * scale_two * gains[1]).astype(bf)
    second_rows = lay.rows_of(second_own_rows)
    feed_behind = lay.ring(feed_chunk, 1)
    feed_ahead = lay.ring(feed_chunk, -1)
    feed_across = lay.ring(lay.tie(feed_ahead, second_own_rows), -1)
    feed_pieces = [feed_chunk, feed_ahead, feed_across, feed_behind]
    down_chunk = lay.spread_far(lay.ordered(down_keep, tall_got[out_rows:], 1), 1, second_own_rows)
    down_pieces = lay.spread_ring(down_chunk, True)
    dy_own = matmul(matmul(landing, lay.tie(got_cot, mixed_own)).astype(bf), turning)
    branch_rows = lay.rows_of((live_own * dy_own).astype(bf))
    pre, hidden = feed_forward(second_rows, feed_pieces)
    depth = features // 4

    def columns_of(rows, piece):
        return rows[:, piece * depth : piece * depth + depth]

    down_own, down_terms, down_sent = lay.collect_ring(lambda r: outer_sum(hidden, columns_of(branch_rows, r)), True)
    grad_pre = feed_backward(lay.tie(branch_rows, *down_terms), down_pieces, pre)
    feed_own, feed_terms, feed_sent = lay.collect_ring(
        lambda r: outer_sum(columns_of(second_rows, r), grad_pre), False
    )
    grad_second = lay.own_of([(0, 0, 0, 0, 2 * hidden_here)], [grad_pre], [feed_pieces], nt, features)
    grad_mid_norm, gain_two_grad = norm_back(middle, scale_two, gains[1], grad_second)
    grad_middle = dy_own + grad_mid_norm
    mix_rows = lay.rows_of((live_own * grad_middle).astype(bf))

    grad_heads = heads_backward(lay.tie(mix_rows, feed_sent[0]), out_pieces)
    out_own, out_terms, out_sent = lay.collect_ring(lambda r: outer_sum(heads_out, columns_of(mix_rows, r)), True)
    grad_proj_first, taps_first, params_first, gain_first = mixer_backward(
        0, heads, core, proj_first, decays, lay.tie(grad_heads, *out_terms), marks, seg_rows, taps[0], params,
        gain_row, states_first, inverses_first, None,
    )
    first_own, first_terms, first_sent = lay.collect_ring(
        lambda r: outer_sum(columns_of(first_rows, r), grad_proj_first[:, :width]), True
    )
    grad_proj_second, taps_second, params_second, gain_second = mixer_backward(
        pair, heads, core, proj_second, decays, lay.tie(grad_heads, feed_sent[1], *first_terms), marks, seg_rows,
        taps[1], params, gain_row, states_second, inverses_second, grad_proj_first,
    )
    second_own, second_terms, second_sent = lay.collect_ring(
        lambda r: outer_sum(columns_of(first_rows, r), grad_proj_second), False
    )
    grad_first = lay.own_of(
        [(0, 0, 0, 0, width), (1, 0, 1, 0, width), (1, width, 0, width, LANES)],
        [grad_proj_first, lay.tie(grad_proj_second, feed_sent[2], out_sent[0], *second_terms)],
        [in_first, in_second], nt, features,
    )
    grad_x_norm, gain_one_grad = norm_back(x_own, scale_one, gains[0], grad_first)
    grad_tokens = (grad_middle + grad_x_norm).astype(bf)

    def sent_out(own, *others):
        straight = times_back(own, turning).astype(bf)
        return exchange(lay.tie(outer_sum(landing, straight).astype(bf), *others))

    def sent_home(back, *others):
        return outer_sum(sending, lay.tie(back, *others)).astype(bf)

    branch_own = lay.own_of([(0, 0, 0, 0, hidden_here)], [lay.tie(hidden, grad_proj_first)], [down_pieces], nn, features)
    output = sent_home(sent_out((middle + live_own * branch_own).astype(bf), out_sent[0]), first_sent[2])
    tokens_grad = sent_home(sent_out(grad_tokens), *second_sent[1:])

    conv_full = jnp.zeros(conv_weights.shape, f32)
    for cut, grad in zip(cuts, (taps_first, taps_second)):
        begin = 0
        for start, size in cut:
            conv_full = lax.dynamic_update_slice_in_dim(conv_full, grad[:, begin : begin + size], start, 1)
            begin += size
    params_grad = params_first + params_second
    log_full = lax.dynamic_update_slice_in_dim(jnp.zeros_like(a_log), params_grad[0, :heads], share * heads, 0)
    bias_full = lax.dynamic_update_slice_in_dim(jnp.zeros_like(dt_bias), params_grad[1, :heads], share * heads, 0)
    gain_grad = gain_first[0] + gain_second[0]
    norm_grads = jnp.stack([straight_gain(gain_one_grad), straight_gain(gain_two_grad)])
    sums = flat([conv_full, norm_grads, gain_grad, log_full, bias_full])
    sums = lay.everywhere(sums, second_sent[1:]).reshape(-1)
    ends = [conv_full.size]
    for size in (2 * features, DV, all_heads, all_heads):
        ends.append(ends[-1] + size)
    norm_grad = sums[ends[0] : ends[1]].reshape(2, features)

    end = second_sent[1:]
    down_grad = lay.collect_last(lay.collect_far(down_own, 1), 1, feed_sent[2])
    first_grad = lay.collect_last(lay.collect_far(first_own, 0), 0, *end)
    second_grad = lay.collect_last(lay.collect_far(second_own, 0), 0)
    feed_grad = lay.collect_last(lay.collect_far(feed_own, 0), 0, *end)
    out_grad = lay.collect_last(lay.collect_far(out_own, 1), 1, *end)
    down_grad, feed_grad, out_grad = [
        (mine, lay.tie(theirs, *end).astype(f32)) for mine, theirs in (down_grad, feed_grad, out_grad)
    ]
    first_grad, second_grad = [(mine, theirs.astype(f32)) for mine, theirs in (first_grad, second_grad)]
    in_grads = []
    begin = 0
    for size in (keys, keys, vals, vals):
        part = slice(begin, begin + size)
        in_grads.append(
            lay.joined(*[[grads[0][:, part], grads[1][:, part]] for grads in zip(first_grad, second_grad)], 1)
        )
        begin += size
    for size in (heads, heads):
        in_grads.append(lay.joined(*[[grad[:, begin : begin + size]] for grad in second_grad], 1))
        begin += size

    def alternate(grad, part):
        return grad.reshape(grad.shape[0], -1, 2, LANES)[:, :, part].reshape(grad.shape[0], -1)

    return (
        output,
        tokens_grad,
        norm_grad,
        *in_grads,
        sums[: ends[0]].reshape(conv_full.shape),
        sums[ends[2] : ends[3]],
        sums[ends[3] : ends[4]],
        sums[ends[1] : ends[2]],
        lay.ordered(*out_grad, 0),
        *[lay.ordered(*[alternate(grad, part) for grad in feed_grad], 1) for part in (0, 1)],
        lay.ordered(*down_grad, 0),
    )


def solution(mesh):
    return jax.shard_map(
        shards,
        mesh=mesh,
        in_specs=(
            P(("dp", "tensor"), None),
            P(("dp", "tensor"), None),
            P("dp", None),
            P(("dp", "tensor")),
            P(),
            P("dp", "tensor"),
            P("dp", "tensor"),
            P("dp", "tensor"),
            P("dp", "tensor"),
            P("dp", "tensor"),
            P("dp", "tensor"),
            P(),
            P(),
            P(),
            P(),
            P("tensor", "dp"),
            P("dp", "tensor"),
            P("dp", "tensor"),
            P("tensor", "dp"),
        ),
        out_specs=(
            P(("dp", "tensor"), None),
            P(("dp", "tensor"), None),
            P(),
            P("dp", "tensor"),
            P("dp", "tensor"),
            P("dp", "tensor"),
            P("dp", "tensor"),
            P("dp", "tensor"),
            P("dp", "tensor"),
            P(),
            P(),
            P(),
            P(),
            P("tensor", "dp"),
            P("dp", "tensor"),
            P("dp", "tensor"),
            P("tensor", "dp"),
        ),
        check_vma=False,
    )
```
